256 devices in a mesh: gx: 4 (over y), gy: 8 (over z), swath: 8 (over x, core).
Axes of the slice: x: 4, y: 4, z: 8, core: 2. Of those that a mesh axis runs over, the one named last changes fastest.
Arguments:
- direction: bfloat16 [120, 10, 128, 512], P(None, None, ('gy', 'swath'), 'gx'), may hold values from -6 to 6
- courant_x: float32 [10, 128, 512], P(None, ('gy', 'swath'), 'gx'), may hold values from -0.5 to 0.5
- courant_y: float32 [10, 128, 512], P(None, ('gy', 'swath'), 'gx'), may hold values from -0.5 to 0.5
- kernel: float32 [10, 128, 512], P(None, ('gy', 'swath'), 'gx'), may hold values from 0.1 to 1.5
- mechanism: int32 [128, 512], P(('gy', 'swath'), 'gx'), may hold values from 0 to 3
- propagator: bfloat16 [4, 120, 120], replicated, may hold values from -0.5 to 0.5
- footprint_pixel: int32 [128, 512], P(('gy', 'swath'), 'gx'), may hold values from 0 to 63
- footprint_weight: float32 [128, 512], P(('gy', 'swath'), 'gx'), may hold values from 0.1 to 1
- footprint_owner: int32 [512, 1], P(('gx', 'gy', 'swath')), may hold values from 0 to 7; in each aligned block of 2 rows (0 to 1, 2 to 3, ...) at most 2 rows name the same one
- precision: float32 [16384], P(('gx', 'gy', 'swath')), may hold values from 0.3 to 3
Outputs:
- product: bfloat16 [120, 10, 128, 512], P(None, None, ('gy', 'swath'), 'gx')
- departures: float32 [16384], P(('gx', 'gy', 'swath'))
The draws below stay inside these ranges and needn't reach their ends.
Inputs may be any that keep to these rules, and one draw needn't show every extreme that they name: `footprint_owner`: among the 2 rows of one device's blocks, no swath index is named more than 2 times.
All inputs are finite; a program needn't handle non-finite values.
Results may differ from the reference program's by a relative error of at most 0.0053.
Values may be sent and summed in bfloat16 or wider, within the bound.
No kernel may reach another device: no remote copies, remote signals or barrier semaphores. Data moves between devices by JAX's collectives and lax.ppermute only.
A program may use at most 128 MiB of HBM per device.

```python
import math
import jax
import jax.numpy as jnp
import numpy as np
from jax import lax

SPEC = 120
LEV = 10
NMECH = 4
CXD = 128
CYD = 2
PIX_DEV = 64
CAPB = 2
NX = 512
NY = 128
NPIX = 16384
NBLK = 512
N_GY = 8
N_SWATH = 8


def with_ends(drawn, own_key, least, top_value):
    extent = drawn.shape
    index_at = [jax.random.randint(jax.random.fold_in(own_key, axis), (), 0, extent[axis]) for axis in range(len(extent))]
    drawn = drawn.at[tuple(index_at)].set(least)
    longest = extent.index(max(extent))
    index_at[longest] = (index_at[longest] + 1) % extent[longest]
    return drawn.at[tuple(index_at)].set(top_value)


def steps_of(stream_key, shape, shards, low, high):
    level = 1.0
    for axis_at, shards_of in shards:
        heights = jax.random.uniform(jax.random.fold_in(jax.random.fold_in(stream_key, 6), axis_at), (shards_of,), jnp.float32, low / len(shards), high / len(shards))
        level = level * jnp.repeat(jnp.exp(heights), shape[axis_at] // shards_of).reshape((-1,) + (1,) * (len(shape) - 1 - axis_at))
    return level


def routed_block(key, own, number, rows, count, top, bound, lean):
    order = jax.random.permutation(key, count)
    heavy_load, common = portions_of(count, rows * top, bound, lean, True), portions_of(count, rows * top, bound, lean, False)
    places = jnp.arange(count)

    def named(tallies, turn):
        used = int((tallies > 0).sum())
        fixed = max(1, used // 4)
        moved = fixed + (places - fixed + turn * (used - fixed)) % max(1, count - fixed)
        return jnp.zeros((count,), jnp.int32).at[order[jnp.where(places < fixed, places, moved)]].set(jnp.asarray(tallies, jnp.int32))

    tallies = jnp.where(number % 4 == 0, named(heavy_load, number // 4), named(common, number - number // 4 - 1))
    mixed = jax.random.permutation(jax.random.fold_in(own, 3), count)
    source_of, sink = mixed[0:count // 2 * 2:2], mixed[1:count // 2 * 2:2]
    room = jnp.minimum(tallies[source_of] - 1, bound - tallies[sink]) // 2
    room = jnp.where((source_of == order[0]) | (sink == order[0]) | (tallies[sink] == 0), 0, jnp.maximum(room, 0))
    moved = jax.random.randint(jax.random.fold_in(own, 4), (count // 2,), 0, 1 << 20) % (room + 1)
    tallies = tallies.at[source_of].add(-moved).at[sink].add(moved)
    items = jnp.searchsorted(jnp.cumsum(tallies), jnp.arange(rows * top), side="right").astype(jnp.int32)
    table = items.reshape(top, rows).T
    table = table[jax.random.permutation(jax.random.fold_in(own, 1), rows)]
    turn = jax.random.randint(jax.random.fold_in(own, 2), (rows, 1), 0, top)
    return jnp.take_along_axis(table, (jnp.arange(top)[None, :] + turn) % top, axis=1)


def portions_of(count, total, bound, lean, full):
    loads = [(1 << 20) // math.isqrt(rank ** lean) + 1 for rank in range(1, count + 1)]
    largest = bound if full else min(bound, max(-(-total // count), total * loads[0] // sum(loads)))
    least = 1 if total - largest >= count - 1 else 0
    counts, surplus = [largest] + [least] * (count - 1), total - largest - least * (count - 1)
    while surplus > 0:
        movable = [i for i in range(1, count) if counts[i] < largest] or [i for i in range(1, count) if counts[i] < bound]
        mass, remaining = sum([loads[i] for i in movable]), surplus
        for i in movable:
            addition = min(bound - counts[i], max(1, remaining * loads[i] // mass), surplus)
            counts[i] = counts[i] + addition
            surplus = surplus - addition
    return np.array(counts)


def centred(own_key, shape, scale, most, pieces=(), dtype=jnp.bfloat16):
    array = jax.random.normal(own_key, shape, jnp.float32) * scale
    if len(pieces) > 0:
        array = steps_of(own_key, shape, pieces, -0.22, 0.18) * array
    return jnp.clip(array, min=-most, max=most).astype(dtype)


def setup_inputs(seed: int = 0) -> dict:
    arg_keys = jax.random.split(jax.random.key(seed), 11)
    direction = centred(arg_keys[0], (SPEC, LEV, NY, NX), 1.0, 6.0, ((2, 64), (3, 4)))
    courant_x = jnp.clip(jax.random.uniform(arg_keys[1], (LEV, NY, NX), jnp.float32, -0.5, 0.5) * steps_of(arg_keys[1], (LEV, NY, NX), ((1, 64), (2, 4)), -0.4, 0.0), -0.5, 0.5)
    courant_y = jnp.clip(jax.random.uniform(arg_keys[2], (LEV, NY, NX), jnp.float32, -0.5, 0.5) * steps_of(arg_keys[2], (LEV, NY, NX), ((1, 64), (2, 4)), -0.4, 0.0), -0.5, 0.5)
    kernel = jnp.clip(jnp.exp(math.log(1.5) - 2.7080502 * jax.random.uniform(arg_keys[3], (LEV, NY, NX), jnp.float32) ** steps_of(arg_keys[3], (LEV, NY, NX), ((1, 64), (2, 4)), -0.2, 0.2)), 0.1, 1.5)
    mechanism = with_ends(jax.random.randint(arg_keys[4], (NY, NX), 0, NMECH), jax.random.fold_in(arg_keys[4], 1), 0, NMECH - 1).astype(jnp.int32)
    propagator = centred(arg_keys[5], (NMECH, SPEC, SPEC), SPEC ** -0.5, 0.5)
    footprint_pixel = with_ends(jax.random.randint(arg_keys[6], (NY, NX), 0, PIX_DEV), jax.random.fold_in(arg_keys[6], 1), 0, PIX_DEV - 1).astype(jnp.int32)
    footprint_weight = jnp.clip(jnp.exp(math.log(1.0) - 2.3025851 * jax.random.uniform(arg_keys[7], (NY, NX), jnp.float32) ** steps_of(arg_keys[7], (NY, NX), ((0, 64), (1, 4)), -0.2, 0.2)), 0.1, 1.0)
    footprint_owner_keys = jax.random.split(jax.random.fold_in(arg_keys[8], 1), NBLK // CYD)
    footprint_owner_turns = jax.random.permutation(jax.random.fold_in(arg_keys[8], 3), NBLK // CYD)
    footprint_owner = jax.vmap(lambda own, number: routed_block(jax.random.fold_in(arg_keys[8], 2), own, number, CYD, N_SWATH, 1, CAPB, 1))(footprint_owner_keys, footprint_owner_turns).reshape((NBLK, 1))
    precision = jnp.clip(jnp.exp(math.log(3.0) - 2.3025851 * jax.random.uniform(arg_keys[9], (NPIX,), jnp.float32) ** steps_of(arg_keys[9], (NPIX,), ((0, 256),), -0.2, 0.2)), 0.3, 3.0)
    return dict(direction=direction, courant_x=courant_x, courant_y=courant_y, kernel=kernel, mechanism=mechanism, propagator=propagator, footprint_pixel=footprint_pixel, footprint_weight=footprint_weight, footprint_owner=footprint_owner, precision=precision)


KD = 0.2


def shifted(field, dy, dx):
    rank = field.ndim
    padded = jnp.pad(field, [(0, 0)] * (rank - 2) + [(1, 1), (1, 1)])
    height = field.shape[-2]
    width = field.shape[-1]
    part = lax.slice_in_dim(padded, 1 + dy, 1 + dy + height, axis=rank - 2)
    return lax.slice_in_dim(part, 1 + dx, 1 + dx + width, axis=rank - 1)


def advect(field, cx, cy):
    return ((1.0 - 4.0 * KD) * field + (KD - 0.5 * cx) * shifted(field, 0, 1)
            + (KD + 0.5 * cx) * shifted(field, 0, -1)
            + (KD - 0.5 * cy) * shifted(field, 1, 0) + (KD + 0.5 * cy) * shifted(field, -1, 0))


def advect_adjoint(field, cx, cy):
    rx = field * cx
    ry = field * cy
    near = shifted(field, 0, -1) + shifted(field, 0, 1) + shifted(field, -1, 0) + shifted(field, 1, 0)
    return ((1.0 - 4.0 * KD) * field + KD * near
            - 0.5 * shifted(rx, 0, -1) + 0.5 * shifted(rx, 0, 1)
            - 0.5 * shifted(ry, -1, 0) + 0.5 * shifted(ry, 1, 0))


def chemistry(base, rounded, mechanism, propagator, transpose):
    species = base.shape[0]
    flat = rounded.reshape(species, -1)
    total = base
    for index in range(propagator.shape[0]):
        matrix = propagator[index].T if transpose else propagator[index]
        term = jnp.dot(matrix, flat, preferred_element_type=jnp.float32).reshape(base.shape)
        total = total + jnp.where(mechanism == index, term, 0.0)
    return total


def reference(direction, courant_x, courant_y, kernel, mechanism, propagator,
              footprint_pixel, footprint_weight, footprint_owner, precision):
    species = direction.shape[0]

    def forward(inputs):
        level_dir, cx, cy = inputs
        first = advect(level_dir.astype(jnp.float32), cx, cy)
        first_bf = first.astype(jnp.bfloat16)
        state = chemistry(first, first_bf, mechanism, propagator, False).astype(jnp.bfloat16)
        second = advect(state.astype(jnp.float32), cx, cy)
        second_bf = second.astype(jnp.bfloat16)
        rows = jnp.dot(propagator[:, 0, :], second_bf.reshape(species, -1),
                       preferred_element_type=jnp.float32).reshape((NMECH,) + second.shape[1:])
        head = second[0]
        for index in range(NMECH):
            head = head + jnp.where(mechanism == index, rows[index], 0.0)
        return head

    heads = lax.map(forward, (jnp.moveaxis(direction, 1, 0), courant_x, courant_y))
    weighted = footprint_weight * jnp.sum(kernel * heads, axis=0)
    groups = N_GY * N_SWATH
    rows_iota = lax.broadcasted_iota(jnp.int32, (NY, NX), 0)
    cols_iota = lax.broadcasted_iota(jnp.int32, (NY, NX), 1)
    tile = (cols_iota // CXD) * groups + rows_iota // CYD
    block = tile * CYD + rows_iota % CYD
    owner = footprint_owner[:, 0][block]
    pixel_ids = ((tile // N_SWATH) * N_SWATH + owner) * PIX_DEV + footprint_pixel
    sums = jax.ops.segment_sum(weighted.reshape(-1), pixel_ids.reshape(-1), num_segments=NPIX)
    departures = precision * sums
    back = footprint_weight * departures[pixel_ids]
    coef = jnp.zeros((species, NY, NX), jnp.float32)
    for index in range(NMECH):
        coef = coef + jnp.where(mechanism == index, propagator[index, 0, :].astype(jnp.float32)[:, None, None], 0.0)

    def backward(inputs):
        level_kernel, cx, cy = inputs
        impulse = level_kernel * back
        late = coef * impulse[None]
        late = late.at[0].add(impulse)
        middle = advect_adjoint(late, cx, cy)
        middle_bf = middle.astype(jnp.bfloat16)
        early = chemistry(middle, middle_bf, mechanism, propagator, True)
        return advect_adjoint(early, cx, cy).astype(jnp.bfloat16)

    product = lax.map(backward, (kernel, courant_x, courant_y))
    return jnp.moveaxis(product, 0, 1), departures
```

```python
import functools

import jax
import jax.numpy as jnp
from jax import lax
from jax.experimental import pallas as pl
from jax.experimental.pallas import tpu as pltpu
from jax.sharding import PartitionSpec as P

KD = 0.2
ALL = ("gx", "gy", "swath")
LANES = 128
NM = 4
NK = NM * NM
BF = jnp.bfloat16
F32 = jnp.float32
VMEM = pl.BlockSpec(memory_space=pltpu.VMEM)
SMEM = pl.BlockSpec(memory_space=pltpu.SMEM)


def iota(shape, dim):
    return lax.broadcasted_iota(jnp.int32, shape, dim)


def lane_roll(v, shift):
    return pltpu.roll(v, shift % v.shape[-1], v.ndim - 1)


def split(v):
    high = v.astype(BF)
    return high, (v - high.astype(F32)).astype(BF)


class Sizes:
    def __init__(self, species, levels):
        self.species = species
        self.levels = levels
        self.rows = 2 * levels
        self.base = 8 * levels
        self.st = self.base + 8
        self.st16 = -(-self.st // 16) * 16
        self.o_st = self.rows * NK
        self.o_hg = self.o_st + 2 * self.st16
        self.o_hs = self.o_hg + NK
        self.msg = self.o_hs + 2 * 16
        self.edge = NK + 8


def project_kernel(
    z, owner_ref, dir_ref, prop_ref, cx_ref, cy_ref, kern_ref, mech_ref, pix_ref, wgt_ref,
    g_ref, msg_ref, edge_ref, st_ref, d_ref, wide,
):
    species = z.species
    wide[...] = dir_ref[...].astype(F32)
    k_of = iota((NK, species), 0)
    heads = jnp.zeros((NK, species), F32)
    for m in range(NM):
        row = prop_ref[m][0:1, :].astype(F32)
        heads = heads + jnp.where(k_of % NM == m, row, 0.0)
    total = heads + jnp.where(iota((NK, species), 1) == 0, 1.0, 0.0)
    lhs = heads.astype(BF)
    for m in range(NM):
        matrix = prop_ref[m]
        term = jnp.dot(lhs, matrix, preferred_element_type=F32)
        total = total + jnp.where(k_of // NM == m, term + matrix[0:1, :].astype(F32), 0.0)
    high, low = split(total)
    both = jnp.concatenate([high, low], axis=0)
    d_ref[...] = jnp.concatenate([high, high, low], axis=0)
    cells = jnp.concatenate(
        [wide[pl.ds(r, species, stride=z.rows), :].astype(BF) for r in range(z.rows)], axis=1
    )
    g32 = jnp.dot(both, cells, preferred_element_type=F32)
    g = g32[:NK] + g32[NK:]
    lane = iota((NK, LANES), 1)
    edge = jnp.zeros((NK, LANES), F32)
    for r in range(z.rows):
        part = g[:, r * LANES : (r + 1) * LANES]
        g_ref[r * NK : (r + 1) * NK, :] = part
        msg_ref[r * NK : (r + 1) * NK, :] = part.astype(BF)
        edge = jnp.where(lane // 4 == r, lane_roll(part, 4 * r + 2), edge)
    edge_ref[0:NK, :] = edge
    lane = iota((8, LANES), 1)
    side = jnp.zeros((8, LANES), F32)
    blank = jnp.zeros((2, LANES), F32)
    own = jnp.where(iota((2, LANES), 0) == 0, owner_ref[0], owner_ref[1])
    for l in range(z.levels + 1):
        if l < z.levels:
            parts = [cx_ref[l], cy_ref[l], kern_ref[l], blank]
        else:
            parts = [
                (mech_ref[...] + 1).astype(F32),
                pix_ref[...].astype(F32),
                wgt_ref[...],
                own.astype(F32),
            ]
        block = jnp.concatenate(parts, axis=0)
        st_ref[8 * l : 8 * l + 8, :] = block
        side = jnp.where(lane // 4 == l, lane_roll(block, 4 * l + 2), side)
    st_ref[z.st :, :] = jnp.zeros((z.st16 - z.st, LANES), F32)
    edge_ref[NK:, :] = side
    high, low = split(st_ref[...])
    msg_ref[z.o_st : z.o_st + z.st16, :] = high
    msg_ref[z.o_st + z.st16 : z.o_st + 2 * z.st16, :] = low
    msg_ref[z.o_hg :, :] = jnp.zeros((z.msg - z.o_hg, LANES), BF)


def edges_kernel(z, pos_ref, x0_ref, x1_ref, main_ref, msg_ref, side_ref, part, sem):
    gx = pos_ref[0]
    even = gx % 2 == 0
    x0 = x0_ref[...]
    x1 = x1_ref[...]
    right = jnp.where(even, x0, x1)
    left = jnp.where(even, x1, x0)
    right = jnp.where(gx < pos_ref[1] - 1, right, 0.0)
    left = jnp.where(gx > 0, left, 0.0)
    side = jnp.where(iota(x0.shape, 1) % 4 < 2, left, right)
    side_ref[...] = side
    part[0:NK, :] = side[0:NK].astype(BF)
    high, low = split(jnp.concatenate([side[NK:], jnp.zeros((8, LANES), F32)], axis=0))
    part[NK : NK + 16, :] = high
    part[NK + 16 :, :] = low
    copy = pltpu.make_async_copy(part, msg_ref.at[pl.ds(z.o_hg, z.msg - z.o_hg), :], sem)
    copy.start()
    copy.wait()


def columns_kernel(
    z, pos_ref, g_ref, st_ref, side_ref, a_ref, b_ref, prec_ref,
    part_ref, ext_ref, gx3, hg3,
):
    t = pos_ref[2]
    swath = pos_ref[3]
    odd = t % 2 == 1
    n = z.o_st
    for slot in range(3):
        if slot == 1:
            gx3[n : 2 * n, :] = g_ref[...]
            hg3[NK : 2 * NK, :] = side_ref[0:NK, :]
            stat = st_ref[...]
            side = side_ref[NK:, :]
        else:
            first, second = (a_ref, b_ref) if slot == 0 else (b_ref, a_ref)
            valid = t > 0 if slot == 0 else t < pos_ref[4] - 1

            def pick(lo, hi, first=first, second=second, valid=valid):
                chosen = jnp.where(odd, first[lo:hi, :].astype(F32), second[lo:hi, :].astype(F32))
                return jnp.where(valid, chosen, 0.0)

            gx3[slot * n : (slot + 1) * n, :] = pick(0, n)
            hg3[slot * NK : (slot + 1) * NK, :] = pick(z.o_hg, z.o_hs)
            stat = pick(z.o_st, z.o_st + z.st16) + pick(z.o_st + z.st16, z.o_hg)
            side = (pick(z.o_hs, z.o_hs + 16) + pick(z.o_hs + 16, z.msg))[0:8]
        for l in range(z.levels + 1):
            ext_ref[slot, l, :, 0:LANES] = stat[8 * l : 8 * l + 8]
            ext_ref[slot, l, :, LANES:] = lane_roll(side, LANES - (4 * l + 2))
    W = 2 * LANES
    k_of = iota((NK, W), 0) // NM
    m_of = iota((8, LANES), 0)
    place = ((0, 1), (1, 0), (1, 1), (2, 0))
    masks = [
        ext_ref[s, z.levels, y : y + 1, :] == (k_of + 1).astype(F32) for s, y in place
    ]
    final = [
        ext_ref[1, z.levels, y : y + 1, 0:LANES] == (m_of + 1).astype(F32) for y in range(2)
    ]

    def level(l, sums):
        def field(s, y):
            r = 2 * l + y
            own = gx3[pl.ds(pl.multiple_of((s * z.rows + r) * NK, NK), NK), :]
            side = pltpu.roll(hg3[s * NK : (s + 1) * NK, :], LANES - 2 - 4 * r, 1)
            return jnp.concatenate([own, side], axis=1)

        stats = [ext_ref[s, l] for s in range(3)]

        def winds(s, y):
            return 0.5 * stats[s][y : y + 1, :], 0.5 * stats[s][2 + y : 3 + y, :]

        fields = [field(s, y) for s in range(3) for y in range(2)]
        firsts = []
        for i, (s, y) in enumerate(place):
            cx, cy = winds(s, y)
            mid = fields[i + 1]
            out = (
                (1.0 - 4.0 * KD) * mid
                + (KD - cx) * pltpu.roll(mid, W - 1, 1)
                + (KD + cx) * pltpu.roll(mid, 1, 1)
                + (KD - cy) * fields[i + 2]
                + (KD + cy) * fields[i]
            )
            out = jnp.where(masks[i], out, 0.0)
            half = out[0:8] + out[8:16]
            firsts.append(half + pltpu.roll(half, 4, 0))
        new = []
        for y in range(2):
            cx, cy = winds(1, y)
            cx, cy = cx[:, 0:LANES], cy[:, 0:LANES]
            mid = firsts[y + 1]
            out = (
                (1.0 - 4.0 * KD) * mid[:, 0:LANES]
                + (KD - cx) * pltpu.roll(mid, W - 1, 1)[:, 0:LANES]
                + (KD + cx) * pltpu.roll(mid, 1, 1)[:, 0:LANES]
                + (KD - cy) * firsts[y + 2][:, 0:LANES]
                + (KD + cy) * firsts[y][:, 0:LANES]
            )
            kern = stats[1][4 + y : 5 + y, 0:LANES]
            new.append(sums[y] + kern * out)
        return tuple(new)

    zero = jnp.zeros((8, LANES), F32)
    sums = lax.fori_loop(0, z.levels, level, (zero, zero))
    pixels = prec_ref.shape[1]
    sub = iota((pixels, LANES), 0)
    lane = iota((pixels, LANES), 1)
    wide8 = iota((8, LANES), 0)
    lane8 = iota((8, LANES), 1)
    total = jnp.zeros((8, LANES), F32)
    base = z.base
    for y in range(2):
        column = jnp.sum(jnp.where(final[y], sums[y], 0.0), axis=0, keepdims=True)
        column = column * st_ref[base + 4 + y : base + 5 + y, :]
        pix = st_ref[base + 2 + y : base + 3 + y, :]
        hit = jnp.where(pix == sub.astype(F32), column, 0.0)
        tall = jnp.sum(hit, axis=1, keepdims=True)
        row = jnp.sum(jnp.where(sub == lane, tall, 0.0), axis=0, keepdims=True)
        owner = st_ref[base + 6 + y : base + 7 + y, :]
        total = total + jnp.where(owner == wide8.astype(F32), row, 0.0)
    prec = jnp.concatenate([jnp.zeros((1, LANES - pixels), F32), prec_ref[...]], axis=1)
    part_ref[...] = jnp.where(
        lane8 < pixels, total, jnp.where(wide8 == swath, prec, 0.0)
    )


def pixels_kernel(z, pos_ref, p0_ref, p1_ref, p2_ref, p3_ref, ext_ref, dep_ref, back_ref):
    total = (p0_ref[...] + p1_ref[...]) + (p2_ref[...] + p3_ref[...])
    pixels = dep_ref.shape[1]
    dep = total * pltpu.roll(total, LANES - pixels, 1)
    swath = pos_ref[3]
    sub = iota((8, LANES), 0)
    dep_ref[...] = jnp.sum(jnp.where(sub == swath, dep, 0.0), axis=0, keepdims=True)[:, 0:pixels]

    def stack(f):
        out = jnp.zeros((8, LANES), F32)
        for s in range(3):
            for y in range(2):
                row = ext_ref[s, z.levels, 2 * f + y : 2 * f + y + 1, 0:LANES]
                out = jnp.where(sub == 2 * s + y, row, out)
        return out

    owner = stack(3)
    table = jnp.zeros((8, LANES), F32)
    for o in range(8):
        table = jnp.where(owner == float(o), dep[o : o + 1, :], table)
    index = stack(1).astype(jnp.int32)
    found = jnp.take_along_axis(table, index, axis=1)
    known = (sub >= 2) & (sub < 4)
    known = known | ((sub < 2) & (swath > 0)) | ((sub >= 4) & (swath < pos_ref[5] - 1))
    back_ref[...] = jnp.where(known, stack(2) * found, 0.0)


def sides_kernel(pos_ref, own_ref, x0_ref, x1_ref, wide_ref):
    gx = pos_ref[0]
    even = gx % 2 == 0
    x0 = x0_ref[...]
    x1 = x1_ref[...]
    right = jnp.where(even, x0, x1)
    left = jnp.where(even, x1, x0)
    right = jnp.where(gx < pos_ref[1] - 1, right, 0.0)
    left = jnp.where(gx > 0, left, 0.0)
    lane = iota(x0.shape, 1)
    wide_ref[:, 0:LANES] = own_ref[...]
    wide_ref[:, LANES:] = jnp.where(lane < 2, right, jnp.where(lane >= LANES - 2, left, 0.0))


def product_kernel(z, pos_ref, back_ref, other_ref, ext_ref, d_ref, out_ref, v3, tall):
    t = pos_ref[2]
    swath = pos_ref[3]
    W = 2 * LANES
    sub = iota((8, W), 0)
    other = other_ref[...]
    back = back_ref[...]
    upper = pltpu.roll(other, 6, 0)
    lower = pltpu.roll(other, 2, 0)
    back = jnp.where((sub < 2) & (swath == 0), jnp.where(t > 0, upper, 0.0), back)
    back = jnp.where(
        (sub >= 4) & (swath == pos_ref[5] - 1), jnp.where(t < pos_ref[4] - 1, lower, 0.0), back
    )
    place = [(s, y) for s in range(3) for y in range(2)]
    k_of = iota((NK, W), 0) // NM
    m_of = iota((8, W), 0) % NM
    drive = []
    for i, (s, y) in enumerate(place):
        mech = ext_ref[s, z.levels, y : y + 1, :]
        drive.append(jnp.where(mech == (m_of + 1).astype(F32), back[i : i + 1, :], 0.0))
    masks = [
        ext_ref[s, z.levels, y : y + 1, :] == (k_of + 1).astype(F32) for s, y in place[1:5]
    ]

    def unadvect(mid, cx, up, cy_up, down, cy_down):
        return (
            (1.0 - 4.0 * KD) * mid
            + pltpu.roll((KD - cx) * mid, 1, 1)
            + pltpu.roll((KD + cx) * mid, W - 1, 1)
            + (KD - cy_up) * up
            + (KD + cy_down) * down
        )

    def level(l, carry):
        stats = [ext_ref[s, l] for s in range(3)]
        cx = [0.5 * stats[s][y : y + 1] for s, y in place]
        cy = [0.5 * stats[s][2 + y : 3 + y] for s, y in place]
        kern = [stats[s][4 + y : 5 + y] for s, y in place]
        w = [kern[i] * drive[i] for i in range(6)]
        u = []
        for i in range(1, 5):
            mid = unadvect(w[i], cx[i], w[i - 1], cy[i - 1], w[i + 1], cy[i + 1])
            twice = jnp.concatenate([mid, mid], axis=0)
            u.append(jnp.where(masks[i - 1], twice, 0.0))
        for y in range(2):
            i = 2 + y
            v = unadvect(u[i - 1], cx[i], u[i - 2], cy[i - 1], u[i], cy[i + 1])[:, 0:LANES]
            high, low = split(v)
            at = pl.ds(pl.multiple_of((2 * l + y) * LANES, LANES), LANES)
            v3[0:NK, at] = high
            v3[NK : 2 * NK, at] = low
            v3[2 * NK :, at] = high
        return carry

    lax.fori_loop(0, z.levels, level, 0)
    d = d_ref[...]
    for r in range(0, z.rows, 2):
        both = lax.dot_general(
            d, v3[:, r * LANES : (r + 2) * LANES], (((0,), (0,)), ((), ())),
            preferred_element_type=F32,
        )
        tall[pl.ds(r, z.species, stride=z.rows), :] = both[:, 0:LANES]
        tall[pl.ds(r + 1, z.species, stride=z.rows), :] = both[:, LANES:]
    out_ref[...] = tall[...].astype(BF)


def shape(*dims, dtype=F32):
    return jax.ShapeDtypeStruct(dims, dtype)


LIMIT = pltpu.CompilerParams(vmem_limit_bytes=32 * 1024 * 1024)


def swaps_of(sizes):
    ngx, ngy, nsw = sizes
    nt = ngy * nsw

    def pairs(f):
        return [(g * nt + t, f(g, t)) for g in range(ngx) for t in range(nt)]

    def other(i, n, parity):
        return (i + 1) % n if i % 2 == parity else (i - 1) % n

    x0 = pairs(lambda g, t: other(g, ngx, 0) * nt + t)
    x1 = pairs(lambda g, t: other(g, ngx, 1) * nt + t)
    ya = pairs(lambda g, t: g * nt + other(t, nt, 0))
    yb = pairs(lambda g, t: g * nt + other(t, nt, 1))
    rim = [
        (g * nt + t, g * nt + (t + (1 if t % nsw else -1)) % nt)
        for g in range(ngx)
        for t in range(nt)
        if t % nsw in (0, nsw - 1)
    ]
    return x0, x1, ya, yb, rim


def per_device(
    sizes,
    direction,
    courant_x,
    courant_y,
    kernel,
    mechanism,
    propagator,
    footprint_pixel,
    footprint_weight,
    footprint_owner,
    precision,
):
    species, levels = direction.shape[:2]
    z = Sizes(species, levels)
    ngx, ngy, nsw = sizes
    x0, x1, ya, yb, rim = swaps_of(sizes)
    gx = lax.axis_index("gx")
    swath = lax.axis_index("swath")
    t = lax.axis_index("gy") * nsw + swath
    pos = jnp.stack([gx, jnp.int32(ngx), t, swath, jnp.int32(ngy * nsw), jnp.int32(nsw)]).astype(
        jnp.int32
    )

    def move(v, perm):
        return lax.ppermute(v, ALL, perm)

    g, msg, edge, st, d = pl.pallas_call(
        functools.partial(project_kernel, z),
        out_shape=(
            shape(z.o_st, LANES),
            shape(z.msg, LANES, dtype=BF),
            shape(z.edge, LANES),
            shape(z.st16, LANES),
            shape(3 * NK, species, dtype=BF),
        ),
        in_specs=[SMEM] + [VMEM] * 8,
        out_specs=(VMEM,) * 5,
        scratch_shapes=[pltpu.VMEM((species * z.rows, LANES), F32)],
        compiler_params=LIMIT,
        name="project",
    )(
        footprint_owner[:, 0],
        direction.reshape(species * z.rows, LANES),
        propagator, courant_x, courant_y, kernel, mechanism, footprint_pixel, footprint_weight,
    )
    e0 = move(edge, x0)
    e1 = move(edge, x1)
    msg, side = pl.pallas_call(
        functools.partial(edges_kernel, z),
        out_shape=(shape(z.msg, LANES, dtype=BF), shape(z.edge, LANES)),
        in_specs=[SMEM, VMEM, VMEM, pl.BlockSpec(memory_space=pl.ANY)],
        out_specs=(pl.BlockSpec(memory_space=pl.ANY), VMEM),
        scratch_shapes=[pltpu.VMEM((z.msg - z.o_hg, LANES), BF), pltpu.SemaphoreType.DMA],
        input_output_aliases={3: 0},
        compiler_params=LIMIT,
        name="edges",
    )(pos, e0, e1, msg)
    m_b = move(msg, yb)
    m_a = move(msg, ya)
    part, ext = pl.pallas_call(
        functools.partial(columns_kernel, z),
        out_shape=(shape(8, LANES), shape(3, levels + 1, 8, 2 * LANES)),
        in_specs=[SMEM] + [VMEM] * 6,
        out_specs=(VMEM, VMEM),
        scratch_shapes=[
            pltpu.VMEM((3 * z.o_st, LANES), F32),
            pltpu.VMEM((3 * NK, LANES), F32),
        ],
        compiler_params=LIMIT,
        name="columns",
    )(pos, g, st, side, m_a, m_b, precision.reshape(1, -1))
    part = part + lax.ppermute(part, "swath", [(i, i ^ 1) for i in range(nsw)])
    turns = [
        lax.ppermute(part, "swath", [(i, (i + 2 * k) % nsw) for i in range(nsw)])
        for k in range(1, 4)
    ]
    dep, back = pl.pallas_call(
        functools.partial(pixels_kernel, z),
        out_shape=(shape(1, precision.shape[0]), shape(8, LANES)),
        in_specs=[SMEM] + [VMEM] * 5,
        out_specs=(VMEM, VMEM),
        compiler_params=LIMIT,
        name="pixels",
    )(pos, part, *turns, ext)
    b0 = move(back, x0)
    b1 = move(back, x1)
    wide = pl.pallas_call(
        sides_kernel,
        out_shape=shape(8, 2 * LANES),
        in_specs=[SMEM] + [VMEM] * 3,
        out_specs=VMEM,
        compiler_params=LIMIT,
        name="sides",
    )(pos, back, b0, b1)
    across = move(wide, rim)
    product = pl.pallas_call(
        functools.partial(product_kernel, z),
        out_shape=shape(species * z.rows, LANES, dtype=BF),
        in_specs=[SMEM] + [VMEM] * 4,
        out_specs=VMEM,
        scratch_shapes=[
            pltpu.VMEM((3 * NK, z.rows * LANES), BF),
            pltpu.VMEM((species * z.rows, LANES), F32),
        ],
        compiler_params=LIMIT,
        name="product",
    )(pos, wide, across, ext, d)
    return product.reshape(direction.shape), dep.reshape(-1)


def solution(mesh):
    placed = (
        P(None, None, ("gy", "swath"), "gx"),
        P(None, ("gy", "swath"), "gx"),
        P(None, ("gy", "swath"), "gx"),
        P(None, ("gy", "swath"), "gx"),
        P(("gy", "swath"), "gx"),
        P(),
        P(("gy", "swath"), "gx"),
        P(("gy", "swath"), "gx"),
        P(("gx", "gy", "swath"), None),
        P(("gx", "gy", "swath")),
    )
    sizes = tuple(mesh.shape[a] for a in ALL)
    return jax.shard_map(
        functools.partial(per_device, sizes),
        mesh=mesh,
        in_specs=placed,
        out_specs=(P(None, None, ("gy", "swath"), "gx"), P(("gx", "gy", "swath"))),
        check_vma=False,
    )
```

```python
import functools

import jax
import jax.numpy as jnp
from jax import lax
from jax.experimental import pallas as pl
from jax.experimental.pallas import tpu as pltpu
from jax.sharding import PartitionSpec as P

KD = 0.2
UNROLL = 10
ALL = ("gx", "gy", "swath")
LANES = 128
NM = 4
NK = NM * NM
BF = jnp.bfloat16
F32 = jnp.float32
VMEM = pl.BlockSpec(memory_space=pltpu.VMEM)
ANY = pl.BlockSpec(memory_space=pl.ANY)
HBM = pl.BlockSpec(memory_space=pltpu.HBM)


def iota(shape, dim):
    return lax.broadcasted_iota(jnp.int32, shape, dim)


def lane_roll(v, shift):
    return pltpu.roll(v, shift % v.shape[-1], v.ndim - 1)


def split(v):
    high = v.astype(BF)
    return high, (v - high.astype(F32)).astype(BF)


class Sizes:
    def __init__(self, sizes, species, levels):
        self.ngx, self.ngy, self.nsw = sizes
        self.nt = self.ngy * self.nsw
        self.species = species
        self.levels = levels
        self.rows = 2 * levels
        self.base = 8 * levels
        self.st = self.base + 8
        self.st16 = -(-(self.st + 1) // 16) * 16
        self.o_st = self.rows * NK
        self.msg = self.o_st + 2 * self.st16
        self.edge = NK + 8
        self.far = NK + 2 * 16

    def place(self):
        gx = lax.axis_index("gx")
        swath = lax.axis_index("swath")
        return gx, swath, lax.axis_index("gy") * self.nsw + swath


def project_kernel(
    z, dir_hbm, prop_hbm, cx_hbm, cy_hbm, kern_hbm, mech_hbm, pix_hbm, wgt_hbm, own_hbm, prec_hbm,
    g_ref, msg_ref, edge_ref, st_ref, d_ref,
    dir_ref, prop_ref, cx_ref, cy_ref, kern_ref, mech_ref, pix_ref, wgt_ref, own_ref, prec_ref,
    wide, sems,
):
    sources = (
        prop_hbm, dir_hbm, cx_hbm, cy_hbm, kern_hbm, mech_hbm, pix_hbm, wgt_hbm, own_hbm, prec_hbm
    )
    targets = (
        prop_ref, dir_ref, cx_ref, cy_ref, kern_ref, mech_ref, pix_ref, wgt_ref, own_ref, prec_ref
    )
    copies = [
        pltpu.make_async_copy(a, b, sems.at[i]) for i, (a, b) in enumerate(zip(sources, targets))
    ]
    for copy in copies:
        copy.start()
    species = z.species
    copies[0].wait()
    k_of = iota((NK, species), 0)
    heads = jnp.zeros((NK, species), F32)
    for m in range(NM):
        row = prop_ref[m][0:1, :].astype(F32)
        heads = heads + jnp.where(k_of % NM == m, row, 0.0)
    total = heads + jnp.where(iota((NK, species), 1) == 0, 1.0, 0.0)
    lhs = heads.astype(BF)
    for m in range(NM):
        matrix = prop_ref[m]
        term = jnp.dot(lhs, matrix, preferred_element_type=F32)
        total = total + jnp.where(k_of // NM == m, term + matrix[0:1, :].astype(F32), 0.0)
    high, low = split(total)
    both = jnp.concatenate([high, low], axis=0)
    d_ref[...] = jnp.concatenate([high, high, low], axis=0)
    copies[1].wait()
    wide[...] = dir_ref[...].astype(F32)
    cells = jnp.concatenate(
        [wide[pl.ds(r, species, stride=z.rows), :].astype(BF) for r in range(z.rows)], axis=1
    )
    g32 = jnp.dot(both, cells, preferred_element_type=F32)
    g = g32[:NK] + g32[NK:]
    lane = iota((NK, LANES), 1)
    edge = jnp.zeros((NK, LANES), F32)
    for r in range(z.rows):
        part = g[:, r * LANES : (r + 1) * LANES]
        g_ref[r * NK : (r + 1) * NK, :] = part
        msg_ref[r * NK : (r + 1) * NK, :] = part.astype(BF)
        edge = jnp.where(lane // 4 == r, lane_roll(part, 4 * r + 2), edge)
    edge_ref[0:NK, :] = edge
    for copy in copies[2:]:
        copy.wait()
    lane = iota((8, LANES), 1)
    side = jnp.zeros((8, LANES), F32)
    blank = jnp.zeros((2, LANES), F32)
    own = jnp.where(iota((2, LANES), 0) == 0, own_ref[:, 0:1], own_ref[:, 1:2])
    for l in range(z.levels + 1):
        if l < z.levels:
            parts = [cx_ref[l], cy_ref[l], kern_ref[l], blank]
        else:
            parts = [
                (mech_ref[...] + 1).astype(F32),
                pix_ref[...].astype(F32),
                wgt_ref[...],
                own.astype(F32),
            ]
        block = jnp.concatenate(parts, axis=0)
        st_ref[8 * l : 8 * l + 8, :] = block
        side = jnp.where(lane // 4 == l, lane_roll(block, 4 * l + 2), side)
    pixels = prec_ref.shape[1]
    last = jnp.concatenate([jnp.zeros((1, LANES - pixels), F32), prec_ref[...]], axis=1)
    st_ref[z.st :, :] = jnp.broadcast_to(last, (z.st16 - z.st, LANES))
    edge_ref[NK:, :] = side
    high, low = split(st_ref[...])
    msg_ref[z.o_st : z.o_st + z.st16, :] = high
    msg_ref[z.o_st + z.st16 : z.o_st + 2 * z.st16, :] = low


def sides_of(z, gx, x0, x1):
    even = gx % 2 == 0
    right = jnp.where(even, x0, x1)
    left = jnp.where(even, x1, x0)
    return jnp.where(gx > 0, left, 0.0), jnp.where(gx < z.ngx - 1, right, 0.0)


def join_kernel(z, own_ref, other_ref, msg_ref, edges_ref, out_ref):
    edges_ref[0 : z.edge, :] = own_ref[...]
    edges_ref[z.edge :, :] = other_ref[...]


def edges_kernel(z, x0_ref, x1_ref, side_ref, far_ref):
    gx, _, _ = z.place()
    left, right = sides_of(z, gx, x0_ref[...], x1_ref[...])
    side = jnp.where(iota(left.shape, 1) % 4 < 2, left, right)
    side_ref[z.edge :, :] = side[0 : z.edge]
    own = side[z.edge :]
    side_ref[0 : z.edge, :] = own
    far_ref[0:NK, :] = own[0:NK].astype(BF)
    high, low = split(jnp.concatenate([own[NK:], jnp.zeros((8, LANES), F32)], axis=0))
    far_ref[NK : NK + 16, :] = high
    far_ref[NK + 16 :, :] = low


def spread(z, side, l):
    return lane_roll(side, LANES - (4 * l + 2))


def columns_kernel(
    z, a_ref, b_ref, g_ref, st_ref, side_ref,
    part_ref, ext_ref, corner_ref, gx3, hg3,
):
    _, swath, t = z.place()
    odd = t % 2 == 1
    has_b = jnp.logical_and(t > 0, t < z.nt - 1)
    n = z.o_st
    zero = jnp.zeros((NK, LANES), F32)
    for slot in range(3):
        if slot == 1:
            gx3[n : 2 * n, :] = g_ref[...]
            hg3[NK : 2 * NK, :] = side_ref[0:NK, :]
            stat = st_ref[...]
            side = side_ref[NK : z.edge, :]
        else:
            is_a = odd if slot == 0 else jnp.logical_not(odd)

            def pick(lo, hi, is_a=is_a):
                beyond = jnp.where(has_b, b_ref[lo:hi, :].astype(F32), 0.0)
                return jnp.where(is_a, a_ref[lo:hi, :].astype(F32), beyond)

            gx3[slot * n : (slot + 1) * n, :] = pick(0, n)
            hg3[slot * NK : (slot + 1) * NK, :] = jnp.where(
                is_a, side_ref[z.edge : z.edge + NK, :], zero
            )
            stat = pick(z.o_st, z.o_st + z.st16) + pick(z.o_st + z.st16, z.msg)
            side = jnp.where(is_a, side_ref[z.edge + NK :, :], zero[0:8])
        for l in range(z.levels + 1):
            ext_ref[slot, l, :, 0:LANES] = stat[8 * l : 8 * l + 8]
            ext_ref[slot, l, :, LANES:] = spread(z, side, l)
    W = 2 * LANES
    k_of = iota((NK, W), 0) // NM
    m_of = iota((8, LANES), 0)
    place = ((0, 1), (1, 0), (1, 1), (2, 0))
    masks = [
        ext_ref[s, z.levels, y : y + 1, :] == (k_of + 1).astype(F32) for s, y in place
    ]
    final = [
        ext_ref[1, z.levels, y : y + 1, 0:LANES] == (m_of + 1).astype(F32) for y in range(2)
    ]

    def level(l, sums):
        def field(s, y):
            r = 2 * l + y
            own = gx3[pl.ds(pl.multiple_of((s * z.rows + r) * NK, NK), NK), :]
            side = pltpu.roll(hg3[s * NK : (s + 1) * NK, :], LANES - 2 - 4 * r, 1)
            return jnp.concatenate([own, side], axis=1)

        stats = [ext_ref[s, l] for s in range(3)]

        def winds(s, y):
            return 0.5 * stats[s][y : y + 1, :], 0.5 * stats[s][2 + y : 3 + y, :]

        fields = [field(s, y) for s in range(3) for y in range(2)]
        firsts = []
        for i, (s, y) in enumerate(place):
            cx, cy = winds(s, y)
            mid = fields[i + 1]
            out = (
                (1.0 - 4.0 * KD) * mid
                + (KD - cx) * pltpu.roll(mid, W - 1, 1)
                + (KD + cx) * pltpu.roll(mid, 1, 1)
                + (KD - cy) * fields[i + 2]
                + (KD + cy) * fields[i]
            )
            out = jnp.where(masks[i], out, 0.0)
            half = out[0:8] + out[8:16]
            firsts.append(half + pltpu.roll(half, 4, 0))
        new = []
        for y in range(2):
            cx, cy = winds(1, y)
            cx, cy = cx[:, 0:LANES], cy[:, 0:LANES]
            mid = firsts[y + 1]
            out = (
                (1.0 - 4.0 * KD) * mid[:, 0:LANES]
                + (KD - cx) * pltpu.roll(mid, W - 1, 1)[:, 0:LANES]
                + (KD + cx) * pltpu.roll(mid, 1, 1)[:, 0:LANES]
                + (KD - cy) * firsts[y + 2][:, 0:LANES]
                + (KD + cy) * firsts[y][:, 0:LANES]
            )
            kern = stats[1][4 + y : 5 + y, 0:LANES]
            new.append(sums[y] + kern * out)
        stat_b = jnp.where(odd, stats[2], stats[0])
        cx_b = 0.5 * jnp.where(odd, stat_b[0:1], stat_b[1:2])
        cx_0 = 0.5 * jnp.where(odd, stats[1][1:2], stats[1][0:1])
        cy_0 = jnp.where(odd, -0.5, 0.5) * jnp.where(odd, stats[1][3:4], stats[1][2:3])
        kern = jnp.where(odd, stats[1][5:6], stats[1][4:5]) * weight_b
        sides = []
        for sign, shift in ((0.5, 1), (-0.5, W - 1)):
            first = (KD + 2 * sign * cx_b) * (KD + cy_0) * near_b
            second = pltpu.roll((KD + cy_0) * near_0, shift, 1) * (KD + 2 * sign * cx_0)
            sides.append(jnp.where(head_0, kern * (first + second), 0.0)[:, 0:LANES])
        left = pltpu.roll(sides[0], 8 * l + 1, 1)
        right = pltpu.roll(sides[1], 8 * l + 3, 1)
        lane = iota((NK, LANES), 1)
        corner = jnp.where(
            lane == 8 * l + 1, left, jnp.where(lane == 8 * l + 2, right, sums[2])
        )
        return tuple(new) + (corner,)

    misc = ext_ref[1, z.levels]
    misc_b = jnp.where(odd, ext_ref[2, z.levels], ext_ref[0, z.levels])
    mech_0 = jnp.where(odd, misc[1:2], misc[0:1])
    mech_b = jnp.where(odd, misc_b[0:1], misc_b[1:2])
    weight_b = jnp.where(odd, misc[5:6], misc[4:5])
    near_0 = (mech_0 == (k_of + 1).astype(F32)).astype(F32)
    near_b = (mech_b == (k_of + 1).astype(F32)).astype(F32)
    head_0 = mech_0 == (iota((NK, W), 0) % NM + 1).astype(F32)
    none = jnp.zeros((8, LANES), F32)
    sums = lax.fori_loop(0, z.levels, level, (none, none, zero), unroll=UNROLL)
    corner_ref[...] = sums[2]
    pixels = LANES // 2
    sub = iota((pixels, LANES), 0)
    lane = iota((pixels, LANES), 1)
    wide8 = iota((8, LANES), 0)
    lane8 = iota((8, LANES), 1)
    total = jnp.zeros((8, LANES), F32)
    base = z.base
    for y in range(2):
        column = jnp.sum(jnp.where(final[y], sums[y], 0.0), axis=0, keepdims=True)
        column = column * st_ref[base + 4 + y : base + 5 + y, :]
        pix = st_ref[base + 2 + y : base + 3 + y, :]
        hit = jnp.where(pix == sub.astype(F32), column, 0.0)
        tall = jnp.sum(hit, axis=1, keepdims=True)
        row = jnp.sum(jnp.where(sub == lane, tall, 0.0), axis=0, keepdims=True)
        owner = st_ref[base + 6 + y : base + 7 + y, :]
        total = total + jnp.where(owner == wide8.astype(F32), row, 0.0)
    prec = st_ref[z.st : z.st + 1, :]
    part_ref[...] = jnp.where(
        lane8 < pixels, total, jnp.where(wide8 == swath, prec, 0.0)
    )


def corner_kernel(z, part_ref, corner_ref, far_ref, st_ref, ext_ref, out_ref, full_ref, block, sem):
    _, _, t = z.place()
    odd = t % 2 == 1
    has_b = jnp.logical_and(t > 0, t < z.nt - 1)
    far = jnp.where(has_b, far_ref[...].astype(F32), 0.0)
    side = (far[NK : NK + 16] + far[NK + 16 :])[0:8]
    for l in range(z.levels + 1):
        block[l] = spread(z, side, l)
    slot = jnp.where(odd, 2, 0)
    copy = pltpu.make_async_copy(block, full_ref.at[slot, :, :, pl.ds(LANES, LANES)], sem)
    copy.start()
    g = far[0:NK]
    g = jnp.where(odd, g, pltpu.roll(g, LANES - 4, 1))
    share = jnp.sum(corner_ref[...] * g, axis=0, keepdims=True)
    lane = iota((1, LANES), 1)
    sub8 = iota((8, LANES), 0)
    lane8 = iota((8, LANES), 1)
    st = st_ref[z.base : z.base + 8, :]
    pixel = jnp.where(odd, st[3:4], st[2:3])
    owner = jnp.where(odd, st[7:8], st[6:7])
    total = part_ref[...]
    for c, column in ((1, 0), (2, LANES - 1)):
        value = jnp.sum(jnp.where(lane % 8 == c, share, 0.0), axis=1, keepdims=True)
        at = slice(column, column + 1)
        hit = (lane8.astype(F32) == pixel[:, at]) & (sub8.astype(F32) == owner[:, at])
        total = total + jnp.where(hit, value, 0.0)
    out_ref[...] = total
    copy.wait()


def product_kernel(z, own_ref, x0_ref, x1_ref, ext_ref, d_ref, out_ref, dep_ref, v3, tall):
    gx, swath, _ = z.place()
    W = 2 * LANES
    pixels = LANES // 2
    left, right = sides_of(z, gx, x0_ref[...], x1_ref[...])

    def weigh(v):
        return v * lane_roll(v, pixels)

    deps = [weigh(v) for v in (own_ref[...], left, right)]
    sub = iota((8, LANES), 0)
    dep_ref[...] = jnp.sum(jnp.where(sub == swath, deps[0][0:8], 0.0), axis=0, keepdims=True)[
        :, 0:pixels
    ]
    outer = ((sub < 2) & (swath == 0)) | ((sub >= 4) & (swath == z.nsw - 1))

    def stack(f):
        out = jnp.zeros((8, W), F32)
        for s in range(3):
            for y in range(2):
                row = ext_ref[s, z.levels, 2 * f + y : 2 * f + y + 1, :]
                out = jnp.where(iota((8, W), 0) == 2 * s + y, row, out)
        return out

    owner = stack(3)
    index = stack(1).astype(jnp.int32)
    weight = stack(2)

    def find(dep, owner, index):
        found = jnp.zeros((8, LANES), F32)
        for o in range(z.nsw):
            row = jnp.where(outer, dep[8 + o : 9 + o, :], dep[o : o + 1, :])
            value = jnp.take_along_axis(row, index, axis=1)
            found = jnp.where(owner == float(o), value, found)
        return found

    lane = iota((8, LANES), 1)
    far = (owner[:, LANES:], index[:, LANES:])
    beside = jnp.where(
        lane < 2, find(deps[2], *far), jnp.where(lane >= LANES - 2, find(deps[1], *far), 0.0)
    )
    near = find(deps[0], owner[:, 0:LANES], index[:, 0:LANES])
    back = weight * jnp.concatenate([near, beside], axis=1)
    place = [(s, y) for s in range(3) for y in range(2)]
    k_of = iota((NK, W), 0) // NM
    m_of = iota((8, W), 0) % NM
    drive = []
    for i, (s, y) in enumerate(place):
        mech = ext_ref[s, z.levels, y : y + 1, :]
        drive.append(jnp.where(mech == (m_of + 1).astype(F32), back[i : i + 1, :], 0.0))
    masks = [
        ext_ref[s, z.levels, y : y + 1, :] == (k_of + 1).astype(F32) for s, y in place[1:5]
    ]

    def unadvect(mid, cx, up, cy_up, down, cy_down):
        return (
            (1.0 - 4.0 * KD) * mid
            + pltpu.roll((KD - cx) * mid, 1, 1)
            + pltpu.roll((KD + cx) * mid, W - 1, 1)
            + (KD - cy_up) * up
            + (KD + cy_down) * down
        )

    def level(l, carry):
        stats = [ext_ref[s, l] for s in range(3)]
        cx = [0.5 * stats[s][y : y + 1] for s, y in place]
        cy = [0.5 * stats[s][2 + y : 3 + y] for s, y in place]
        kern = [stats[s][4 + y : 5 + y] for s, y in place]
        w = [kern[i] * drive[i] for i in range(6)]
        u = []
        for i in range(1, 5):
            mid = unadvect(w[i], cx[i], w[i - 1], cy[i - 1], w[i + 1], cy[i + 1])
            twice = jnp.concatenate([mid, mid], axis=0)
            u.append(jnp.where(masks[i - 1], twice, 0.0))
        for y in range(2):
            i = 2 + y
            v = unadvect(u[i - 1], cx[i], u[i - 2], cy[i - 1], u[i], cy[i + 1])[:, 0:LANES]
            high, low = split(v)
            at = pl.ds(pl.multiple_of((2 * l + y) * LANES, LANES), LANES)
            v3[0:NK, at] = high
            v3[NK : 2 * NK, at] = low
            v3[2 * NK :, at] = high
        return carry

    lax.fori_loop(0, z.levels, level, 0, unroll=UNROLL)
    d = d_ref[...]
    for r in range(0, z.rows, 2):
        both = lax.dot_general(
            d, v3[:, r * LANES : (r + 2) * LANES], (((0,), (0,)), ((), ())),
            preferred_element_type=F32,
        )
        tall[pl.ds(r, z.species, stride=z.rows), :] = both[:, 0:LANES]
        tall[pl.ds(r + 1, z.species, stride=z.rows), :] = both[:, LANES:]
    out_ref[...] = tall[...].astype(BF)


def shape(*dims, dtype=F32):
    return jax.ShapeDtypeStruct(dims, dtype)


LIMIT = pltpu.CompilerParams(vmem_limit_bytes=32 * 1024 * 1024)


def swaps_of(sizes):
    ngx, ngy, nsw = sizes
    nt = ngy * nsw

    def pairs(f):
        return [(g * nt + t, f(g, t)) for g in range(ngx) for t in range(nt)]

    def other(i, parity):
        return i + 1 if i % 2 == parity else i - 1

    def along_x(parity, flip):
        def to(g, t):
            n = other(g, parity)
            return n * nt + (t ^ flip) if 0 <= n < ngx else g * nt + (t ^ 1)

        return pairs(to)

    def along_y(parity):
        def to(g, t):
            n = other(t, parity)
            return g * nt + n if 0 <= n < nt else (g ^ 1) * nt + t

        return pairs(to)

    def along_z(g, t):
        gy, s = divmod(t, nsw)
        chip, core = divmod(s, 2)
        last = nsw // 2 - 1
        up = 1 if chip == 0 else -1
        if chip in (0, last) and 0 <= gy + up < ngy:
            gy, core = gy + up, 1 - core
        elif gy == ngy - 1 and chip < last:
            chip += 1
        elif gy == 0 and chip > 0:
            chip -= 1
        else:
            core = 1 - core
        return g * nt + gy * nsw + 2 * chip + core

    return along_x, along_y, pairs(along_z)


def per_device(
    sizes,
    direction,
    courant_x,
    courant_y,
    kernel,
    mechanism,
    propagator,
    footprint_pixel,
    footprint_weight,
    footprint_owner,
    precision,
):
    species, levels = direction.shape[:2]
    z = Sizes(sizes, species, levels)
    along_x, along_y, along_z = swaps_of(sizes)
    nsw = z.nsw

    def move(v, perm):
        return lax.ppermute(v, ALL, perm)

    cells = (species * z.rows, LANES)
    pixels = precision.shape[0]
    g, msg, edge, st, d = pl.pallas_call(
        functools.partial(project_kernel, z),
        out_shape=(
            shape(z.o_st, LANES),
            shape(z.msg, LANES, dtype=BF),
            shape(z.edge, LANES),
            shape(z.st16, LANES),
            shape(3 * NK, species, dtype=BF),
        ),
        in_specs=[HBM] * 10,
        out_specs=(VMEM,) * 5,
        scratch_shapes=[
            pltpu.VMEM(cells, BF),
            pltpu.VMEM(propagator.shape, BF),
            pltpu.VMEM(courant_x.shape, F32),
            pltpu.VMEM(courant_x.shape, F32),
            pltpu.VMEM(courant_x.shape, F32),
            pltpu.VMEM(mechanism.shape, jnp.int32),
            pltpu.VMEM(mechanism.shape, jnp.int32),
            pltpu.VMEM(mechanism.shape, F32),
            pltpu.VMEM((1, 2), jnp.int32),
            pltpu.VMEM((1, pixels), F32),
            pltpu.VMEM(cells, F32),
            pltpu.SemaphoreType.DMA((10,)),
        ],
        compiler_params=LIMIT,
        name="project",
    )(
        *(
            pltpu.with_memory_space_constraint(v, pltpu.HBM)
            for v in (
                direction.reshape(cells), propagator, courant_x, courant_y, kernel, mechanism,
                footprint_pixel, footprint_weight, footprint_owner.reshape(1, 2),
                precision.reshape(1, -1),
            )
        )
    )
    edges, msg = pl.pallas_call(
        functools.partial(join_kernel, z),
        out_shape=(shape(2 * z.edge, LANES), shape(z.msg, LANES, dtype=BF)),
        in_specs=[VMEM, VMEM, ANY],
        out_specs=(VMEM, ANY),
        input_output_aliases={2: 1},
        compiler_params=LIMIT,
        name="join",
    )(edge, move(edge, along_y(0)), msg)
    e0 = move(edges, along_x(0, 1))
    e1 = move(edges, along_x(1, 1))
    m_b = move(msg, along_y(1))
    m_a = move(msg, along_y(0))
    side, far = pl.pallas_call(
        functools.partial(edges_kernel, z),
        out_shape=(shape(2 * z.edge, LANES), shape(z.far, LANES, dtype=BF)),
        in_specs=[VMEM, VMEM],
        out_specs=(VMEM, VMEM),
        compiler_params=LIMIT,
        cost_estimate=pl.CostEstimate(
            flops=20_000_000_000, bytes_accessed=1024, transcendentals=0
        ),
        name="edges",
    )(e0, e1)
    far_b = move(far, along_y(1))
    part, ext, corner = pl.pallas_call(
        functools.partial(columns_kernel, z),
        out_shape=(
            shape(8, LANES), shape(3, levels + 1, 8, 2 * LANES), shape(NK, LANES)
        ),
        in_specs=[VMEM] * 5,
        out_specs=(VMEM,) * 3,
        scratch_shapes=[
            pltpu.VMEM((3 * z.o_st, LANES), F32),
            pltpu.VMEM((3 * NK, LANES), F32),
        ],
        compiler_params=LIMIT,
        name="columns",
    )(m_a, m_b, g, st, side)
    part, ext = pl.pallas_call(
        functools.partial(corner_kernel, z),
        out_shape=(shape(8, LANES), shape(3, levels + 1, 8, 2 * LANES)),
        in_specs=[VMEM] * 4 + [ANY],
        out_specs=(VMEM, ANY),
        scratch_shapes=[pltpu.VMEM((levels + 1, 8, LANES), F32), pltpu.SemaphoreType.DMA],
        input_output_aliases={4: 1},
        compiler_params=LIMIT,
        name="corner",
    )(part, corner, far_b, st, ext)
    part = part + lax.ppermute(part, "swath", [(i, i ^ 1) for i in range(nsw)])
    turns = [
        lax.ppermute(part, "swath", [(i, (i + 2 * k) % nsw ^ 1) for i in range(nsw)])
        for k in range(1, nsw // 2)
    ]
    for turn in turns:
        part = part + turn
    both = jnp.concatenate([part, move(part, along_z)], axis=0)
    b0 = move(both, along_x(0, 1))
    b1 = move(both, along_x(1, 1))
    product, dep = pl.pallas_call(
        functools.partial(product_kernel, z),
        out_shape=(shape(*cells, dtype=BF), shape(1, pixels)),
        in_specs=[VMEM] * 5,
        out_specs=(VMEM, VMEM),
        scratch_shapes=[
            pltpu.VMEM((3 * NK, z.rows * LANES), BF),
            pltpu.VMEM(cells, F32),
        ],
        compiler_params=LIMIT,
        name="product",
    )(both, b0, b1, ext, d)
    return product.reshape(direction.shape), dep.reshape(-1)


def solution(mesh):
    placed = (
        P(None, None, ("gy", "swath"), "gx"),
        P(None, ("gy", "swath"), "gx"),
        P(None, ("gy", "swath"), "gx"),
        P(None, ("gy", "swath"), "gx"),
        P(("gy", "swath"), "gx"),
        P(),
        P(("gy", "swath"), "gx"),
        P(("gy", "swath"), "gx"),
        P(("gx", "gy", "swath"), None),
        P(("gx", "gy", "swath")),
    )
    sizes = tuple(mesh.shape[a] for a in ALL)
    return jax.shard_map(
        functools.partial(per_device, sizes),
        mesh=mesh,
        in_specs=placed,
        out_specs=(P(None, None, ("gy", "swath"), "gx"), P(("gx", "gy", "swath"))),
        check_vma=False,
    )
```

```python
import functools

import jax
import jax.numpy as jnp
from jax import lax
from jax.experimental import pallas as pl
from jax.experimental.pallas import tpu as pltpu
from jax.sharding import PartitionSpec as P

KD = 0.2
UNROLL = 10
TURNS = (1, 3, 2)
ALL = ("gx", "gy", "swath")
LANES = 128
NM = 4
NK = NM * NM
BF = jnp.bfloat16
F32 = jnp.float32
VMEM = pl.BlockSpec(memory_space=pltpu.VMEM)
ANY = pl.BlockSpec(memory_space=pl.ANY)
HBM = pl.BlockSpec(memory_space=pltpu.HBM)


def iota(shape, dim):
    return lax.broadcasted_iota(jnp.int32, shape, dim)


def lane_roll(v, shift):
    return pltpu.roll(v, shift % v.shape[-1], v.ndim - 1)


def split(v):
    high = v.astype(BF)
    return high, (v - high.astype(F32)).astype(BF)


class Sizes:
    def __init__(self, sizes, species, levels):
        self.ngx, self.ngy, self.nsw = sizes
        self.nt = self.ngy * self.nsw
        self.species = species
        self.levels = levels
        self.rows = 2 * levels
        self.base = 8 * levels
        self.st = self.base + 8
        self.st16 = -(-(self.st + 1) // 16) * 16
        self.o_st = self.rows * NK
        self.msg = self.o_st + 2 * self.st16
        self.edge = NK + 8
        self.far = NK + 2 * 16

    def place(self):
        gx = lax.axis_index("gx")
        swath = lax.axis_index("swath")
        return gx, swath, lax.axis_index("gy") * self.nsw + swath


def project_kernel(
    z, dir_hbm, prop_hbm, cx_hbm, cy_hbm, kern_hbm, mech_hbm, pix_hbm, wgt_hbm, own_hbm, prec_hbm,
    g_ref, msg_ref, edge_ref, st_ref, d_ref,
    dir_ref, prop_ref, cx_ref, cy_ref, kern_ref, mech_ref, pix_ref, wgt_ref, own_ref, prec_ref,
    wide, sems,
):
    sources = (
        prop_hbm, dir_hbm, cx_hbm, cy_hbm, kern_hbm, mech_hbm, pix_hbm, wgt_hbm, own_hbm, prec_hbm
    )
    targets = (
        prop_ref, dir_ref, cx_ref, cy_ref, kern_ref, mech_ref, pix_ref, wgt_ref, own_ref, prec_ref
    )
    copies = [
        pltpu.make_async_copy(a, b, sems.at[i]) for i, (a, b) in enumerate(zip(sources, targets))
    ]
    for copy in copies:
        copy.start()
    species = z.species
    copies[0].wait()
    k_of = iota((NK, species), 0)
    heads = jnp.zeros((NK, species), F32)
    for m in range(NM):
        row = prop_ref[m][0:1, :].astype(F32)
        heads = heads + jnp.where(k_of % NM == m, row, 0.0)
    total = heads + jnp.where(iota((NK, species), 1) == 0, 1.0, 0.0)
    lhs = heads.astype(BF)
    for m in range(NM):
        matrix = prop_ref[m]
        term = jnp.dot(lhs, matrix, preferred_element_type=F32)
        total = total + jnp.where(k_of // NM == m, term + matrix[0:1, :].astype(F32), 0.0)
    high, low = split(total)
    both = jnp.concatenate([high, low], axis=0)
    d_ref[...] = jnp.concatenate([high, high, low], axis=0)
    copies[1].wait()
    wide[...] = dir_ref[...].astype(F32)
    cells = jnp.concatenate(
        [wide[pl.ds(r, species, stride=z.rows), :].astype(BF) for r in range(z.rows)], axis=1
    )
    g32 = jnp.dot(both, cells, preferred_element_type=F32)
    g = g32[:NK] + g32[NK:]
    lane = iota((NK, LANES), 1)
    edge = jnp.zeros((NK, LANES), F32)
    for r in range(z.rows):
        part = g[:, r * LANES : (r + 1) * LANES]
        g_ref[r * NK : (r + 1) * NK, :] = part
        msg_ref[r * NK : (r + 1) * NK, :] = part.astype(BF)
        edge = jnp.where(lane // 4 == r, lane_roll(part, 4 * r + 2), edge)
    edge_ref[0:NK, :] = edge
    for copy in copies[2:]:
        copy.wait()
    lane = iota((8, LANES), 1)
    side = jnp.zeros((8, LANES), F32)
    blank = jnp.zeros((2, LANES), F32)
    own = jnp.where(iota((2, LANES), 0) == 0, own_ref[:, 0:1], own_ref[:, 1:2])
    for l in range(z.levels + 1):
        if l < z.levels:
            parts = [cx_ref[l], cy_ref[l], kern_ref[l], blank]
        else:
            parts = [
                (mech_ref[...] + 1).astype(F32),
                pix_ref[...].astype(F32),
                wgt_ref[...],
                own.astype(F32),
            ]
        block = jnp.concatenate(parts, axis=0)
        st_ref[8 * l : 8 * l + 8, :] = block
        side = jnp.where(lane // 4 == l, lane_roll(block, 4 * l + 2), side)
    pixels = prec_ref.shape[1]
    last = jnp.concatenate([jnp.zeros((1, LANES - pixels), F32), prec_ref[...]], axis=1)
    st_ref[z.st :, :] = jnp.broadcast_to(last, (z.st16 - z.st, LANES))
    edge_ref[NK:, :] = side
    high, low = split(st_ref[...])
    msg_ref[z.o_st : z.o_st + z.st16, :] = high
    msg_ref[z.o_st + z.st16 : z.o_st + 2 * z.st16, :] = low


def sides_of(z, gx, x0, x1):
    even = gx % 2 == 0
    right = jnp.where(even, x0, x1)
    left = jnp.where(even, x1, x0)
    return jnp.where(gx > 0, left, 0.0), jnp.where(gx < z.ngx - 1, right, 0.0)


def edges_kernel(z, x0_ref, x1_ref, side_ref, far_ref):
    gx, _, _ = z.place()
    left, right = sides_of(z, gx, x0_ref[...], x1_ref[...])
    side = jnp.where(iota(left.shape, 1) % 4 < 2, left, right)
    side_ref[...] = side
    far_ref[0:NK, :] = side[0:NK].astype(BF)
    high, low = split(jnp.concatenate([side[NK:], jnp.zeros((8, LANES), F32)], axis=0))
    far_ref[NK : NK + 16, :] = high
    far_ref[NK + 16 :, :] = low


def spread(z, side, l):
    return lane_roll(side, LANES - (4 * l + 2))


def edge_lanes(z, l, left, right, old):
    lane = iota((NK, LANES), 1)
    left = pltpu.roll(left, 8 * l + 1, 1)
    right = pltpu.roll(right, 8 * l + 3, 1)
    return jnp.where(lane == 8 * l + 1, left, jnp.where(lane == 8 * l + 2, right, old))


def fold(v):
    half = v[0:8] + v[8:16]
    return half + pltpu.roll(half, 4, 0)


def row_of(stats, odd, first):
    return jnp.where(odd, stats[first ^ 1 : (first ^ 1) + 1], stats[first : first + 1])


def columns_kernel(z, a_ref, g_ref, st_ref, side_ref, far_ref, sums_ref, ext_ref, corner_ref, ga, ha):
    _, _, t = z.place()
    odd = t % 2 == 1
    even = jnp.where(odd, 0, 1)
    sg = jnp.where(odd, -0.5, 0.5)
    W = 2 * LANES
    ga[...] = a_ref[0 : z.o_st, :].astype(F32)
    ha[...] = far_ref[0:NK, :]
    stat_a = a_ref[z.o_st : z.o_st + z.st16, :].astype(F32) + a_ref[
        z.o_st + z.st16 : z.msg, :
    ].astype(F32)
    for l in range(z.levels + 1):
        ext_ref[0, l, :, 0:LANES] = st_ref[8 * l : 8 * l + 8, :]
        ext_ref[0, l, :, LANES:] = spread(z, side_ref[NK:, :], l)
        ext_ref[1, l, :, 0:LANES] = stat_a[8 * l : 8 * l + 8]
        ext_ref[1, l, :, LANES:] = spread(z, far_ref[NK:, :], l)
    k_of = iota((NK, W), 0)
    misc = ext_ref[0, z.levels]
    misc_a = ext_ref[1, z.levels]

    def sort(mech):
        return mech == (k_of // NM + 1).astype(F32)

    mech_0 = row_of(misc, odd, 0)
    mask_0, mask_1, mask_a = sort(mech_0), sort(row_of(misc, odd, 1)), sort(row_of(misc_a, odd, 0))
    head_0 = mech_0 == (k_of % NM + 1).astype(F32)
    weight_0 = row_of(misc, odd, 4)

    def level(l, carry):
        def field(ref, side, y):
            r = 2 * l + y
            own = ref[pl.ds(pl.multiple_of(r * NK, NK), NK), :]
            return jnp.concatenate([own, pltpu.roll(side, LANES - 2 - 4 * r, 1)], axis=1)

        side = side_ref[0:NK, :]
        q0, q1 = field(g_ref, side, 1 - even), field(g_ref, side, even)
        a1, a2 = field(ga, ha[...], 1 - even), field(ga, ha[...], even)
        own, other = ext_ref[0, l], ext_ref[1, l]
        cx_0, cx_1, cx_a = (
            0.5 * row_of(own, odd, 0), 0.5 * row_of(own, odd, 1), 0.5 * row_of(other, odd, 0)
        )
        cy_0, cy_1, cy_a = (
            sg * row_of(own, odd, 2), sg * row_of(own, odd, 3), sg * row_of(other, odd, 2)
        )

        def along(mid, cx):
            return (
                (1.0 - 4.0 * KD) * mid
                + (KD - cx) * pltpu.roll(mid, W - 1, 1)
                + (KD + cx) * pltpu.roll(mid, 1, 1)
            )

        f0 = along(q0, cx_0) + (KD - cy_0) * q1
        f1 = along(q1, cx_1) + (KD - cy_1) * a1 + (KD + cy_1) * q0
        fa = along(a1, cx_a) + (KD - cy_a) * a2 + (KD + cy_a) * q1
        f0, f1, fa = (
            fold(jnp.where(m, f, 0.0)) for m, f in ((mask_0, f0), (mask_1, f1), (mask_a, fa))
        )
        h0 = along(f0, cx_0) + (KD - cy_0) * f1
        h1 = along(f1, cx_1) + (KD - cy_1) * fa + (KD + cy_1) * f0
        kern_0, kern_1 = row_of(own, odd, 4), row_of(own, odd, 5)
        s0 = carry[0] + (kern_0 * h0)[:, 0:LANES]
        s1 = carry[1] + (kern_1 * h1)[:, 0:LANES]
        step = jnp.where(mask_0, KD + cy_0, 0.0)
        scale = jnp.where(head_0, kern_0 * weight_0, 0.0)
        left = (scale * pltpu.roll(step, 1, 1) * (KD + cx_0))[:, 0:LANES]
        right = (scale * pltpu.roll(step, W - 1, 1) * (KD - cx_0))[:, 0:LANES]
        return s0, s1, edge_lanes(z, l, left, right, carry[2])

    none = jnp.zeros((8, LANES), F32)
    s0, s1, corner = lax.fori_loop(
        0, z.levels, level, (none, none, jnp.zeros((NK, LANES), F32)), unroll=UNROLL
    )
    sums_ref[0:8, :] = s0
    sums_ref[8:16, :] = s1
    corner_ref[...] = corner


def beyond_kernel(z, b_ref, g_ref, st_ref, sums_ref, old_ref, part_ref, corner_ref, stat_ref):
    _, swath, t = z.place()
    odd = t % 2 == 1
    even = jnp.where(odd, 0, 1)
    has_b = jnp.logical_and(t > 0, t < z.nt - 1)
    sg = jnp.where(odd, -0.5, 0.5)
    for l in range(z.levels + 1):
        high = z.o_st + 8 * l
        both = b_ref[high : high + 8, :].astype(F32) + b_ref[
            high + z.st16 : high + z.st16 + 8, :
        ].astype(F32)
        stat_ref[l] = jnp.where(has_b, both, 0.0)
    k_of = iota((NK, LANES), 0)
    lane = iota((NK, LANES), 1)
    lane8 = iota((8, LANES), 1)
    sub8 = iota((8, LANES), 0)
    misc = st_ref[z.base : z.base + 8, :]
    mech_0 = row_of(misc, odd, 0)
    mech_b = row_of(stat_ref[z.levels], odd, 1)
    mask_0 = (mech_0 == (k_of // NM + 1).astype(F32)) & has_b
    mask_b = mech_b == (k_of // NM + 1).astype(F32)
    head_0 = mech_0 == (k_of % NM + 1).astype(F32)
    weight_0 = row_of(misc, odd, 4)

    def level(l, carry):
        def field(ref, y):
            at = pl.ds(pl.multiple_of((2 * l + y) * NK, NK), NK)
            return ref[at, :].astype(F32)

        q0 = field(g_ref, 1 - even)
        b1, b2 = field(b_ref, even), field(b_ref, 1 - even)
        own = st_ref[pl.ds(pl.multiple_of(8 * l, 8), 8), :]
        other = stat_ref[l]
        cx_0, cx_b = 0.5 * row_of(own, odd, 0), 0.5 * row_of(other, odd, 1)
        cy_0, cy_1, cy_b = (
            sg * row_of(own, odd, 2), sg * row_of(own, odd, 3), sg * row_of(other, odd, 3)
        )

        def along(mid, cx, lane):
            east = jnp.where(lane < LANES - 1, pltpu.roll(mid, LANES - 1, 1), 0.0)
            west = jnp.where(lane > 0, pltpu.roll(mid, 1, 1), 0.0)
            return (1.0 - 4.0 * KD) * mid + (KD - cx) * east + (KD + cx) * west

        fb = along(b1, cx_b, lane) + (KD - cy_b) * q0 + (KD + cy_b) * b2
        fb = fold(jnp.where(mask_b, fb, 0.0))
        f0 = fold(jnp.where(mask_0, (KD + cy_0) * b1, 0.0))
        kern_0, kern_1 = row_of(own, odd, 4), row_of(own, odd, 5)
        s0 = carry[0] + kern_0 * (along(f0, cx_0, lane8) + (KD + cy_0) * fb)
        s1 = carry[1] + kern_1 * (KD + cy_1) * f0
        step = jnp.where(head_0 & mask_b, kern_0 * weight_0 * (KD + cy_0), 0.0)
        left, right = step * (KD + cx_b), step * (KD - cx_b)
        corner = edge_lanes(z, l, left, right, carry[2])
        return s0, s1, corner

    s0, s1, corner = lax.fori_loop(
        0,
        z.levels,
        level,
        (sums_ref[0:8, :], sums_ref[8:16, :], jnp.zeros((NK, LANES), F32)),
        unroll=UNROLL,
    )
    corner_ref[...] = corner + old_ref[...]
    pixels = LANES // 2
    sub = iota((pixels, LANES), 0)
    total = jnp.zeros((8, LANES), F32)
    for y, sums in ((0, s0), (1, s1)):
        final = row_of(misc, odd, y) == (sub8 + 1).astype(F32)
        column = jnp.sum(jnp.where(final, sums, 0.0), axis=0, keepdims=True)
        column = column * row_of(misc, odd, 4 + y)
        hit = jnp.where(row_of(misc, odd, 2 + y) == sub.astype(F32), column, 0.0)
        tall = jnp.sum(hit, axis=1, keepdims=True)
        row = jnp.sum(
            jnp.where(sub == iota((pixels, LANES), 1), tall, 0.0), axis=0, keepdims=True
        )
        total = total + jnp.where(row_of(misc, odd, 6 + y) == sub8.astype(F32), row, 0.0)
    part_ref[...] = jnp.where(
        lane8 < pixels, total, jnp.where(sub8 == swath, st_ref[z.st : z.st + 1, :], 0.0)
    )


def corner_kernel(z, part_ref, corner_ref, far_ref, st_ref, out_ref, block_ref):
    _, _, t = z.place()
    odd = t % 2 == 1
    has_b = jnp.logical_and(t > 0, t < z.nt - 1)
    far = jnp.where(has_b, far_ref[...].astype(F32), 0.0)
    side = (far[NK : NK + 16] + far[NK + 16 :])[0:8]
    for l in range(z.levels + 1):
        block_ref[l] = spread(z, side, l)
    g = far[0:NK]
    g = jnp.where(odd, g, pltpu.roll(g, LANES - 4, 1))
    share = jnp.sum(corner_ref[...] * g, axis=0, keepdims=True)
    lane = iota((1, LANES), 1)
    sub8 = iota((8, LANES), 0)
    lane8 = iota((8, LANES), 1)
    misc = st_ref[z.base : z.base + 8, :]
    pixel = row_of(misc, odd, 2)
    owner = row_of(misc, odd, 6)
    total = part_ref[...]
    for c, column in ((1, 0), (2, LANES - 1)):
        value = jnp.sum(jnp.where(lane % 8 == c, share, 0.0), axis=1, keepdims=True)
        at = slice(column, column + 1)
        hit = (lane8.astype(F32) == pixel[:, at]) & (sub8.astype(F32) == owner[:, at])
        total = total + jnp.where(hit, value, 0.0)
    out_ref[...] = total


def product_kernel(
    z, own_ref, x0_ref, x1_ref, oa_ref, stat_ref, block_ref, d_ref, out_ref, dep_ref, v3, tall
):
    gx, swath, t = z.place()
    odd = t % 2 == 1

    def tiles(l):
        a = oa_ref[1, l]
        b = jnp.concatenate([stat_ref[l], block_ref[l]], axis=1)
        return jnp.where(odd, a, b), oa_ref[0, l], jnp.where(odd, b, a)

    miscs = tiles(z.levels)
    W = 2 * LANES
    pixels = LANES // 2
    left, right = sides_of(z, gx, x0_ref[...], x1_ref[...])

    def weigh(v):
        return v * lane_roll(v, pixels)

    deps = [weigh(v) for v in (own_ref[...], left, right)]
    sub = iota((8, LANES), 0)
    dep_ref[...] = jnp.sum(jnp.where(sub == swath, deps[0][0:8], 0.0), axis=0, keepdims=True)[
        :, 0:pixels
    ]
    outer = ((sub < 2) & (swath == 0)) | ((sub >= 4) & (swath == z.nsw - 1))

    def stack(f):
        out = jnp.zeros((8, W), F32)
        for s in range(3):
            for y in range(2):
                row = miscs[s][2 * f + y : 2 * f + y + 1]
                out = jnp.where(iota((8, W), 0) == 2 * s + y, row, out)
        return out

    owner = stack(3)
    index = stack(1).astype(jnp.int32)
    weight = stack(2)

    def find(dep, owner, index):
        found = jnp.zeros((8, LANES), F32)
        for o in range(z.nsw):
            row = jnp.where(outer, dep[8 + o : 9 + o, :], dep[o : o + 1, :])
            value = jnp.take_along_axis(row, index, axis=1)
            found = jnp.where(owner == float(o), value, found)
        return found

    lane = iota((8, LANES), 1)
    far = (owner[:, LANES:], index[:, LANES:])
    beside = jnp.where(
        lane < 2, find(deps[2], *far), jnp.where(lane >= LANES - 2, find(deps[1], *far), 0.0)
    )
    near = find(deps[0], owner[:, 0:LANES], index[:, 0:LANES])
    back = weight * jnp.concatenate([near, beside], axis=1)
    place = [(s, y) for s in range(3) for y in range(2)]
    k_of = iota((NK, W), 0) // NM
    m_of = iota((8, W), 0) % NM
    drive = []
    for i, (s, y) in enumerate(place):
        mech = miscs[s][y : y + 1]
        drive.append(jnp.where(mech == (m_of + 1).astype(F32), back[i : i + 1, :], 0.0))
    masks = [
        miscs[s][y : y + 1] == (k_of + 1).astype(F32) for s, y in place[1:5]
    ]

    def unadvect(mid, cx, up, cy_up, down, cy_down):
        return (
            (1.0 - 4.0 * KD) * mid
            + pltpu.roll((KD - cx) * mid, 1, 1)
            + pltpu.roll((KD + cx) * mid, W - 1, 1)
            + (KD - cy_up) * up
            + (KD + cy_down) * down
        )

    def level(l, carry):
        stats = tiles(l)
        cx = [0.5 * stats[s][y : y + 1] for s, y in place]
        cy = [0.5 * stats[s][2 + y : 3 + y] for s, y in place]
        kern = [stats[s][4 + y : 5 + y] for s, y in place]
        w = [kern[i] * drive[i] for i in range(6)]
        u = []
        for i in range(1, 5):
            mid = unadvect(w[i], cx[i], w[i - 1], cy[i - 1], w[i + 1], cy[i + 1])
            twice = jnp.concatenate([mid, mid], axis=0)
            u.append(jnp.where(masks[i - 1], twice, 0.0))
        for y in range(2):
            i = 2 + y
            v = unadvect(u[i - 1], cx[i], u[i - 2], cy[i - 1], u[i], cy[i + 1])[:, 0:LANES]
            high, low = split(v)
            at = pl.ds(pl.multiple_of((2 * l + y) * LANES, LANES), LANES)
            v3[0:NK, at] = high
            v3[NK : 2 * NK, at] = low
            v3[2 * NK :, at] = high
        return carry

    lax.fori_loop(0, z.levels, level, 0, unroll=UNROLL)
    d = d_ref[...]
    for r in range(0, z.rows, 2):
        both = lax.dot_general(
            d, v3[:, r * LANES : (r + 2) * LANES], (((0,), (0,)), ((), ())),
            preferred_element_type=F32,
        )
        tall[pl.ds(r, z.species, stride=z.rows), :] = both[:, 0:LANES]
        tall[pl.ds(r + 1, z.species, stride=z.rows), :] = both[:, LANES:]
    out_ref[...] = tall[...].astype(BF)


def shape(*dims, dtype=F32):
    return jax.ShapeDtypeStruct(dims, dtype)


LIMIT = pltpu.CompilerParams(vmem_limit_bytes=32 * 1024 * 1024)


def swaps_of(sizes):
    ngx, ngy, nsw = sizes
    nt = ngy * nsw

    def pairs(f):
        return [(g * nt + t, f(g, t)) for g in range(ngx) for t in range(nt)]

    def other(i, parity):
        return i + 1 if i % 2 == parity else i - 1

    def along_x(parity, flip):
        def to(g, t):
            n = other(g, parity)
            return n * nt + (t ^ flip) if 0 <= n < ngx else g * nt + (t ^ 1)

        return pairs(to)

    def along_y(parity):
        def to(g, t):
            n = other(t, parity)
            return g * nt + n if 0 <= n < nt else (g ^ 1) * nt + t

        return pairs(to)

    def along_z(g, t):
        gy, s = divmod(t, nsw)
        chip, core = divmod(s, 2)
        last = nsw // 2 - 1
        up = 1 if chip == 0 else -1
        if chip in (0, last) and 0 <= gy + up < ngy:
            gy, core = gy + up, 1 - core
        elif gy == ngy - 1 and chip < last:
            chip += 1
        elif gy == 0 and chip > 0:
            chip -= 1
        else:
            core = 1 - core
        return g * nt + gy * nsw + 2 * chip + core

    return along_x, along_y, pairs(along_z)


def per_device(
    sizes,
    direction,
    courant_x,
    courant_y,
    kernel,
    mechanism,
    propagator,
    footprint_pixel,
    footprint_weight,
    footprint_owner,
    precision,
):
    species, levels = direction.shape[:2]
    z = Sizes(sizes, species, levels)
    along_x, along_y, along_z = swaps_of(sizes)
    nsw = z.nsw

    def move(v, perm):
        return lax.ppermute(v, ALL, perm)

    cells = (species * z.rows, LANES)
    pixels = precision.shape[0]
    g, msg, edge, st, d = pl.pallas_call(
        functools.partial(project_kernel, z),
        out_shape=(
            shape(z.o_st, LANES),
            shape(z.msg, LANES, dtype=BF),
            shape(z.edge, LANES),
            shape(z.st16, LANES),
            shape(3 * NK, species, dtype=BF),
        ),
        in_specs=[HBM] * 10,
        out_specs=(VMEM,) * 5,
        scratch_shapes=[
            pltpu.VMEM(cells, BF),
            pltpu.VMEM(propagator.shape, BF),
            pltpu.VMEM(courant_x.shape, F32),
            pltpu.VMEM(courant_x.shape, F32),
            pltpu.VMEM(courant_x.shape, F32),
            pltpu.VMEM(mechanism.shape, jnp.int32),
            pltpu.VMEM(mechanism.shape, jnp.int32),
            pltpu.VMEM(mechanism.shape, F32),
            pltpu.VMEM((1, 2), jnp.int32),
            pltpu.VMEM((1, pixels), F32),
            pltpu.VMEM(cells, F32),
            pltpu.SemaphoreType.DMA((10,)),
        ],
        compiler_params=LIMIT,
        name="project",
    )(
        *(
            pltpu.with_memory_space_constraint(v, pltpu.HBM)
            for v in (
                direction.reshape(cells), propagator, courant_x, courant_y, kernel, mechanism,
                footprint_pixel, footprint_weight, footprint_owner.reshape(1, 2),
                precision.reshape(1, -1),
            )
        )
    )
    e0 = move(edge, along_x(0, 0))
    e1 = move(edge, along_x(1, 0))
    m_b = move(msg, along_y(1))
    m_a = move(msg, along_y(0))
    side, far = pl.pallas_call(
        functools.partial(edges_kernel, z),
        out_shape=(shape(z.edge, LANES), shape(z.far, LANES, dtype=BF)),
        in_specs=[VMEM, VMEM],
        out_specs=(VMEM, VMEM),
        compiler_params=LIMIT,
        cost_estimate=pl.CostEstimate(
            flops=20_000_000_000, bytes_accessed=1024, transcendentals=0
        ),
        name="edges",
    )(e0, e1)
    far_b = move(far, along_y(1))
    sums, ext, corner = pl.pallas_call(
        functools.partial(columns_kernel, z),
        out_shape=(
            shape(16, LANES), shape(2, levels + 1, 8, 2 * LANES), shape(NK, LANES)
        ),
        in_specs=[VMEM] * 5,
        out_specs=(VMEM,) * 3,
        scratch_shapes=[pltpu.VMEM((z.o_st, LANES), F32), pltpu.VMEM((NK, LANES), F32)],
        compiler_params=LIMIT,
        name="columns",
    )(m_a, g, st, side, move(side, along_y(0)))
    part, corner, stat = pl.pallas_call(
        functools.partial(beyond_kernel, z),
        out_shape=(shape(8, LANES), shape(NK, LANES), shape(levels + 1, 8, LANES)),
        in_specs=[VMEM] * 5,
        out_specs=(VMEM,) * 3,
        compiler_params=LIMIT,
        name="beyond",
    )(m_b, g, st, sums, corner)
    part, block = pl.pallas_call(
        functools.partial(corner_kernel, z),
        out_shape=(shape(8, LANES), shape(levels + 1, 8, LANES)),
        in_specs=[VMEM] * 4,
        out_specs=(VMEM, VMEM),
        compiler_params=LIMIT,
        name="corner",
    )(part, corner, far_b, st)
    part = part + lax.ppermute(part, "swath", [(i, i ^ 1) for i in range(nsw)])
    turns = [
        lax.ppermute(part, "swath", [(i, (i + 2 * k) % nsw ^ 1) for i in range(nsw)])
        for k in TURNS
    ]
    for turn in turns:
        part = part + turn
    both = jnp.concatenate([part, move(part, along_z)], axis=0)
    b0 = move(both, along_x(0, 1))
    b1 = move(both, along_x(1, 1))
    product, dep = pl.pallas_call(
        functools.partial(product_kernel, z),
        out_shape=(shape(*cells, dtype=BF), shape(1, pixels)),
        in_specs=[VMEM] * 7,
        out_specs=(VMEM, VMEM),
        scratch_shapes=[
            pltpu.VMEM((3 * NK, z.rows * LANES), BF),
            pltpu.VMEM(cells, F32),
        ],
        compiler_params=LIMIT,
        name="product",
    )(both, b0, b1, ext, stat, block, d)
    return product.reshape(direction.shape), dep.reshape(-1)


def solution(mesh):
    placed = (
        P(None, None, ("gy", "swath"), "gx"),
        P(None, ("gy", "swath"), "gx"),
        P(None, ("gy", "swath"), "gx"),
        P(None, ("gy", "swath"), "gx"),
        P(("gy", "swath"), "gx"),
        P(),
        P(("gy", "swath"), "gx"),
        P(("gy", "swath"), "gx"),
        P(("gx", "gy", "swath"), None),
        P(("gx", "gy", "swath")),
    )
    sizes = tuple(mesh.shape[a] for a in ALL)
    return jax.shard_map(
        functools.partial(per_device, sizes),
        mesh=mesh,
        in_specs=placed,
        out_specs=(P(None, None, ("gy", "swath"), "gx"), P(("gx", "gy", "swath"))),
        check_vma=False,
    )
```

```python
import functools

import jax
import jax.numpy as jnp
from jax import lax
from jax.experimental import pallas as pl
from jax.experimental.pallas import tpu as pltpu
from jax.sharding import PartitionSpec as P

KD = 0.2
UNROLL = 10
TURNS = (1, 3, 2)
ALL = ("gx", "gy", "swath")
LANES = 128
NM = 4
NK = NM * NM
BF = jnp.bfloat16
F32 = jnp.float32
VMEM = pl.BlockSpec(memory_space=pltpu.VMEM)
ANY = pl.BlockSpec(memory_space=pl.ANY)
HBM = pl.BlockSpec(memory_space=pltpu.HBM)


def iota(shape, dim):
    return lax.broadcasted_iota(jnp.int32, shape, dim)


def lane_roll(v, shift):
    return pltpu.roll(v, shift % v.shape[-1], v.ndim - 1)


def split(v):
    high = v.astype(BF)
    return high, (v - high.astype(F32)).astype(BF)


class Sizes:
    def __init__(self, sizes, species, levels):
        self.ngx, self.ngy, self.nsw = sizes
        self.nt = self.ngy * self.nsw
        self.species = species
        self.levels = levels
        self.rows = 2 * levels
        self.base = 8 * levels
        self.st = self.base + 8
        self.st16 = -(-(self.st + 1) // 16) * 16
        self.o_st = self.rows * NK
        self.msg = self.o_st + 2 * self.st16
        self.edge = NK + 8
        self.far = NK + 2 * 16

    def place(self):
        gx = lax.axis_index("gx")
        swath = lax.axis_index("swath")
        return gx, swath, lax.axis_index("gy") * self.nsw + swath


def project_kernel(
    z, dir_hbm, prop_hbm, cx_hbm, cy_hbm, kern_hbm, mech_hbm, pix_hbm, wgt_hbm, own_hbm, prec_hbm,
    g_ref, msg_ref, edge_ref, st_ref, d_ref,
    dir_ref, prop_ref, cx_ref, cy_ref, kern_ref, mech_ref, pix_ref, wgt_ref, own_ref, prec_ref,
    wide, sems,
):
    sources = (
        prop_hbm, dir_hbm, cx_hbm, cy_hbm, kern_hbm, mech_hbm, pix_hbm, wgt_hbm, own_hbm, prec_hbm
    )
    targets = (
        prop_ref, dir_ref, cx_ref, cy_ref, kern_ref, mech_ref, pix_ref, wgt_ref, own_ref, prec_ref
    )
    copies = [
        pltpu.make_async_copy(a, b, sems.at[i]) for i, (a, b) in enumerate(zip(sources, targets))
    ]
    for copy in copies:
        copy.start()
    species = z.species
    copies[0].wait()
    k_of = iota((NK, species), 0)
    heads = jnp.zeros((NK, species), F32)
    for m in range(NM):
        row = prop_ref[m][0:1, :].astype(F32)
        heads = heads + jnp.where(k_of % NM == m, row, 0.0)
    total = heads + jnp.where(iota((NK, species), 1) == 0, 1.0, 0.0)
    lhs = heads.astype(BF)
    for m in range(NM):
        matrix = prop_ref[m]
        term = jnp.dot(lhs, matrix, preferred_element_type=F32)
        total = total + jnp.where(k_of // NM == m, term + matrix[0:1, :].astype(F32), 0.0)
    high, low = split(total)
    both = jnp.concatenate([high, low], axis=0)
    d_ref[...] = jnp.concatenate([high, high, low], axis=0)
    copies[1].wait()
    wide[...] = dir_ref[...].astype(F32)
    cells = jnp.concatenate(
        [wide[pl.ds(r, species, stride=z.rows), :].astype(BF) for r in range(z.rows)], axis=1
    )
    g32 = jnp.dot(both, cells, preferred_element_type=F32)
    g = g32[:NK] + g32[NK:]
    lane = iota((NK, LANES), 1)
    edge = jnp.zeros((NK, LANES), F32)
    for r in range(z.rows):
        part = g[:, r * LANES : (r + 1) * LANES]
        g_ref[r * NK : (r + 1) * NK, :] = part
        msg_ref[r * NK : (r + 1) * NK, :] = part.astype(BF)
        edge = jnp.where(lane // 4 == r, lane_roll(part, 4 * r + 2), edge)
    edge_ref[0:NK, :] = edge
    for copy in copies[2:]:
        copy.wait()
    lane = iota((8, LANES), 1)
    side = jnp.zeros((8, LANES), F32)
    blank = jnp.zeros((2, LANES), F32)
    own = jnp.where(iota((2, LANES), 0) == 0, own_ref[:, 0:1], own_ref[:, 1:2])
    for l in range(z.levels + 1):
        if l < z.levels:
            parts = [cx_ref[l], cy_ref[l], kern_ref[l], blank]
        else:
            parts = [
                (mech_ref[...] + 1).astype(F32),
                pix_ref[...].astype(F32),
                wgt_ref[...],
                own.astype(F32),
            ]
        block = jnp.concatenate(parts, axis=0)
        st_ref[8 * l : 8 * l + 8, :] = block
        side = jnp.where(lane // 4 == l, lane_roll(block, 4 * l + 2), side)
    pixels = prec_ref.shape[1]
    last = jnp.concatenate([jnp.zeros((1, LANES - pixels), F32), prec_ref[...]], axis=1)
    st_ref[z.st :, :] = jnp.broadcast_to(last, (z.st16 - z.st, LANES))
    edge_ref[NK:, :] = side
    high, low = split(st_ref[...])
    msg_ref[z.o_st : z.o_st + z.st16, :] = high
    msg_ref[z.o_st + z.st16 : z.o_st + 2 * z.st16, :] = low


def sides_of(z, gx, x0, x1):
    even = gx % 2 == 0
    right = jnp.where(even, x0, x1)
    left = jnp.where(even, x1, x0)
    return jnp.where(gx > 0, left, 0.0), jnp.where(gx < z.ngx - 1, right, 0.0)


def edges_kernel(z, x0_ref, x1_ref, side_ref, far_ref):
    gx, _, _ = z.place()
    left, right = sides_of(z, gx, x0_ref[...], x1_ref[...])
    side = jnp.where(iota(left.shape, 1) % 4 < 2, left, right)
    side_ref[...] = side
    far_ref[0:NK, :] = side[0:NK].astype(BF)
    high, low = split(jnp.concatenate([side[NK:], jnp.zeros((8, LANES), F32)], axis=0))
    far_ref[NK : NK + 16, :] = high
    far_ref[NK + 16 :, :] = low


def spread(z, side, l):
    return lane_roll(side, LANES - (4 * l + 2))


def edge_lanes(z, l, left, right, old):
    lane = iota((NK, LANES), 1)
    left = pltpu.roll(left, 8 * l + 1, 1)
    right = pltpu.roll(right, 8 * l + 3, 1)
    return jnp.where(lane == 8 * l + 1, left, jnp.where(lane == 8 * l + 2, right, old))


def fold(v):
    half = v[0:8] + v[8:16]
    return half + pltpu.roll(half, 4, 0)


def row_of(stats, odd, first):
    return jnp.where(odd, stats[first ^ 1 : (first ^ 1) + 1], stats[first : first + 1])


def columns_kernel(z, a_ref, g_ref, st_ref, side_ref, far_ref, sums_ref, ext_ref, corner_ref, ga, ha):
    _, _, t = z.place()
    odd = t % 2 == 1
    even = jnp.where(odd, 0, 1)
    sg = jnp.where(odd, -0.5, 0.5)
    W = 2 * LANES
    ga[...] = a_ref[0 : z.o_st, :].astype(F32)
    ha[...] = far_ref[0:NK, :]
    stat_a = a_ref[z.o_st : z.o_st + z.st16, :].astype(F32) + a_ref[
        z.o_st + z.st16 : z.msg, :
    ].astype(F32)
    for l in range(z.levels + 1):
        ext_ref[0, l, :, 0:LANES] = st_ref[8 * l : 8 * l + 8, :]
        ext_ref[0, l, :, LANES:] = spread(z, side_ref[NK:, :], l)
        ext_ref[1, l, :, 0:LANES] = stat_a[8 * l : 8 * l + 8]
        ext_ref[1, l, :, LANES:] = spread(z, far_ref[NK:, :], l)
    k_of = iota((NK, W), 0)
    misc = ext_ref[0, z.levels]
    misc_a = ext_ref[1, z.levels]

    def sort(mech):
        return mech == (k_of // NM + 1).astype(F32)

    mech_0 = row_of(misc, odd, 0)
    mask_0, mask_1, mask_a = sort(mech_0), sort(row_of(misc, odd, 1)), sort(row_of(misc_a, odd, 0))
    head_0 = mech_0 == (k_of % NM + 1).astype(F32)
    weight_0 = row_of(misc, odd, 4)

    def level(l, carry):
        def field(ref, side, y):
            r = 2 * l + y
            own = ref[pl.ds(pl.multiple_of(r * NK, NK), NK), :]
            return jnp.concatenate([own, pltpu.roll(side, LANES - 2 - 4 * r, 1)], axis=1)

        side = side_ref[0:NK, :]
        q0, q1 = field(g_ref, side, 1 - even), field(g_ref, side, even)
        a1, a2 = field(ga, ha[...], 1 - even), field(ga, ha[...], even)
        own, other = ext_ref[0, l], ext_ref[1, l]
        cx_0, cx_1, cx_a = (
            0.5 * row_of(own, odd, 0), 0.5 * row_of(own, odd, 1), 0.5 * row_of(other, odd, 0)
        )
        cy_0, cy_1, cy_a = (
            sg * row_of(own, odd, 2), sg * row_of(own, odd, 3), sg * row_of(other, odd, 2)
        )

        def along(mid, cx):
            return (
                (1.0 - 4.0 * KD) * mid
                + (KD - cx) * pltpu.roll(mid, W - 1, 1)
                + (KD + cx) * pltpu.roll(mid, 1, 1)
            )

        f0 = along(q0, cx_0) + (KD - cy_0) * q1
        f1 = along(q1, cx_1) + (KD - cy_1) * a1 + (KD + cy_1) * q0
        fa = along(a1, cx_a) + (KD - cy_a) * a2 + (KD + cy_a) * q1
        f0, f1, fa = (
            fold(jnp.where(m, f, 0.0)) for m, f in ((mask_0, f0), (mask_1, f1), (mask_a, fa))
        )
        h0 = along(f0, cx_0) + (KD - cy_0) * f1
        h1 = along(f1, cx_1) + (KD - cy_1) * fa + (KD + cy_1) * f0
        kern_0, kern_1 = row_of(own, odd, 4), row_of(own, odd, 5)
        s0 = carry[0] + (kern_0 * h0)[:, 0:LANES]
        s1 = carry[1] + (kern_1 * h1)[:, 0:LANES]
        step = jnp.where(mask_0, KD + cy_0, 0.0)
        scale = jnp.where(head_0, kern_0 * weight_0, 0.0)
        left = (scale * pltpu.roll(step, 1, 1) * (KD + cx_0))[:, 0:LANES]
        right = (scale * pltpu.roll(step, W - 1, 1) * (KD - cx_0))[:, 0:LANES]
        return s0, s1, edge_lanes(z, l, left, right, carry[2])

    none = jnp.zeros((8, LANES), F32)
    s0, s1, corner = lax.fori_loop(
        0, z.levels, level, (none, none, jnp.zeros((NK, LANES), F32)), unroll=UNROLL
    )
    sums_ref[0:8, :] = s0
    sums_ref[8:16, :] = s1
    corner_ref[...] = corner


def beyond_kernel(z, b_ref, g_ref, st_ref, sums_ref, old_ref, part_ref, corner_ref, stat_ref):
    _, swath, t = z.place()
    odd = t % 2 == 1
    even = jnp.where(odd, 0, 1)
    has_b = jnp.logical_and(t > 0, t < z.nt - 1)
    sg = jnp.where(odd, -0.5, 0.5)
    for l in range(z.levels + 1):
        high = z.o_st + 8 * l
        both = b_ref[high : high + 8, :].astype(F32) + b_ref[
            high + z.st16 : high + z.st16 + 8, :
        ].astype(F32)
        stat_ref[l] = jnp.where(has_b, both, 0.0)
    k_of = iota((NK, LANES), 0)
    lane = iota((NK, LANES), 1)
    lane8 = iota((8, LANES), 1)
    sub8 = iota((8, LANES), 0)
    misc = st_ref[z.base : z.base + 8, :]
    mech_0 = row_of(misc, odd, 0)
    mech_b = row_of(stat_ref[z.levels], odd, 1)
    mask_0 = (mech_0 == (k_of // NM + 1).astype(F32)) & has_b
    mask_b = mech_b == (k_of // NM + 1).astype(F32)
    head_0 = mech_0 == (k_of % NM + 1).astype(F32)
    weight_0 = row_of(misc, odd, 4)

    def level(l, carry):
        def field(ref, y):
            at = pl.ds(pl.multiple_of((2 * l + y) * NK, NK), NK)
            return ref[at, :].astype(F32)

        q0 = field(g_ref, 1 - even)
        b1, b2 = field(b_ref, even), field(b_ref, 1 - even)
        own = st_ref[pl.ds(pl.multiple_of(8 * l, 8), 8), :]
        other = stat_ref[l]
        cx_0, cx_b = 0.5 * row_of(own, odd, 0), 0.5 * row_of(other, odd, 1)
        cy_0, cy_1, cy_b = (
            sg * row_of(own, odd, 2), sg * row_of(own, odd, 3), sg * row_of(other, odd, 3)
        )

        def along(mid, cx, lane):
            east = jnp.where(lane < LANES - 1, pltpu.roll(mid, LANES - 1, 1), 0.0)
            west = jnp.where(lane > 0, pltpu.roll(mid, 1, 1), 0.0)
            return (1.0 - 4.0 * KD) * mid + (KD - cx) * east + (KD + cx) * west

        fb = along(b1, cx_b, lane) + (KD - cy_b) * q0 + (KD + cy_b) * b2
        fb = fold(jnp.where(mask_b, fb, 0.0))
        f0 = fold(jnp.where(mask_0, (KD + cy_0) * b1, 0.0))
        kern_0, kern_1 = row_of(own, odd, 4), row_of(own, odd, 5)
        s0 = carry[0] + kern_0 * (along(f0, cx_0, lane8) + (KD + cy_0) * fb)
        s1 = carry[1] + kern_1 * (KD + cy_1) * f0
        step = jnp.where(head_0 & mask_b, kern_0 * weight_0 * (KD + cy_0), 0.0)
        left, right = step * (KD + cx_b), step * (KD - cx_b)
        corner = edge_lanes(z, l, left, right, carry[2])
        return s0, s1, corner

    s0, s1, corner = lax.fori_loop(
        0,
        z.levels,
        level,
        (sums_ref[0:8, :], sums_ref[8:16, :], jnp.zeros((NK, LANES), F32)),
        unroll=UNROLL,
    )
    corner_ref[...] = corner + old_ref[...]
    pixels = LANES // 2
    sub = iota((pixels, LANES), 0)
    total = jnp.zeros((8, LANES), F32)
    for y, sums in ((0, s0), (1, s1)):
        final = row_of(misc, odd, y) == (sub8 + 1).astype(F32)
        column = jnp.sum(jnp.where(final, sums, 0.0), axis=0, keepdims=True)
        column = column * row_of(misc, odd, 4 + y)
        hit = jnp.where(row_of(misc, odd, 2 + y) == sub.astype(F32), column, 0.0)
        tall = jnp.sum(hit, axis=1, keepdims=True)
        row = jnp.sum(
            jnp.where(sub == iota((pixels, LANES), 1), tall, 0.0), axis=0, keepdims=True
        )
        total = total + jnp.where(row_of(misc, odd, 6 + y) == sub8.astype(F32), row, 0.0)
    part_ref[...] = jnp.where(
        lane8 < pixels, total, jnp.where(sub8 == swath, st_ref[z.st : z.st + 1, :], 0.0)
    )


def corner_kernel(z, part_ref, corner_ref, far_ref, st_ref, out_ref, block_ref):
    _, _, t = z.place()
    odd = t % 2 == 1
    has_b = jnp.logical_and(t > 0, t < z.nt - 1)
    far = jnp.where(has_b, far_ref[...].astype(F32), 0.0)
    side = (far[NK : NK + 16] + far[NK + 16 :])[0:8]
    for l in range(z.levels + 1):
        block_ref[l] = spread(z, side, l)
    g = far[0:NK]
    g = jnp.where(odd, g, pltpu.roll(g, LANES - 4, 1))
    share = jnp.sum(corner_ref[...] * g, axis=0, keepdims=True)
    lane = iota((1, LANES), 1)
    sub8 = iota((8, LANES), 0)
    lane8 = iota((8, LANES), 1)
    misc = st_ref[z.base : z.base + 8, :]
    pixel = row_of(misc, odd, 2)
    owner = row_of(misc, odd, 6)
    total = part_ref[...]
    for c, column in ((1, 0), (2, LANES - 1)):
        value = jnp.sum(jnp.where(lane % 8 == c, share, 0.0), axis=1, keepdims=True)
        at = slice(column, column + 1)
        hit = (lane8.astype(F32) == pixel[:, at]) & (sub8.astype(F32) == owner[:, at])
        total = total + jnp.where(hit, value, 0.0)
    out_ref[...] = total


def product_kernel(
    z, own_ref, x0_ref, x1_ref, oa_ref, stat_ref, block_ref, d_ref, out_ref, dep_ref, v3, tall
):
    gx, swath, t = z.place()
    odd = t % 2 == 1

    def tiles(l):
        a = oa_ref[1, l]
        b = jnp.concatenate([stat_ref[l], block_ref[l]], axis=1)
        return jnp.where(odd, a, b), oa_ref[0, l], jnp.where(odd, b, a)

    miscs = tiles(z.levels)
    W = 2 * LANES
    pixels = LANES // 2
    left, right = sides_of(z, gx, x0_ref[...], x1_ref[...])

    def weigh(v):
        return v * lane_roll(v, pixels)

    deps = [weigh(v) for v in (own_ref[...], left, right)]
    sub = iota((8, LANES), 0)
    dep_ref[...] = jnp.sum(jnp.where(sub == swath, deps[0][0:8], 0.0), axis=0, keepdims=True)[
        :, 0:pixels
    ]
    outer = ((sub < 2) & (swath == 0)) | ((sub >= 4) & (swath == z.nsw - 1))

    def stack(f):
        out = jnp.zeros((8, W), F32)
        for s in range(3):
            for y in range(2):
                row = miscs[s][2 * f + y : 2 * f + y + 1]
                out = jnp.where(iota((8, W), 0) == 2 * s + y, row, out)
        return out

    owner = stack(3)
    index = stack(1).astype(jnp.int32)
    weight = stack(2)

    def find(dep, owner, index):
        found = jnp.zeros((8, LANES), F32)
        for o in range(z.nsw):
            row = jnp.where(outer, dep[8 + o : 9 + o, :], dep[o : o + 1, :])
            value = jnp.take_along_axis(row, index, axis=1)
            found = jnp.where(owner == float(o), value, found)
        return found

    lane = iota((8, LANES), 1)
    far = (owner[:, LANES:], index[:, LANES:])
    beside = jnp.where(
        lane < 2, find(deps[2], *far), jnp.where(lane >= LANES - 2, find(deps[1], *far), 0.0)
    )
    near = find(deps[0], owner[:, 0:LANES], index[:, 0:LANES])
    back = weight * jnp.concatenate([near, beside], axis=1)
    place = [(s, y) for s in range(3) for y in range(2)]
    k_of = iota((NK, W), 0) // NM
    m_of = iota((8, W), 0) % NM
    drive = []
    for i, (s, y) in enumerate(place):
        mech = miscs[s][y : y + 1]
        drive.append(jnp.where(mech == (m_of + 1).astype(F32), back[i : i + 1, :], 0.0))
    masks = [
        miscs[s][y : y + 1] == (k_of + 1).astype(F32) for s, y in place[1:5]
    ]

    def unadvect(mid, cx, up, cy_up, down, cy_down):
        return (
            (1.0 - 4.0 * KD) * mid
            + pltpu.roll((KD - cx) * mid, 1, 1)
            + pltpu.roll((KD + cx) * mid, W - 1, 1)
            + (KD - cy_up) * up
            + (KD + cy_down) * down
        )

    def level(l, carry):
        stats = tiles(l)
        cx = [0.5 * stats[s][y : y + 1] for s, y in place]
        cy = [0.5 * stats[s][2 + y : 3 + y] for s, y in place]
        kern = [stats[s][4 + y : 5 + y] for s, y in place]
        w = [kern[i] * drive[i] for i in range(6)]
        u = []
        for i in range(1, 5):
            mid = unadvect(w[i], cx[i], w[i - 1], cy[i - 1], w[i + 1], cy[i + 1])
            twice = jnp.concatenate([mid, mid], axis=0)
            u.append(jnp.where(masks[i - 1], twice, 0.0))
        for y in range(2):
            i = 2 + y
            v = unadvect(u[i - 1], cx[i], u[i - 2], cy[i - 1], u[i], cy[i + 1])[:, 0:LANES]
            high, low = split(v)
            at = pl.ds(pl.multiple_of((2 * l + y) * LANES, LANES), LANES)
            v3[0:NK, at] = high
            v3[NK : 2 * NK, at] = low
            v3[2 * NK :, at] = high
        return carry

    lax.fori_loop(0, z.levels, level, 0, unroll=UNROLL)
    d = d_ref[...]
    for r in range(0, z.rows, 2):
        both = lax.dot_general(
            d, v3[:, r * LANES : (r + 2) * LANES], (((0,), (0,)), ((), ())),
            preferred_element_type=F32,
        )
        tall[pl.ds(r, z.species, stride=z.rows), :] = both[:, 0:LANES]
        tall[pl.ds(r + 1, z.species, stride=z.rows), :] = both[:, LANES:]
    out_ref[...] = tall[...].astype(BF)


def shape(*dims, dtype=F32):
    return jax.ShapeDtypeStruct(dims, dtype)


LIMIT = pltpu.CompilerParams(vmem_limit_bytes=32 * 1024 * 1024)


def swaps_of(sizes):
    ngx, ngy, nsw = sizes
    nt = ngy * nsw

    def pairs(f):
        return [(g * nt + t, f(g, t)) for g in range(ngx) for t in range(nt)]

    def other(i, parity):
        return i + 1 if i % 2 == parity else i - 1

    def along_x(parity, flip):
        def to(g, t):
            n = other(g, parity)
            return n * nt + (t ^ flip) if 0 <= n < ngx else g * nt + (t ^ 1)

        return pairs(to)

    def along_y(parity):
        def to(g, t):
            n = other(t, parity)
            return g * nt + n if 0 <= n < nt else (g ^ 1) * nt + t

        return pairs(to)

    def along_z(g, t):
        gy, s = divmod(t, nsw)
        chip, core = divmod(s, 2)
        last = nsw // 2 - 1
        up = 1 if chip == 0 else -1
        if chip in (0, last) and 0 <= gy + up < ngy:
            gy, core = gy + up, 1 - core
        elif gy == ngy - 1 and chip < last:
            chip += 1
        elif gy == 0 and chip > 0:
            chip -= 1
        else:
            core = 1 - core
        return g * nt + gy * nsw + 2 * chip + core

    return along_x, along_y, pairs(along_z)


def per_device(
    sizes,
    direction,
    courant_x,
    courant_y,
    kernel,
    mechanism,
    propagator,
    footprint_pixel,
    footprint_weight,
    footprint_owner,
    precision,
):
    species, levels = direction.shape[:2]
    z = Sizes(sizes, species, levels)
    along_x, along_y, along_z = swaps_of(sizes)
    nsw = z.nsw

    def move(v, perm):
        return lax.ppermute(v, ALL, perm)

    cells = (species * z.rows, LANES)
    pixels = precision.shape[0]
    g, msg, edge, st, d = pl.pallas_call(
        functools.partial(project_kernel, z),
        out_shape=(
            shape(z.o_st, LANES),
            shape(z.msg, LANES, dtype=BF),
            shape(z.edge, LANES),
            shape(z.st16, LANES),
            shape(3 * NK, species, dtype=BF),
        ),
        in_specs=[HBM] * 10,
        out_specs=(VMEM,) * 5,
        scratch_shapes=[
            pltpu.VMEM(cells, BF),
            pltpu.VMEM(propagator.shape, BF),
            pltpu.VMEM(courant_x.shape, F32),
            pltpu.VMEM(courant_x.shape, F32),
            pltpu.VMEM(courant_x.shape, F32),
            pltpu.VMEM(mechanism.shape, jnp.int32),
            pltpu.VMEM(mechanism.shape, jnp.int32),
            pltpu.VMEM(mechanism.shape, F32),
            pltpu.VMEM((1, 2), jnp.int32),
            pltpu.VMEM((1, pixels), F32),
            pltpu.VMEM(cells, F32),
            pltpu.SemaphoreType.DMA((10,)),
        ],
        compiler_params=LIMIT,
        name="project",
    )(
        *(
            pltpu.with_memory_space_constraint(v, pltpu.HBM)
            for v in (
                direction.reshape(cells), propagator, courant_x, courant_y, kernel, mechanism,
                footprint_pixel, footprint_weight, footprint_owner.reshape(1, 2),
                precision.reshape(1, -1),
            )
        )
    )
    e0 = move(edge, along_x(0, 0))
    e1 = move(edge, along_x(1, 0))
    m_b = move(msg, along_y(1))
    m_a = move(msg, along_y(0))
    side, far = pl.pallas_call(
        functools.partial(edges_kernel, z),
        out_shape=(shape(z.edge, LANES), shape(z.far, LANES, dtype=BF)),
        in_specs=[VMEM, VMEM],
        out_specs=(VMEM, VMEM),
        compiler_params=LIMIT,
        cost_estimate=pl.CostEstimate(
            flops=20_000_000_000, bytes_accessed=1024, transcendentals=0
        ),
        name="edges",
    )(e0, e1)
    far_b = move(far, along_y(1))
    sums, ext, corner = pl.pallas_call(
        functools.partial(columns_kernel, z),
        out_shape=(
            shape(16, LANES), shape(2, levels + 1, 8, 2 * LANES), shape(NK, LANES)
        ),
        in_specs=[VMEM] * 5,
        out_specs=(VMEM,) * 3,
        scratch_shapes=[pltpu.VMEM((z.o_st, LANES), F32), pltpu.VMEM((NK, LANES), F32)],
        compiler_params=LIMIT,
        name="columns",
    )(m_a, g, st, side, move(side, along_y(0)))
    part, corner, stat = pl.pallas_call(
        functools.partial(beyond_kernel, z),
        out_shape=(shape(8, LANES), shape(NK, LANES), shape(levels + 1, 8, LANES)),
        in_specs=[VMEM] * 5,
        out_specs=(VMEM,) * 3,
        compiler_params=LIMIT,
        name="beyond",
    )(m_b, g, st, sums, corner)
    part, block = pl.pallas_call(
        functools.partial(corner_kernel, z),
        out_shape=(shape(8, LANES), shape(levels + 1, 8, LANES)),
        in_specs=[VMEM] * 4,
        out_specs=(VMEM, VMEM),
        compiler_params=LIMIT,
        name="corner",
    )(part, corner, far_b, st)
    part = part + lax.ppermute(part, "swath", [(i, i ^ 1) for i in range(nsw)])
    turns = [
        lax.ppermute(part, "swath", [(i, i ^ (2 * k) ^ 1) for i in range(nsw)])
        for k in (1, 3, 2)
    ]
    for turn in turns:
        part = part + turn
    both = jnp.concatenate([part, move(part, along_z)], axis=0)
    b0 = move(both, along_x(0, 1))
    b1 = move(both, along_x(1, 1))
    product, dep = pl.pallas_call(
        functools.partial(product_kernel, z),
        out_shape=(shape(*cells, dtype=BF), shape(1, pixels)),
        in_specs=[VMEM] * 7,
        out_specs=(VMEM, VMEM),
        scratch_shapes=[
            pltpu.VMEM((3 * NK, z.rows * LANES), BF),
            pltpu.VMEM(cells, F32),
        ],
        compiler_params=LIMIT,
        name="product",
    )(both, b0, b1, ext, stat, block, d)
    return product.reshape(direction.shape), dep.reshape(-1)


def solution(mesh):
    placed = (
        P(None, None, ("gy", "swath"), "gx"),
        P(None, ("gy", "swath"), "gx"),
        P(None, ("gy", "swath"), "gx"),
        P(None, ("gy", "swath"), "gx"),
        P(("gy", "swath"), "gx"),
        P(),
        P(("gy", "swath"), "gx"),
        P(("gy", "swath"), "gx"),
        P(("gx", "gy", "swath"), None),
        P(("gx", "gy", "swath")),
    )
    sizes = tuple(mesh.shape[a] for a in ALL)
    return jax.shard_map(
        functools.partial(per_device, sizes),
        mesh=mesh,
        in_specs=placed,
        out_specs=(P(None, None, ("gy", "swath"), "gx"), P(("gx", "gy", "swath"))),
        check_vma=False,
    )
```

```python
import functools

import jax
import jax.numpy as jnp
from jax import lax
from jax.experimental import pallas as pl
from jax.experimental.pallas import tpu as pltpu
from jax.sharding import PartitionSpec as P

KD = 0.2
UNROLL = 10
TURNS = (1, 3, 2)
ALL = ("gx", "gy", "swath")
LANES = 128
NM = 4
NK = NM * NM
BF = jnp.bfloat16
F32 = jnp.float32
VMEM = pl.BlockSpec(memory_space=pltpu.VMEM)
ANY = pl.BlockSpec(memory_space=pl.ANY)
HBM = pl.BlockSpec(memory_space=pltpu.HBM)


def iota(shape, dim):
    return lax.broadcasted_iota(jnp.int32, shape, dim)


def lane_roll(v, shift):
    return pltpu.roll(v, shift % v.shape[-1], v.ndim - 1)


def split(v):
    high = v.astype(BF)
    return high, (v - high.astype(F32)).astype(BF)


class Sizes:
    def __init__(self, sizes, species, levels):
        self.ngx, self.ngy, self.nsw = sizes
        self.nt = self.ngy * self.nsw
        self.species = species
        self.levels = levels
        self.rows = 2 * levels
        self.base = 8 * levels
        self.st = self.base + 8
        self.st16 = -(-(self.st + 1) // 16) * 16
        self.o_st = self.rows * NK
        self.msg = self.o_st + 2 * self.st16
        self.edge = NK + 8
        self.far = NK + 2 * 16

    def place(self):
        gx = lax.axis_index("gx")
        swath = lax.axis_index("swath")
        return gx, swath, lax.axis_index("gy") * self.nsw + swath


def project_kernel(
    z, dir_hbm, prop_hbm, cx_hbm, cy_hbm, kern_hbm, mech_hbm, pix_hbm, wgt_hbm, own_hbm, prec_hbm,
    g_ref, msg_ref, edge_ref, st_ref, d_ref,
    dir_ref, prop_ref, cx_ref, cy_ref, kern_ref, mech_ref, pix_ref, wgt_ref, own_ref, prec_ref,
    wide, sems,
):
    sources = (
        prop_hbm, dir_hbm, cx_hbm, cy_hbm, kern_hbm, mech_hbm, pix_hbm, wgt_hbm, own_hbm, prec_hbm
    )
    targets = (
        prop_ref, dir_ref, cx_ref, cy_ref, kern_ref, mech_ref, pix_ref, wgt_ref, own_ref, prec_ref
    )
    copies = [
        pltpu.make_async_copy(a, b, sems.at[i]) for i, (a, b) in enumerate(zip(sources, targets))
    ]
    for copy in copies:
        copy.start()
    species = z.species
    copies[0].wait()
    k_of = iota((NK, species), 0)
    heads = jnp.zeros((NK, species), F32)
    for m in range(NM):
        row = prop_ref[m][0:1, :].astype(F32)
        heads = heads + jnp.where(k_of % NM == m, row, 0.0)
    total = heads + jnp.where(iota((NK, species), 1) == 0, 1.0, 0.0)
    lhs = heads.astype(BF)
    for m in range(NM):
        matrix = prop_ref[m]
        term = jnp.dot(lhs, matrix, preferred_element_type=F32)
        total = total + jnp.where(k_of // NM == m, term + matrix[0:1, :].astype(F32), 0.0)
    high, low = split(total)
    both = jnp.concatenate([high, low], axis=0)
    d_ref[...] = jnp.concatenate([high, high, low], axis=0)
    copies[1].wait()
    wide[...] = dir_ref[...].astype(F32)
    cells = jnp.concatenate(
        [wide[pl.ds(r, species, stride=z.rows), :].astype(BF) for r in range(z.rows)], axis=1
    )
    g32 = jnp.dot(both, cells, preferred_element_type=F32)
    g = g32[:NK] + g32[NK:]
    lane = iota((NK, LANES), 1)
    edge = jnp.zeros((NK, LANES), F32)
    for r in range(z.rows):
        part = g[:, r * LANES : (r + 1) * LANES]
        g_ref[r * NK : (r + 1) * NK, :] = part
        msg_ref[r * NK : (r + 1) * NK, :] = part.astype(BF)
        edge = jnp.where(lane // 4 == r, lane_roll(part, 4 * r + 2), edge)
    edge_ref[0:NK, :] = edge
    for copy in copies[2:]:
        copy.wait()
    lane = iota((8, LANES), 1)
    side = jnp.zeros((8, LANES), F32)
    blank = jnp.zeros((2, LANES), F32)
    own = jnp.where(iota((2, LANES), 0) == 0, own_ref[:, 0:1], own_ref[:, 1:2])
    for l in range(z.levels + 1):
        if l < z.levels:
            parts = [cx_ref[l], cy_ref[l], kern_ref[l], blank]
        else:
            parts = [
                (mech_ref[...] + 1).astype(F32),
                pix_ref[...].astype(F32),
                wgt_ref[...],
                own.astype(F32),
            ]
        block = jnp.concatenate(parts, axis=0)
        st_ref[8 * l : 8 * l + 8, :] = block
        side = jnp.where(lane // 4 == l, lane_roll(block, 4 * l + 2), side)
    pixels = prec_ref.shape[1]
    last = jnp.concatenate([jnp.zeros((1, LANES - pixels), F32), prec_ref[...]], axis=1)
    st_ref[z.st :, :] = jnp.broadcast_to(last, (z.st16 - z.st, LANES))
    edge_ref[NK:, :] = side
    high, low = split(st_ref[...])
    msg_ref[z.o_st : z.o_st + z.st16, :] = high
    msg_ref[z.o_st + z.st16 : z.o_st + 2 * z.st16, :] = low


def sides_of(z, gx, x0, x1):
    even = gx % 2 == 0
    right = jnp.where(even, x0, x1)
    left = jnp.where(even, x1, x0)
    return jnp.where(gx > 0, left, 0.0), jnp.where(gx < z.ngx - 1, right, 0.0)


def edges_kernel(z, x1_ref, x0_ref, side_ref, far_ref):
    gx, _, _ = z.place()
    left, right = sides_of(z, gx, x0_ref[...], x1_ref[...])
    side = jnp.where(iota(left.shape, 1) % 4 < 2, left, right)
    side_ref[...] = side
    far_ref[0:NK, :] = side[0:NK].astype(BF)
    high, low = split(jnp.concatenate([side[NK:], jnp.zeros((8, LANES), F32)], axis=0))
    far_ref[NK : NK + 16, :] = high
    far_ref[NK + 16 :, :] = low


def spread(z, side, l):
    return lane_roll(side, LANES - (4 * l + 2))


def edge_lanes(z, l, left, right, old):
    lane = iota((NK, LANES), 1)
    left = pltpu.roll(left, 8 * l + 1, 1)
    right = pltpu.roll(right, 8 * l + 3, 1)
    return jnp.where(lane == 8 * l + 1, left, jnp.where(lane == 8 * l + 2, right, old))


def fold(v):
    half = v[0:8] + v[8:16]
    return half + pltpu.roll(half, 4, 0)


def row_of(stats, odd, first):
    return jnp.where(odd, stats[first ^ 1 : (first ^ 1) + 1], stats[first : first + 1])


def columns_kernel(z, a_ref, g_ref, st_ref, side_ref, far_ref, sums_ref, ext_ref, corner_ref, ga, ha):
    _, _, t = z.place()
    odd = t % 2 == 1
    even = jnp.where(odd, 0, 1)
    sg = jnp.where(odd, -0.5, 0.5)
    W = 2 * LANES
    ga[...] = a_ref[0 : z.o_st, :].astype(F32)
    ha[...] = far_ref[0:NK, :]
    stat_a = a_ref[z.o_st : z.o_st + z.st16, :].astype(F32) + a_ref[
        z.o_st + z.st16 : z.msg, :
    ].astype(F32)
    for l in range(z.levels + 1):
        ext_ref[0, l, :, 0:LANES] = st_ref[8 * l : 8 * l + 8, :]
        ext_ref[0, l, :, LANES:] = spread(z, side_ref[NK:, :], l)
        ext_ref[1, l, :, 0:LANES] = stat_a[8 * l : 8 * l + 8]
        ext_ref[1, l, :, LANES:] = spread(z, far_ref[NK:, :], l)
    k_of = iota((NK, W), 0)
    misc = ext_ref[0, z.levels]
    misc_a = ext_ref[1, z.levels]

    def sort(mech):
        return mech == (k_of // NM + 1).astype(F32)

    mech_0 = row_of(misc, odd, 0)
    mask_0, mask_1, mask_a = sort(mech_0), sort(row_of(misc, odd, 1)), sort(row_of(misc_a, odd, 0))
    head_0 = mech_0 == (k_of % NM + 1).astype(F32)
    weight_0 = row_of(misc, odd, 4)

    def level(l, carry):
        def field(ref, side, y):
            r = 2 * l + y
            own = ref[pl.ds(pl.multiple_of(r * NK, NK), NK), :]
            return jnp.concatenate([own, pltpu.roll(side, LANES - 2 - 4 * r, 1)], axis=1)

        side = side_ref[0:NK, :]
        q0, q1 = field(g_ref, side, 1 - even), field(g_ref, side, even)
        a1, a2 = field(ga, ha[...], 1 - even), field(ga, ha[...], even)
        own, other = ext_ref[0, l], ext_ref[1, l]
        cx_0, cx_1, cx_a = (
            0.5 * row_of(own, odd, 0), 0.5 * row_of(own, odd, 1), 0.5 * row_of(other, odd, 0)
        )
        cy_0, cy_1, cy_a = (
            sg * row_of(own, odd, 2), sg * row_of(own, odd, 3), sg * row_of(other, odd, 2)
        )

        def along(mid, cx):
            return (
                (1.0 - 4.0 * KD) * mid
                + (KD - cx) * pltpu.roll(mid, W - 1, 1)
                + (KD + cx) * pltpu.roll(mid, 1, 1)
            )

        f0 = along(q0, cx_0) + (KD - cy_0) * q1
        f1 = along(q1, cx_1) + (KD - cy_1) * a1 + (KD + cy_1) * q0
        fa = along(a1, cx_a) + (KD - cy_a) * a2 + (KD + cy_a) * q1
        f0, f1, fa = (
            fold(jnp.where(m, f, 0.0)) for m, f in ((mask_0, f0), (mask_1, f1), (mask_a, fa))
        )
        h0 = along(f0, cx_0) + (KD - cy_0) * f1
        h1 = along(f1, cx_1) + (KD - cy_1) * fa + (KD + cy_1) * f0
        kern_0, kern_1 = row_of(own, odd, 4), row_of(own, odd, 5)
        s0 = carry[0] + (kern_0 * h0)[:, 0:LANES]
        s1 = carry[1] + (kern_1 * h1)[:, 0:LANES]
        step = jnp.where(mask_0, KD + cy_0, 0.0)
        scale = jnp.where(head_0, kern_0 * weight_0, 0.0)
        left = (scale * pltpu.roll(step, 1, 1) * (KD + cx_0))[:, 0:LANES]
        right = (scale * pltpu.roll(step, W - 1, 1) * (KD - cx_0))[:, 0:LANES]
        return s0, s1, edge_lanes(z, l, left, right, carry[2])

    none = jnp.zeros((8, LANES), F32)
    s0, s1, corner = lax.fori_loop(
        0, z.levels, level, (none, none, jnp.zeros((NK, LANES), F32)), unroll=UNROLL
    )
    sums_ref[0:8, :] = s0
    sums_ref[8:16, :] = s1
    corner_ref[...] = corner


def beyond_kernel(z, b_ref, g_ref, st_ref, sums_ref, old_ref, part_ref, corner_ref, stat_ref):
    _, swath, t = z.place()
    odd = t % 2 == 1
    even = jnp.where(odd, 0, 1)
    has_b = jnp.logical_and(t > 0, t < z.nt - 1)
    sg = jnp.where(odd, -0.5, 0.5)
    for l in range(z.levels + 1):
        high = z.o_st + 8 * l
        both = b_ref[high : high + 8, :].astype(F32) + b_ref[
            high + z.st16 : high + z.st16 + 8, :
        ].astype(F32)
        stat_ref[l] = jnp.where(has_b, both, 0.0)
    k_of = iota((NK, LANES), 0)
    lane = iota((NK, LANES), 1)
    lane8 = iota((8, LANES), 1)
    sub8 = iota((8, LANES), 0)
    misc = st_ref[z.base : z.base + 8, :]
    mech_0 = row_of(misc, odd, 0)
    mech_b = row_of(stat_ref[z.levels], odd, 1)
    mask_0 = (mech_0 == (k_of // NM + 1).astype(F32)) & has_b
    mask_b = mech_b == (k_of // NM + 1).astype(F32)
    head_0 = mech_0 == (k_of % NM + 1).astype(F32)
    weight_0 = row_of(misc, odd, 4)

    def level(l, carry):
        def field(ref, y):
            at = pl.ds(pl.multiple_of((2 * l + y) * NK, NK), NK)
            return ref[at, :].astype(F32)

        q0 = field(g_ref, 1 - even)
        b1, b2 = field(b_ref, even), field(b_ref, 1 - even)
        own = st_ref[pl.ds(pl.multiple_of(8 * l, 8), 8), :]
        other = stat_ref[l]
        cx_0, cx_b = 0.5 * row_of(own, odd, 0), 0.5 * row_of(other, odd, 1)
        cy_0, cy_1, cy_b = (
            sg * row_of(own, odd, 2), sg * row_of(own, odd, 3), sg * row_of(other, odd, 3)
        )

        def along(mid, cx, lane):
            east = jnp.where(lane < LANES - 1, pltpu.roll(mid, LANES - 1, 1), 0.0)
            west = jnp.where(lane > 0, pltpu.roll(mid, 1, 1), 0.0)
            return (1.0 - 4.0 * KD) * mid + (KD - cx) * east + (KD + cx) * west

        fb = along(b1, cx_b, lane) + (KD - cy_b) * q0 + (KD + cy_b) * b2
        fb = fold(jnp.where(mask_b, fb, 0.0))
        f0 = fold(jnp.where(mask_0, (KD + cy_0) * b1, 0.0))
        kern_0, kern_1 = row_of(own, odd, 4), row_of(own, odd, 5)
        s0 = carry[0] + kern_0 * (along(f0, cx_0, lane8) + (KD + cy_0) * fb)
        s1 = carry[1] + kern_1 * (KD + cy_1) * f0
        step = jnp.where(head_0 & mask_b, kern_0 * weight_0 * (KD + cy_0), 0.0)
        left, right = step * (KD + cx_b), step * (KD - cx_b)
        corner = edge_lanes(z, l, left, right, carry[2])
        return s0, s1, corner

    s0, s1, corner = lax.fori_loop(
        0,
        z.levels,
        level,
        (sums_ref[0:8, :], sums_ref[8:16, :], jnp.zeros((NK, LANES), F32)),
        unroll=UNROLL,
    )
    corner_ref[...] = corner + old_ref[...]
    pixels = LANES // 2
    sub = iota((pixels, LANES), 0)
    total = jnp.zeros((8, LANES), F32)
    for y, sums in ((0, s0), (1, s1)):
        final = row_of(misc, odd, y) == (sub8 + 1).astype(F32)
        column = jnp.sum(jnp.where(final, sums, 0.0), axis=0, keepdims=True)
        column = column * row_of(misc, odd, 4 + y)
        hit = jnp.where(row_of(misc, odd, 2 + y) == sub.astype(F32), column, 0.0)
        tall = jnp.sum(hit, axis=1, keepdims=True)
        row = jnp.sum(
            jnp.where(sub == iota((pixels, LANES), 1), tall, 0.0), axis=0, keepdims=True
        )
        total = total + jnp.where(row_of(misc, odd, 6 + y) == sub8.astype(F32), row, 0.0)
    part_ref[...] = jnp.where(
        lane8 < pixels, total, jnp.where(sub8 == swath, st_ref[z.st : z.st + 1, :], 0.0)
    )


def corner_kernel(z, part_ref, corner_ref, far_ref, st_ref, out_ref, block_ref):
    _, _, t = z.place()
    odd = t % 2 == 1
    has_b = jnp.logical_and(t > 0, t < z.nt - 1)
    far = jnp.where(has_b, far_ref[...].astype(F32), 0.0)
    side = (far[NK : NK + 16] + far[NK + 16 :])[0:8]
    for l in range(z.levels + 1):
        block_ref[l] = spread(z, side, l)
    g = far[0:NK]
    g = jnp.where(odd, g, pltpu.roll(g, LANES - 4, 1))
    share = jnp.sum(corner_ref[...] * g, axis=0, keepdims=True)
    lane = iota((1, LANES), 1)
    sub8 = iota((8, LANES), 0)
    lane8 = iota((8, LANES), 1)
    misc = st_ref[z.base : z.base + 8, :]
    pixel = row_of(misc, odd, 2)
    owner = row_of(misc, odd, 6)
    total = part_ref[...]
    for c, column in ((1, 0), (2, LANES - 1)):
        value = jnp.sum(jnp.where(lane % 8 == c, share, 0.0), axis=1, keepdims=True)
        at = slice(column, column + 1)
        hit = (lane8.astype(F32) == pixel[:, at]) & (sub8.astype(F32) == owner[:, at])
        total = total + jnp.where(hit, value, 0.0)
    out_ref[...] = total


def product_kernel(
    z, own_ref, x1_ref, x0_ref, oa_ref, stat_ref, block_ref, d_ref, out_ref, dep_ref, v3, tall
):
    gx, swath, t = z.place()
    odd = t % 2 == 1

    def tiles(l):
        a = oa_ref[1, l]
        b = jnp.concatenate([stat_ref[l], block_ref[l]], axis=1)
        return jnp.where(odd, a, b), oa_ref[0, l], jnp.where(odd, b, a)

    miscs = tiles(z.levels)
    W = 2 * LANES
    pixels = LANES // 2
    left, right = sides_of(z, gx, x0_ref[...], x1_ref[...])

    def weigh(v):
        return v * lane_roll(v, pixels)

    deps = [weigh(v) for v in (own_ref[...], left, right)]
    sub = iota((8, LANES), 0)
    dep_ref[...] = jnp.sum(jnp.where(sub == swath, deps[0][0:8], 0.0), axis=0, keepdims=True)[
        :, 0:pixels
    ]
    outer = ((sub < 2) & (swath == 0)) | ((sub >= 4) & (swath == z.nsw - 1))

    def stack(f):
        out = jnp.zeros((8, W), F32)
        for s in range(3):
            for y in range(2):
                row = miscs[s][2 * f + y : 2 * f + y + 1]
                out = jnp.where(iota((8, W), 0) == 2 * s + y, row, out)
        return out

    owner = stack(3)
    index = stack(1).astype(jnp.int32)
    weight = stack(2)

    def find(dep, owner, index):
        found = jnp.zeros((8, LANES), F32)
        for o in range(z.nsw):
            row = jnp.where(outer, dep[8 + o : 9 + o, :], dep[o : o + 1, :])
            value = jnp.take_along_axis(row, index, axis=1)
            found = jnp.where(owner == float(o), value, found)
        return found

    lane = iota((8, LANES), 1)
    far = (owner[:, LANES:], index[:, LANES:])
    beside = jnp.where(
        lane < 2, find(deps[2], *far), jnp.where(lane >= LANES - 2, find(deps[1], *far), 0.0)
    )
    near = find(deps[0], owner[:, 0:LANES], index[:, 0:LANES])
    back = weight * jnp.concatenate([near, beside], axis=1)
    place = [(s, y) for s in range(3) for y in range(2)]
    k_of = iota((NK, W), 0) // NM
    m_of = iota((8, W), 0) % NM
    drive = []
    for i, (s, y) in enumerate(place):
        mech = miscs[s][y : y + 1]
        drive.append(jnp.where(mech == (m_of + 1).astype(F32), back[i : i + 1, :], 0.0))
    masks = [
        miscs[s][y : y + 1] == (k_of + 1).astype(F32) for s, y in place[1:5]
    ]

    def unadvect(mid, cx, up, cy_up, down, cy_down):
        return (
            (1.0 - 4.0 * KD) * mid
            + pltpu.roll((KD - cx) * mid, 1, 1)
            + pltpu.roll((KD + cx) * mid, W - 1, 1)
            + (KD - cy_up) * up
            + (KD + cy_down) * down
        )

    def level(l, carry):
        stats = tiles(l)
        cx = [0.5 * stats[s][y : y + 1] for s, y in place]
        cy = [0.5 * stats[s][2 + y : 3 + y] for s, y in place]
        kern = [stats[s][4 + y : 5 + y] for s, y in place]
        w = [kern[i] * drive[i] for i in range(6)]
        u = []
        for i in range(1, 5):
            mid = unadvect(w[i], cx[i], w[i - 1], cy[i - 1], w[i + 1], cy[i + 1])
            twice = jnp.concatenate([mid, mid], axis=0)
            u.append(jnp.where(masks[i - 1], twice, 0.0))
        for y in range(2):
            i = 2 + y
            v = unadvect(u[i - 1], cx[i], u[i - 2], cy[i - 1], u[i], cy[i + 1])[:, 0:LANES]
            high, low = split(v)
            at = pl.ds(pl.multiple_of((2 * l + y) * LANES, LANES), LANES)
            v3[0:NK, at] = high
            v3[NK : 2 * NK, at] = low
            v3[2 * NK :, at] = high
        return carry

    lax.fori_loop(0, z.levels, level, 0, unroll=UNROLL)
    d = d_ref[...]
    for r in range(0, z.rows, 2):
        both = lax.dot_general(
            d, v3[:, r * LANES : (r + 2) * LANES], (((0,), (0,)), ((), ())),
            preferred_element_type=F32,
        )
        tall[pl.ds(r, z.species, stride=z.rows), :] = both[:, 0:LANES]
        tall[pl.ds(r + 1, z.species, stride=z.rows), :] = both[:, LANES:]
    out_ref[...] = tall[...].astype(BF)


def shape(*dims, dtype=F32):
    return jax.ShapeDtypeStruct(dims, dtype)


LIMIT = pltpu.CompilerParams(vmem_limit_bytes=32 * 1024 * 1024)


def swaps_of(sizes):
    ngx, ngy, nsw = sizes
    nt = ngy * nsw

    def pairs(f):
        return [(g * nt + t, f(g, t)) for g in range(ngx) for t in range(nt)]

    def other(i, parity):
        return i + 1 if i % 2 == parity else i - 1

    def along_x(parity, flip):
        def to(g, t):
            n = other(g, parity)
            return n * nt + (t ^ flip) if 0 <= n < ngx else g * nt + (t ^ 1)

        return pairs(to)

    def along_y(parity):
        def to(g, t):
            n = other(t, parity)
            return g * nt + n if 0 <= n < nt else (g ^ 1) * nt + t

        return pairs(to)

    def along_z(g, t):
        gy, s = divmod(t, nsw)
        chip, core = divmod(s, 2)
        last = nsw // 2 - 1
        up = 1 if chip == 0 else -1
        if chip in (0, last) and 0 <= gy + up < ngy:
            gy, core = gy + up, 1 - core
        elif gy == ngy - 1 and chip < last:
            chip += 1
        elif gy == 0 and chip > 0:
            chip -= 1
        else:
            core = 1 - core
        return g * nt + gy * nsw + 2 * chip + core

    return along_x, along_y, pairs(along_z)


def per_device(
    sizes,
    direction,
    courant_x,
    courant_y,
    kernel,
    mechanism,
    propagator,
    footprint_pixel,
    footprint_weight,
    footprint_owner,
    precision,
):
    species, levels = direction.shape[:2]
    z = Sizes(sizes, species, levels)
    along_x, along_y, along_z = swaps_of(sizes)
    nsw = z.nsw

    def move(v, perm):
        return lax.ppermute(v, ALL, perm)

    cells = (species * z.rows, LANES)
    pixels = precision.shape[0]
    g, msg, edge, st, d = pl.pallas_call(
        functools.partial(project_kernel, z),
        out_shape=(
            shape(z.o_st, LANES),
            shape(z.msg, LANES, dtype=BF),
            shape(z.edge, LANES),
            shape(z.st16, LANES),
            shape(3 * NK, species, dtype=BF),
        ),
        in_specs=[HBM] * 10,
        out_specs=(VMEM,) * 5,
        scratch_shapes=[
            pltpu.VMEM(cells, BF),
            pltpu.VMEM(propagator.shape, BF),
            pltpu.VMEM(courant_x.shape, F32),
            pltpu.VMEM(courant_x.shape, F32),
            pltpu.VMEM(courant_x.shape, F32),
            pltpu.VMEM(mechanism.shape, jnp.int32),
            pltpu.VMEM(mechanism.shape, jnp.int32),
            pltpu.VMEM(mechanism.shape, F32),
            pltpu.VMEM((1, 2), jnp.int32),
            pltpu.VMEM((1, pixels), F32),
            pltpu.VMEM(cells, F32),
            pltpu.SemaphoreType.DMA((10,)),
        ],
        compiler_params=LIMIT,
        name="project",
    )(
        *(
            pltpu.with_memory_space_constraint(v, pltpu.HBM)
            for v in (
                direction.reshape(cells), propagator, courant_x, courant_y, kernel, mechanism,
                footprint_pixel, footprint_weight, footprint_owner.reshape(1, 2),
                precision.reshape(1, -1),
            )
        )
    )
    e0 = move(edge, along_x(0, 0))
    e1 = move(edge, along_x(1, 0))
    m_b = move(msg, along_y(1))
    m_a = move(msg, along_y(0))
    side, far = pl.pallas_call(
        functools.partial(edges_kernel, z),
        out_shape=(shape(z.edge, LANES), shape(z.far, LANES, dtype=BF)),
        in_specs=[VMEM, VMEM],
        out_specs=(VMEM, VMEM),
        compiler_params=LIMIT,
        cost_estimate=pl.CostEstimate(
            flops=20_000_000_000, bytes_accessed=1024, transcendentals=0
        ),
        name="edges",
    )(e1, e0)
    far_b = move(far, along_y(1))
    sums, ext, corner = pl.pallas_call(
        functools.partial(columns_kernel, z),
        out_shape=(
            shape(16, LANES), shape(2, levels + 1, 8, 2 * LANES), shape(NK, LANES)
        ),
        in_specs=[VMEM] * 5,
        out_specs=(VMEM,) * 3,
        scratch_shapes=[pltpu.VMEM((z.o_st, LANES), F32), pltpu.VMEM((NK, LANES), F32)],
        compiler_params=LIMIT,
        name="columns",
    )(m_a, g, st, side, move(side, along_y(0)))
    part, corner, stat = pl.pallas_call(
        functools.partial(beyond_kernel, z),
        out_shape=(shape(8, LANES), shape(NK, LANES), shape(levels + 1, 8, LANES)),
        in_specs=[VMEM] * 5,
        out_specs=(VMEM,) * 3,
        compiler_params=LIMIT,
        name="beyond",
    )(m_b, g, st, sums, corner)
    part, block = pl.pallas_call(
        functools.partial(corner_kernel, z),
        out_shape=(shape(8, LANES), shape(levels + 1, 8, LANES)),
        in_specs=[VMEM] * 4,
        out_specs=(VMEM, VMEM),
        compiler_params=LIMIT,
        name="corner",
    )(part, corner, far_b, st)
    part = part + lax.ppermute(part, "swath", [(i, i ^ 1) for i in range(nsw)])
    turns = [
        lax.ppermute(part, "swath", [(i, i ^ (2 * k) ^ 1) for i in range(nsw)])
        for k in (1, 3, 2)
    ]
    for turn in turns:
        part = part + turn
    both = jnp.concatenate([part, move(part, along_z)], axis=0)
    b0 = move(both, along_x(0, 1))
    b1 = move(both, along_x(1, 1))
    product, dep = pl.pallas_call(
        functools.partial(product_kernel, z),
        out_shape=(shape(*cells, dtype=BF), shape(1, pixels)),
        in_specs=[VMEM] * 7,
        out_specs=(VMEM, VMEM),
        scratch_shapes=[
            pltpu.VMEM((3 * NK, z.rows * LANES), BF),
            pltpu.VMEM(cells, F32),
        ],
        compiler_params=LIMIT,
        name="product",
    )(both, b1, b0, ext, stat, block, d)
    return product.reshape(direction.shape), dep.reshape(-1)


def solution(mesh):
    placed = (
        P(None, None, ("gy", "swath"), "gx"),
        P(None, ("gy", "swath"), "gx"),
        P(None, ("gy", "swath"), "gx"),
        P(None, ("gy", "swath"), "gx"),
        P(("gy", "swath"), "gx"),
        P(),
        P(("gy", "swath"), "gx"),
        P(("gy", "swath"), "gx"),
        P(("gx", "gy", "swath"), None),
        P(("gx", "gy", "swath")),
    )
    sizes = tuple(mesh.shape[a] for a in ALL)
    return jax.shard_map(
        functools.partial(per_device, sizes),
        mesh=mesh,
        in_specs=placed,
        out_specs=(P(None, None, ("gy", "swath"), "gx"), P(("gx", "gy", "swath"))),
        check_vma=False,
    )
```

```python
import functools

import jax
import jax.numpy as jnp
from jax import lax
from jax.experimental import pallas as pl
from jax.experimental.pallas import tpu as pltpu
from jax.sharding import PartitionSpec as P

KD = 0.2
UNROLL = 10
ALL = ("gx", "gy", "swath")
LANES = 128
NM = 4
NK = NM * NM
BF = jnp.bfloat16
F32 = jnp.float32
VMEM = pl.BlockSpec(memory_space=pltpu.VMEM)
HBM = pl.BlockSpec(memory_space=pltpu.HBM)


def iota(shape, dim):
    return lax.broadcasted_iota(jnp.int32, shape, dim)


def lane_roll(v, shift):
    return pltpu.roll(v, shift % v.shape[-1], v.ndim - 1)


def split(v):
    high = v.astype(BF)
    return high, (v - high.astype(F32)).astype(BF)


class Sizes:
    def __init__(self, sizes, species, levels):
        self.ngx, self.ngy, self.nsw = sizes
        self.nt = self.ngy * self.nsw
        self.species = species
        self.levels = levels
        self.rows = 2 * levels
        self.base = 8 * levels
        self.st = self.base + 8
        self.st16 = -(-(self.st + 1) // 16) * 16
        self.o_st = self.rows * NK
        self.msg = self.o_st + 2 * self.st16
        self.edge = NK + 8
        self.far = NK + 2 * 16

    def place(self):
        gx = lax.axis_index("gx")
        swath = lax.axis_index("swath")
        return gx, swath, lax.axis_index("gy") * self.nsw + swath


def project_kernel(
    z, dir_hbm, prop_hbm, cx_hbm, cy_hbm, kern_hbm, mech_hbm, pix_hbm, wgt_hbm, own_hbm, prec_hbm,
    g_ref, msg_ref, edge_ref, st_ref, d_ref,
    dir_ref, prop_ref, cx_ref, cy_ref, kern_ref, mech_ref, pix_ref, wgt_ref, own_ref, prec_ref,
    wide, sems,
):
    sources = (
        prop_hbm, dir_hbm, cx_hbm, cy_hbm, kern_hbm, mech_hbm, pix_hbm, wgt_hbm, own_hbm, prec_hbm
    )
    targets = (
        prop_ref, dir_ref, cx_ref, cy_ref, kern_ref, mech_ref, pix_ref, wgt_ref, own_ref, prec_ref
    )
    copies = [
        pltpu.make_async_copy(a, b, sems.at[i]) for i, (a, b) in enumerate(zip(sources, targets))
    ]
    for copy in copies:
        copy.start()
    species = z.species
    copies[0].wait()
    k_of = iota((NK, species), 0)
    heads = jnp.zeros((NK, species), F32)
    for m in range(NM):
        row = prop_ref[m][0:1, :].astype(F32)
        heads = heads + jnp.where(k_of % NM == m, row, 0.0)
    total = heads + jnp.where(iota((NK, species), 1) == 0, 1.0, 0.0)
    lhs = heads.astype(BF)
    for m in range(NM):
        matrix = prop_ref[m]
        term = jnp.dot(lhs, matrix, preferred_element_type=F32)
        total = total + jnp.where(k_of // NM == m, term + matrix[0:1, :].astype(F32), 0.0)
    high, low = split(total)
    both = jnp.concatenate([high, low], axis=0)
    d_ref[...] = jnp.concatenate([high, high, low], axis=0)
    copies[1].wait()
    wide[...] = dir_ref[...].astype(F32)
    cells = jnp.concatenate(
        [wide[pl.ds(r, species, stride=z.rows), :].astype(BF) for r in range(z.rows)], axis=1
    )
    g32 = jnp.dot(both, cells, preferred_element_type=F32)
    g = g32[:NK] + g32[NK:]
    lane = iota((NK, LANES), 1)
    edge = jnp.zeros((NK, LANES), F32)
    for r in range(z.rows):
        part = g[:, r * LANES : (r + 1) * LANES]
        g_ref[r * NK : (r + 1) * NK, :] = part
        msg_ref[r * NK : (r + 1) * NK, :] = part.astype(BF)
        edge = jnp.where(lane // 4 == r, lane_roll(part, 4 * r + 2), edge)
    edge_ref[0:NK, :] = edge
    for copy in copies[2:]:
        copy.wait()
    lane = iota((8, LANES), 1)
    side = jnp.zeros((8, LANES), F32)
    blank = jnp.zeros((2, LANES), F32)
    own = jnp.where(iota((2, LANES), 0) == 0, own_ref[:, 0:1], own_ref[:, 1:2])
    for l in range(z.levels + 1):
        if l < z.levels:
            parts = [cx_ref[l], cy_ref[l], kern_ref[l], blank]
        else:
            parts = [
                (mech_ref[...] + 1).astype(F32),
                pix_ref[...].astype(F32),
                wgt_ref[...],
                own.astype(F32),
            ]
        block = jnp.concatenate(parts, axis=0)
        st_ref[8 * l : 8 * l + 8, :] = block
        side = jnp.where(lane // 4 == l, lane_roll(block, 4 * l + 2), side)
    pixels = prec_ref.shape[1]
    last = jnp.concatenate([jnp.zeros((1, LANES - pixels), F32), prec_ref[...]], axis=1)
    st_ref[z.st :, :] = jnp.broadcast_to(last, (z.st16 - z.st, LANES))
    edge_ref[NK:, :] = side
    high, low = split(st_ref[...])
    msg_ref[z.o_st : z.o_st + z.st16, :] = high
    msg_ref[z.o_st + z.st16 : z.o_st + 2 * z.st16, :] = low


def sides_of(z, gx, x0, x1):
    even = gx % 2 == 0
    right = jnp.where(even, x0, x1)
    left = jnp.where(even, x1, x0)
    return jnp.where(gx > 0, left, 0.0), jnp.where(gx < z.ngx - 1, right, 0.0)


def edges_kernel(z, x1_ref, x0_ref, side_ref, far_ref):
    gx, _, _ = z.place()
    left, right = sides_of(z, gx, x0_ref[...], x1_ref[...])
    side = jnp.where(iota(left.shape, 1) % 4 < 2, left, right)
    side_ref[...] = side
    far_ref[0:NK, :] = side[0:NK].astype(BF)
    high, low = split(jnp.concatenate([side[NK:], jnp.zeros((8, LANES), F32)], axis=0))
    far_ref[NK : NK + 16, :] = high
    far_ref[NK + 16 :, :] = low


def spread(z, side, l):
    return lane_roll(side, LANES - (4 * l + 2))


def edge_lanes(z, l, left, right, old):
    lane = iota((NK, LANES), 1)
    left = pltpu.roll(left, 8 * l + 1, 1)
    right = pltpu.roll(right, 8 * l + 3, 1)
    return jnp.where(lane == 8 * l + 1, left, jnp.where(lane == 8 * l + 2, right, old))


def fold(v):
    half = v[0:8] + v[8:16]
    return half + pltpu.roll(half, 4, 0)


def row_of(stats, odd, first):
    return jnp.where(odd, stats[first ^ 1 : (first ^ 1) + 1], stats[first : first + 1])


def columns_kernel(z, a_ref, g_ref, st_ref, side_ref, far_ref, sums_ref, ext_ref, corner_ref, ga, ha):
    _, _, t = z.place()
    odd = t % 2 == 1
    even = jnp.where(odd, 0, 1)
    sg = jnp.where(odd, -0.5, 0.5)
    W = 2 * LANES
    ga[...] = a_ref[0 : z.o_st, :].astype(F32)
    ha[...] = far_ref[0:NK, :]
    stat_a = a_ref[z.o_st : z.o_st + z.st16, :].astype(F32) + a_ref[
        z.o_st + z.st16 : z.msg, :
    ].astype(F32)
    for l in range(z.levels + 1):
        ext_ref[0, l, :, 0:LANES] = st_ref[8 * l : 8 * l + 8, :]
        ext_ref[0, l, :, LANES:] = spread(z, side_ref[NK:, :], l)
        ext_ref[1, l, :, 0:LANES] = stat_a[8 * l : 8 * l + 8]
        ext_ref[1, l, :, LANES:] = spread(z, far_ref[NK:, :], l)
    k_of = iota((NK, W), 0)
    misc = ext_ref[0, z.levels]
    misc_a = ext_ref[1, z.levels]

    def sort(mech):
        return mech == (k_of // NM + 1).astype(F32)

    mech_0 = row_of(misc, odd, 0)
    mask_0, mask_1, mask_a = sort(mech_0), sort(row_of(misc, odd, 1)), sort(row_of(misc_a, odd, 0))
    head_0 = mech_0 == (k_of % NM + 1).astype(F32)
    weight_0 = row_of(misc, odd, 4)

    def level(l, carry):
        def field(ref, side, y):
            r = 2 * l + y
            own = ref[pl.ds(pl.multiple_of(r * NK, NK), NK), :]
            return jnp.concatenate([own, pltpu.roll(side, LANES - 2 - 4 * r, 1)], axis=1)

        side = side_ref[0:NK, :]
        q0, q1 = field(g_ref, side, 1 - even), field(g_ref, side, even)
        a1, a2 = field(ga, ha[...], 1 - even), field(ga, ha[...], even)
        own, other = ext_ref[0, l], ext_ref[1, l]
        cx_0, cx_1, cx_a = (
            0.5 * row_of(own, odd, 0), 0.5 * row_of(own, odd, 1), 0.5 * row_of(other, odd, 0)
        )
        cy_0, cy_1, cy_a = (
            sg * row_of(own, odd, 2), sg * row_of(own, odd, 3), sg * row_of(other, odd, 2)
        )

        def along(mid, cx):
            return (
                (1.0 - 4.0 * KD) * mid
                + (KD - cx) * pltpu.roll(mid, W - 1, 1)
                + (KD + cx) * pltpu.roll(mid, 1, 1)
            )

        f0 = along(q0, cx_0) + (KD - cy_0) * q1
        f1 = along(q1, cx_1) + (KD - cy_1) * a1 + (KD + cy_1) * q0
        fa = along(a1, cx_a) + (KD - cy_a) * a2 + (KD + cy_a) * q1
        f0, f1, fa = (
            fold(jnp.where(m, f, 0.0)) for m, f in ((mask_0, f0), (mask_1, f1), (mask_a, fa))
        )
        h0 = along(f0, cx_0) + (KD - cy_0) * f1
        h1 = along(f1, cx_1) + (KD - cy_1) * fa + (KD + cy_1) * f0
        kern_0, kern_1 = row_of(own, odd, 4), row_of(own, odd, 5)
        s0 = carry[0] + (kern_0 * h0)[:, 0:LANES]
        s1 = carry[1] + (kern_1 * h1)[:, 0:LANES]
        step = jnp.where(mask_0, KD + cy_0, 0.0)
        scale = jnp.where(head_0, kern_0 * weight_0, 0.0)
        left = (scale * pltpu.roll(step, 1, 1) * (KD + cx_0))[:, 0:LANES]
        right = (scale * pltpu.roll(step, W - 1, 1) * (KD - cx_0))[:, 0:LANES]
        return s0, s1, edge_lanes(z, l, left, right, carry[2])

    none = jnp.zeros((8, LANES), F32)
    s0, s1, corner = lax.fori_loop(
        0, z.levels, level, (none, none, jnp.zeros((NK, LANES), F32)), unroll=UNROLL
    )
    sums_ref[0:8, :] = s0
    sums_ref[8:16, :] = s1
    corner_ref[...] = corner


def beyond_kernel(z, b_ref, g_ref, st_ref, sums_ref, old_ref, part_ref, corner_ref, stat_ref):
    _, swath, t = z.place()
    odd = t % 2 == 1
    even = jnp.where(odd, 0, 1)
    has_b = jnp.logical_and(t > 0, t < z.nt - 1)
    sg = jnp.where(odd, -0.5, 0.5)
    stat_b = b_ref[z.o_st : z.o_st + z.st16, :].astype(F32) + b_ref[
        z.o_st + z.st16 : z.msg, :
    ].astype(F32)
    stat_b = jnp.where(has_b, stat_b, 0.0)
    for l in range(z.levels + 1):
        stat_ref[l] = stat_b[8 * l : 8 * l + 8]
    k_of = iota((NK, LANES), 0)
    lane = iota((NK, LANES), 1)
    lane8 = iota((8, LANES), 1)
    sub8 = iota((8, LANES), 0)
    misc = st_ref[z.base : z.base + 8, :]
    mech_0 = row_of(misc, odd, 0)
    mech_b = row_of(stat_ref[z.levels], odd, 1)
    mask_0 = (mech_0 == (k_of // NM + 1).astype(F32)) & has_b
    mask_b = mech_b == (k_of // NM + 1).astype(F32)
    head_0 = mech_0 == (k_of % NM + 1).astype(F32)
    weight_0 = row_of(misc, odd, 4)

    def level(l, carry):
        def field(ref, y):
            at = pl.ds(pl.multiple_of((2 * l + y) * NK, NK), NK)
            return ref[at, :].astype(F32)

        q0 = field(g_ref, 1 - even)
        b1, b2 = field(b_ref, even), field(b_ref, 1 - even)
        own = st_ref[pl.ds(pl.multiple_of(8 * l, 8), 8), :]
        other = stat_ref[l]
        cx_0, cx_b = 0.5 * row_of(own, odd, 0), 0.5 * row_of(other, odd, 1)
        cy_0, cy_1, cy_b = (
            sg * row_of(own, odd, 2), sg * row_of(own, odd, 3), sg * row_of(other, odd, 3)
        )

        def along(mid, cx, lane):
            east = jnp.where(lane < LANES - 1, pltpu.roll(mid, LANES - 1, 1), 0.0)
            west = jnp.where(lane > 0, pltpu.roll(mid, 1, 1), 0.0)
            return (1.0 - 4.0 * KD) * mid + (KD - cx) * east + (KD + cx) * west

        fb = along(b1, cx_b, lane) + (KD - cy_b) * q0 + (KD + cy_b) * b2
        fb = fold(jnp.where(mask_b, fb, 0.0))
        f0 = fold(jnp.where(mask_0, (KD + cy_0) * b1, 0.0))
        kern_0, kern_1 = row_of(own, odd, 4), row_of(own, odd, 5)
        s0 = carry[0] + kern_0 * (along(f0, cx_0, lane8) + (KD + cy_0) * fb)
        s1 = carry[1] + kern_1 * (KD + cy_1) * f0
        step = jnp.where(head_0 & mask_b, kern_0 * weight_0 * (KD + cy_0), 0.0)
        left, right = step * (KD + cx_b), step * (KD - cx_b)
        corner = edge_lanes(z, l, left, right, carry[2])
        return s0, s1, corner

    s0, s1, corner = lax.fori_loop(
        0,
        z.levels,
        level,
        (sums_ref[0:8, :], sums_ref[8:16, :], jnp.zeros((NK, LANES), F32)),
        unroll=UNROLL,
    )
    corner_ref[...] = corner + old_ref[...]
    pixels = LANES // 2
    sub = iota((pixels, LANES), 0)
    total = jnp.zeros((8, LANES), F32)
    for y, sums in ((0, s0), (1, s1)):
        final = row_of(misc, odd, y) == (sub8 + 1).astype(F32)
        column = jnp.sum(jnp.where(final, sums, 0.0), axis=0, keepdims=True)
        column = column * row_of(misc, odd, 4 + y)
        hit = jnp.where(row_of(misc, odd, 2 + y) == sub.astype(F32), column, 0.0)
        tall = jnp.sum(hit, axis=1, keepdims=True)
        row = jnp.sum(
            jnp.where(sub == iota((pixels, LANES), 1), tall, 0.0), axis=0, keepdims=True
        )
        total = total + jnp.where(row_of(misc, odd, 6 + y) == sub8.astype(F32), row, 0.0)
    part_ref[...] = jnp.where(
        lane8 < pixels, total, jnp.where(sub8 == swath, st_ref[z.st : z.st + 1, :], 0.0)
    )


def corner_kernel(z, part_ref, corner_ref, far_ref, st_ref, out_ref, block_ref):
    _, _, t = z.place()
    odd = t % 2 == 1
    has_b = jnp.logical_and(t > 0, t < z.nt - 1)
    far = jnp.where(has_b, far_ref[...].astype(F32), 0.0)
    side = (far[NK : NK + 16] + far[NK + 16 :])[0:8]
    for l in range(z.levels + 1):
        block_ref[l] = spread(z, side, l)
    g = far[0:NK]
    g = jnp.where(odd, g, pltpu.roll(g, LANES - 4, 1))
    share = jnp.sum(corner_ref[...] * g, axis=0, keepdims=True)
    lane = iota((1, LANES), 1)
    sub8 = iota((8, LANES), 0)
    lane8 = iota((8, LANES), 1)
    misc = st_ref[z.base : z.base + 8, :]
    pixel = row_of(misc, odd, 2)
    owner = row_of(misc, odd, 6)
    total = part_ref[...]
    for c, column in ((1, 0), (2, LANES - 1)):
        value = jnp.sum(jnp.where(lane % 8 == c, share, 0.0), axis=1, keepdims=True)
        at = slice(column, column + 1)
        hit = (lane8.astype(F32) == pixel[:, at]) & (sub8.astype(F32) == owner[:, at])
        total = total + jnp.where(hit, value, 0.0)
    out_ref[...] = total


def product_kernel(
    z, own_ref, x1_ref, x0_ref, oa_ref, stat_ref, block_ref, d_ref, out_ref, dep_ref, v3, tall
):
    gx, swath, t = z.place()
    odd = t % 2 == 1

    def tiles(l):
        a = oa_ref[1, l]
        b = jnp.concatenate([stat_ref[l], block_ref[l]], axis=1)
        return jnp.where(odd, a, b), oa_ref[0, l], jnp.where(odd, b, a)

    miscs = tiles(z.levels)
    W = 2 * LANES
    pixels = LANES // 2
    left, right = sides_of(z, gx, x0_ref[...], x1_ref[...])

    def weigh(v):
        return v * lane_roll(v, pixels)

    deps = [weigh(v) for v in (own_ref[...], left, right)]
    sub = iota((8, LANES), 0)
    dep_ref[...] = jnp.sum(jnp.where(sub == swath, deps[0][0:8], 0.0), axis=0, keepdims=True)[
        :, 0:pixels
    ]
    outer = ((sub < 2) & (swath == 0)) | ((sub >= 4) & (swath == z.nsw - 1))

    def stack(f):
        out = jnp.zeros((8, W), F32)
        for s in range(3):
            for y in range(2):
                row = miscs[s][2 * f + y : 2 * f + y + 1]
                out = jnp.where(iota((8, W), 0) == 2 * s + y, row, out)
        return out

    owner = stack(3)
    index = stack(1).astype(jnp.int32)
    weight = stack(2)

    def find(dep, owner, index):
        found = jnp.zeros((8, LANES), F32)
        for o in range(z.nsw):
            row = jnp.where(outer, dep[8 + o : 9 + o, :], dep[o : o + 1, :])
            value = jnp.take_along_axis(row, index, axis=1)
            found = jnp.where(owner == float(o), value, found)
        return found

    lane = iota((8, LANES), 1)
    far = (owner[:, LANES:], index[:, LANES:])
    beside = jnp.where(
        lane < 2, find(deps[2], *far), jnp.where(lane >= LANES - 2, find(deps[1], *far), 0.0)
    )
    near = find(deps[0], owner[:, 0:LANES], index[:, 0:LANES])
    back = weight * jnp.concatenate([near, beside], axis=1)
    place = [(s, y) for s in range(3) for y in range(2)]
    k_of = iota((NK, W), 0) // NM
    m_of = iota((8, W), 0) % NM
    drive = []
    for i, (s, y) in enumerate(place):
        mech = miscs[s][y : y + 1]
        drive.append(jnp.where(mech == (m_of + 1).astype(F32), back[i : i + 1, :], 0.0))
    masks = [
        miscs[s][y : y + 1] == (k_of + 1).astype(F32) for s, y in place[1:5]
    ]

    def unadvect(mid, cx, up, cy_up, down, cy_down):
        return (
            (1.0 - 4.0 * KD) * mid
            + pltpu.roll((KD - cx) * mid, 1, 1)
            + pltpu.roll((KD + cx) * mid, W - 1, 1)
            + (KD - cy_up) * up
            + (KD + cy_down) * down
        )

    def level(l, carry):
        stats = tiles(l)
        cx = [0.5 * stats[s][y : y + 1] for s, y in place]
        cy = [0.5 * stats[s][2 + y : 3 + y] for s, y in place]
        kern = [stats[s][4 + y : 5 + y] for s, y in place]
        w = [kern[i] * drive[i] for i in range(6)]
        u = []
        for i in range(1, 5):
            mid = unadvect(w[i], cx[i], w[i - 1], cy[i - 1], w[i + 1], cy[i + 1])
            twice = jnp.concatenate([mid, mid], axis=0)
            u.append(jnp.where(masks[i - 1], twice, 0.0))
        for y in range(2):
            i = 2 + y
            v = unadvect(u[i - 1], cx[i], u[i - 2], cy[i - 1], u[i], cy[i + 1])[:, 0:LANES]
            high, low = split(v)
            at = pl.ds(pl.multiple_of((2 * l + y) * LANES, LANES), LANES)
            v3[0:NK, at] = high
            v3[NK : 2 * NK, at] = low
            v3[2 * NK :, at] = high
        return carry

    lax.fori_loop(0, z.levels, level, 0, unroll=UNROLL)
    d = d_ref[...]
    for r in range(0, z.rows, 2):
        both = lax.dot_general(
            d, v3[:, r * LANES : (r + 2) * LANES], (((0,), (0,)), ((), ())),
            preferred_element_type=F32,
        )
        tall[pl.ds(r, z.species, stride=z.rows), :] = both[:, 0:LANES]
        tall[pl.ds(r + 1, z.species, stride=z.rows), :] = both[:, LANES:]
    out_ref[...] = tall[...].astype(BF)


def shape(*dims, dtype=F32):
    return jax.ShapeDtypeStruct(dims, dtype)


LIMIT = pltpu.CompilerParams(vmem_limit_bytes=32 * 1024 * 1024)


def swaps_of(sizes):
    ngx, ngy, nsw = sizes
    nt = ngy * nsw

    def pairs(f):
        return [(g * nt + t, f(g, t)) for g in range(ngx) for t in range(nt)]

    def other(i, parity):
        return i + 1 if i % 2 == parity else i - 1

    def along_x(parity, flip):
        def to(g, t):
            n = other(g, parity)
            return n * nt + (t ^ flip) if 0 <= n < ngx else g * nt + (t ^ 1)

        return pairs(to)

    def along_y(parity):
        def to(g, t):
            n = other(t, parity)
            return g * nt + n if 0 <= n < nt else (g ^ 1) * nt + t

        return pairs(to)

    def along_z(g, t):
        gy, s = divmod(t, nsw)
        chip, core = divmod(s, 2)
        last = nsw // 2 - 1
        up = 1 if chip == 0 else -1
        if chip in (0, last) and 0 <= gy + up < ngy:
            gy, core = gy + up, 1 - core
        elif gy == ngy - 1 and chip < last:
            chip += 1
        elif gy == 0 and chip > 0:
            chip -= 1
        else:
            core = 1 - core
        return g * nt + gy * nsw + 2 * chip + core

    return along_x, along_y, pairs(along_z)


def per_device(
    sizes,
    direction,
    courant_x,
    courant_y,
    kernel,
    mechanism,
    propagator,
    footprint_pixel,
    footprint_weight,
    footprint_owner,
    precision,
):
    species, levels = direction.shape[:2]
    z = Sizes(sizes, species, levels)
    along_x, along_y, along_z = swaps_of(sizes)
    nsw = z.nsw

    def move(v, perm):
        return lax.ppermute(v, ALL, perm)

    cells = (species * z.rows, LANES)
    pixels = precision.shape[0]
    g, msg, edge, st, d = pl.pallas_call(
        functools.partial(project_kernel, z),
        out_shape=(
            shape(z.o_st, LANES),
            shape(z.msg, LANES, dtype=BF),
            shape(z.edge, LANES),
            shape(z.st16, LANES),
            shape(3 * NK, species, dtype=BF),
        ),
        in_specs=[HBM] * 10,
        out_specs=(VMEM,) * 5,
        scratch_shapes=[
            pltpu.VMEM(cells, BF),
            pltpu.VMEM(propagator.shape, BF),
            pltpu.VMEM(courant_x.shape, F32),
            pltpu.VMEM(courant_x.shape, F32),
            pltpu.VMEM(courant_x.shape, F32),
            pltpu.VMEM(mechanism.shape, jnp.int32),
            pltpu.VMEM(mechanism.shape, jnp.int32),
            pltpu.VMEM(mechanism.shape, F32),
            pltpu.VMEM((1, 2), jnp.int32),
            pltpu.VMEM((1, pixels), F32),
            pltpu.VMEM(cells, F32),
            pltpu.SemaphoreType.DMA((10,)),
        ],
        compiler_params=LIMIT,
        name="project",
    )(
        *(
            pltpu.with_memory_space_constraint(v, pltpu.HBM)
            for v in (
                direction.reshape(cells), propagator, courant_x, courant_y, kernel, mechanism,
                footprint_pixel, footprint_weight, footprint_owner.reshape(1, 2),
                precision.reshape(1, -1),
            )
        )
    )
    e0 = move(edge, along_x(0, 0))
    e1 = move(edge, along_x(1, 0))
    m_b = move(msg, along_y(1))
    m_a = move(msg, along_y(0))
    side, far = pl.pallas_call(
        functools.partial(edges_kernel, z),
        out_shape=(shape(z.edge, LANES), shape(z.far, LANES, dtype=BF)),
        in_specs=[VMEM, VMEM],
        out_specs=(VMEM, VMEM),
        compiler_params=LIMIT,
        cost_estimate=pl.CostEstimate(
            flops=20_000_000_000, bytes_accessed=1024, transcendentals=0
        ),
        name="edges",
    )(e1, e0)
    far_b = move(far, along_y(1))
    sums, ext, corner = pl.pallas_call(
        functools.partial(columns_kernel, z),
        out_shape=(
            shape(16, LANES), shape(2, levels + 1, 8, 2 * LANES), shape(NK, LANES)
        ),
        in_specs=[VMEM] * 5,
        out_specs=(VMEM,) * 3,
        scratch_shapes=[pltpu.VMEM((z.o_st, LANES), F32), pltpu.VMEM((NK, LANES), F32)],
        compiler_params=LIMIT,
        name="columns",
    )(m_a, g, st, side, move(side, along_y(0)))
    part, corner, stat = pl.pallas_call(
        functools.partial(beyond_kernel, z),
        out_shape=(shape(8, LANES), shape(NK, LANES), shape(levels + 1, 8, LANES)),
        in_specs=[VMEM] * 5,
        out_specs=(VMEM,) * 3,
        compiler_params=LIMIT,
        name="beyond",
    )(m_b, g, st, sums, corner)
    part, block = pl.pallas_call(
        functools.partial(corner_kernel, z),
        out_shape=(shape(8, LANES), shape(levels + 1, 8, LANES)),
        in_specs=[VMEM] * 4,
        out_specs=(VMEM, VMEM),
        compiler_params=LIMIT,
        name="corner",
    )(part, corner, far_b, st)
    part = part + lax.ppermute(part, "swath", [(i, i ^ 1) for i in range(nsw)])
    turns = [
        lax.ppermute(part, "swath", [(i, i ^ (2 * k) ^ 1) for i in range(nsw)])
        for k in (1, 3, 2)
    ]
    for turn in turns:
        part = part + turn
    both = jnp.concatenate([part, move(part, along_z)], axis=0)
    b0 = move(both, along_x(0, 1))
    b1 = move(both, along_x(1, 1))
    product, dep = pl.pallas_call(
        functools.partial(product_kernel, z),
        out_shape=(shape(*cells, dtype=BF), shape(1, pixels)),
        in_specs=[VMEM] * 7,
        out_specs=(VMEM, VMEM),
        scratch_shapes=[
            pltpu.VMEM((3 * NK, z.rows * LANES), BF),
            pltpu.VMEM(cells, F32),
        ],
        compiler_params=LIMIT,
        name="product",
    )(both, b1, b0, ext, stat, block, d)
    return product.reshape(direction.shape), dep.reshape(-1)


def solution(mesh):
    placed = (
        P(None, None, ("gy", "swath"), "gx"),
        P(None, ("gy", "swath"), "gx"),
        P(None, ("gy", "swath"), "gx"),
        P(None, ("gy", "swath"), "gx"),
        P(("gy", "swath"), "gx"),
        P(),
        P(("gy", "swath"), "gx"),
        P(("gy", "swath"), "gx"),
        P(("gx", "gy", "swath"), None),
        P(("gx", "gy", "swath")),
    )
    sizes = tuple(mesh.shape[a] for a in ALL)
    return jax.shard_map(
        functools.partial(per_device, sizes),
        mesh=mesh,
        in_specs=placed,
        out_specs=(P(None, None, ("gy", "swath"), "gx"), P(("gx", "gy", "swath"))),
        check_vma=False,
    )
```

```python
import functools

import jax
import jax.numpy as jnp
from jax import lax
from jax.experimental import pallas as pl
from jax.experimental.pallas import tpu as pltpu
from jax.sharding import PartitionSpec as P

KD = 0.2
UNROLL = 10
ALL = ("gx", "gy", "swath")
LANES = 128
NM = 4
NK = NM * NM
BF = jnp.bfloat16
F32 = jnp.float32
VMEM = pl.BlockSpec(memory_space=pltpu.VMEM)
HBM = pl.BlockSpec(memory_space=pltpu.HBM)


def iota(shape, dim):
    return lax.broadcasted_iota(jnp.int32, shape, dim)


def lane_roll(v, shift):
    return pltpu.roll(v, shift % v.shape[-1], v.ndim - 1)


def split(v):
    high = v.astype(BF)
    return high, (v - high.astype(F32)).astype(BF)


class Sizes:
    def __init__(self, sizes, species, levels):
        self.ngx, self.ngy, self.nsw = sizes
        self.nt = self.ngy * self.nsw
        self.species = species
        self.levels = levels
        self.rows = 2 * levels
        self.base = 8 * levels
        self.st = self.base + 8
        self.st16 = -(-(self.st + 1) // 16) * 16
        self.o_st = self.rows * NK
        self.msg = self.o_st + 2 * self.st16
        self.edge = NK + 8
        self.halves = -(-levels // PER)
        self.far = NK + 2 * 16

    def place(self):
        gx = lax.axis_index("gx")
        swath = lax.axis_index("swath")
        return gx, swath, lax.axis_index("gy") * self.nsw + swath


def project_kernel(
    z, dir_hbm, prop_hbm, cx_hbm, cy_hbm, kern_hbm, mech_hbm, pix_hbm, wgt_hbm, own_hbm, prec_hbm,
    g_ref, msg_ref, edge_ref, st_ref, d_ref,
    dir_ref, prop_ref, cx_ref, cy_ref, kern_ref, mech_ref, pix_ref, wgt_ref, own_ref, prec_ref,
    wide, sems,
):
    sources = (
        prop_hbm, dir_hbm, cx_hbm, cy_hbm, kern_hbm, mech_hbm, pix_hbm, wgt_hbm, own_hbm, prec_hbm
    )
    targets = (
        prop_ref, dir_ref, cx_ref, cy_ref, kern_ref, mech_ref, pix_ref, wgt_ref, own_ref, prec_ref
    )
    copies = [
        pltpu.make_async_copy(a, b, sems.at[i]) for i, (a, b) in enumerate(zip(sources, targets))
    ]
    for copy in copies:
        copy.start()
    species = z.species
    copies[0].wait()
    k_of = iota((NK, species), 0)
    heads = jnp.zeros((NK, species), F32)
    for m in range(NM):
        row = prop_ref[m][0:1, :].astype(F32)
        heads = heads + jnp.where(k_of % NM == m, row, 0.0)
    total = heads + jnp.where(iota((NK, species), 1) == 0, 1.0, 0.0)
    lhs = heads.astype(BF)
    for m in range(NM):
        matrix = prop_ref[m]
        term = jnp.dot(lhs, matrix, preferred_element_type=F32)
        total = total + jnp.where(k_of // NM == m, term + matrix[0:1, :].astype(F32), 0.0)
    high, low = split(total)
    both = jnp.concatenate([high, low], axis=0)
    d_ref[...] = jnp.concatenate([high, high, low], axis=0)
    copies[1].wait()
    wide[...] = dir_ref[...].astype(F32)
    cells = jnp.concatenate(
        [wide[pl.ds(r, species, stride=z.rows), :].astype(BF) for r in range(z.rows)], axis=1
    )
    g32 = jnp.dot(both, cells, preferred_element_type=F32)
    g = g32[:NK] + g32[NK:]
    lane = iota((NK, LANES), 1)
    edge = jnp.zeros((NK, LANES), F32)
    for r in range(z.rows):
        part = g[:, r * LANES : (r + 1) * LANES]
        g_ref[r * NK : (r + 1) * NK, :] = part
        msg_ref[r * NK : (r + 1) * NK, :] = part.astype(BF)
        edge = jnp.where(lane // 4 == r, lane_roll(part, 4 * r + 2), edge)
    edge_ref[0:NK, :] = edge
    for copy in copies[2:]:
        copy.wait()
    lane = iota((8, LANES), 1)
    side = jnp.zeros((8, LANES), F32)
    blank = jnp.zeros((2, LANES), F32)
    own = jnp.where(iota((2, LANES), 0) == 0, own_ref[:, 0:1], own_ref[:, 1:2])
    for l in range(z.levels + 1):
        if l < z.levels:
            parts = [cx_ref[l], cy_ref[l], kern_ref[l], blank]
        else:
            parts = [
                (mech_ref[...] + 1).astype(F32),
                pix_ref[...].astype(F32),
                wgt_ref[...],
                own.astype(F32),
            ]
        block = jnp.concatenate(parts, axis=0)
        st_ref[8 * l : 8 * l + 8, :] = block
        side = jnp.where(lane // 4 == l, lane_roll(block, 4 * l + 2), side)
    pixels = prec_ref.shape[1]
    last = jnp.concatenate([jnp.zeros((1, LANES - pixels), F32), prec_ref[...]], axis=1)
    st_ref[z.st :, :] = jnp.broadcast_to(last, (z.st16 - z.st, LANES))
    edge_ref[NK:, :] = side
    high, low = split(st_ref[...])
    msg_ref[z.o_st : z.o_st + z.st16, :] = high
    msg_ref[z.o_st + z.st16 : z.o_st + 2 * z.st16, :] = low


def sides_of(z, gx, x0, x1):
    even = gx % 2 == 0
    right = jnp.where(even, x0, x1)
    left = jnp.where(even, x1, x0)
    return jnp.where(gx > 0, left, 0.0), jnp.where(gx < z.ngx - 1, right, 0.0)


def edges_kernel(z, x1_ref, x0_ref, side_ref, far_ref):
    gx, _, _ = z.place()
    left, right = sides_of(z, gx, x0_ref[...], x1_ref[...])
    side = jnp.where(iota(left.shape, 1) % 4 < 2, left, right)
    side_ref[...] = side
    far_ref[0:NK, :] = side[0:NK].astype(BF)
    high, low = split(jnp.concatenate([side[NK:], jnp.zeros((8, LANES), F32)], axis=0))
    far_ref[NK : NK + 16, :] = high
    far_ref[NK + 16 :, :] = low


def spread(z, side, l):
    return lane_roll(side, LANES - (4 * l + 2))


def edge_lanes(z, l, left, right, old):
    lane = iota((NK, LANES), 1)
    left = pltpu.roll(left, 8 * l + 1, 1)
    right = pltpu.roll(right, 8 * l + 3, 1)
    return jnp.where(lane == 8 * l + 1, left, jnp.where(lane == 8 * l + 2, right, old))


def fold(v):
    half = v[0:8] + v[8:16]
    return half + pltpu.roll(half, 4, 0)


def row_of(stats, odd, first):
    return jnp.where(odd, stats[first ^ 1 : (first ^ 1) + 1], stats[first : first + 1])


def columns_kernel(z, a_ref, g_ref, st_ref, side_ref, far_ref, sums_ref, ext_ref, corner_ref, ga, ha):
    _, _, t = z.place()
    odd = t % 2 == 1
    even = jnp.where(odd, 0, 1)
    sg = jnp.where(odd, -0.5, 0.5)
    W = 2 * LANES
    ga[...] = a_ref[0 : z.o_st, :].astype(F32)
    ha[...] = far_ref[0:NK, :]
    stat_a = a_ref[z.o_st : z.o_st + z.st16, :].astype(F32) + a_ref[
        z.o_st + z.st16 : z.msg, :
    ].astype(F32)
    for l in range(z.levels + 1):
        ext_ref[0, l, :, 0:LANES] = st_ref[8 * l : 8 * l + 8, :]
        ext_ref[0, l, :, LANES:] = spread(z, side_ref[NK:, :], l)
        ext_ref[1, l, :, 0:LANES] = stat_a[8 * l : 8 * l + 8]
        ext_ref[1, l, :, LANES:] = spread(z, far_ref[NK:, :], l)
    k_of = iota((NK, W), 0)
    misc = ext_ref[0, z.levels]
    misc_a = ext_ref[1, z.levels]

    def sort(mech):
        return mech == (k_of // NM + 1).astype(F32)

    mech_0 = row_of(misc, odd, 0)
    mask_0, mask_1, mask_a = sort(mech_0), sort(row_of(misc, odd, 1)), sort(row_of(misc_a, odd, 0))
    head_0 = mech_0 == (k_of % NM + 1).astype(F32)
    weight_0 = row_of(misc, odd, 4)

    def level(l, carry):
        def field(ref, side, y):
            r = 2 * l + y
            own = ref[pl.ds(pl.multiple_of(r * NK, NK), NK), :]
            return jnp.concatenate([own, pltpu.roll(side, LANES - 2 - 4 * r, 1)], axis=1)

        side = side_ref[0:NK, :]
        q0, q1 = field(g_ref, side, 1 - even), field(g_ref, side, even)
        a1, a2 = field(ga, ha[...], 1 - even), field(ga, ha[...], even)
        own, other = ext_ref[0, l], ext_ref[1, l]
        cx_0, cx_1, cx_a = (
            0.5 * row_of(own, odd, 0), 0.5 * row_of(own, odd, 1), 0.5 * row_of(other, odd, 0)
        )
        cy_0, cy_1, cy_a = (
            sg * row_of(own, odd, 2), sg * row_of(own, odd, 3), sg * row_of(other, odd, 2)
        )

        def along(mid, cx):
            return (
                (1.0 - 4.0 * KD) * mid
                + (KD - cx) * pltpu.roll(mid, W - 1, 1)
                + (KD + cx) * pltpu.roll(mid, 1, 1)
            )

        f0 = along(q0, cx_0) + (KD - cy_0) * q1
        f1 = along(q1, cx_1) + (KD - cy_1) * a1 + (KD + cy_1) * q0
        fa = along(a1, cx_a) + (KD - cy_a) * a2 + (KD + cy_a) * q1
        f0, f1, fa = (
            fold(jnp.where(m, f, 0.0)) for m, f in ((mask_0, f0), (mask_1, f1), (mask_a, fa))
        )
        h0 = along(f0, cx_0) + (KD - cy_0) * f1
        h1 = along(f1, cx_1) + (KD - cy_1) * fa + (KD + cy_1) * f0
        kern_0, kern_1 = row_of(own, odd, 4), row_of(own, odd, 5)
        s0 = carry[0] + (kern_0 * h0)[:, 0:LANES]
        s1 = carry[1] + (kern_1 * h1)[:, 0:LANES]
        step = jnp.where(mask_0, KD + cy_0, 0.0)
        scale = jnp.where(head_0, kern_0 * weight_0, 0.0)
        left = (scale * pltpu.roll(step, 1, 1) * (KD + cx_0))[:, 0:LANES]
        right = (scale * pltpu.roll(step, W - 1, 1) * (KD - cx_0))[:, 0:LANES]
        return s0, s1, edge_lanes(z, l, left, right, carry[2])

    none = jnp.zeros((8, LANES), F32)
    s0, s1, corner = lax.fori_loop(
        0, z.levels, level, (none, none, jnp.zeros((NK, LANES), F32)), unroll=UNROLL
    )
    sums_ref[0:8, :] = s0
    sums_ref[8:16, :] = s1
    corner_ref[...] = corner


def beyond_kernel(z, b_ref, g_ref, st_ref, sums_ref, old_ref, part_ref, corner_ref, stat_ref):
    _, swath, t = z.place()
    odd = t % 2 == 1
    even = jnp.where(odd, 0, 1)
    has_b = jnp.logical_and(t > 0, t < z.nt - 1)
    sg = jnp.where(odd, -0.5, 0.5)
    stat_b = b_ref[z.o_st : z.o_st + z.st16, :].astype(F32) + b_ref[
        z.o_st + z.st16 : z.msg, :
    ].astype(F32)
    stat_b = jnp.where(has_b, stat_b, 0.0)
    for l in range(z.levels + 1):
        stat_ref[l] = stat_b[8 * l : 8 * l + 8]
    k_of = iota((NK, LANES), 0)
    lane = iota((NK, LANES), 1)
    lane8 = iota((8, LANES), 1)
    sub8 = iota((8, LANES), 0)
    misc = st_ref[z.base : z.base + 8, :]
    mech_0 = row_of(misc, odd, 0)
    mech_b = row_of(stat_ref[z.levels], odd, 1)
    mask_0 = (mech_0 == (k_of // NM + 1).astype(F32)) & has_b
    mask_b = mech_b == (k_of // NM + 1).astype(F32)
    head_0 = mech_0 == (k_of % NM + 1).astype(F32)
    weight_0 = row_of(misc, odd, 4)

    def level(l, carry):
        def field(ref, y):
            at = pl.ds(pl.multiple_of((2 * l + y) * NK, NK), NK)
            return ref[at, :].astype(F32)

        q0 = field(g_ref, 1 - even)
        b1, b2 = field(b_ref, even), field(b_ref, 1 - even)
        own = st_ref[pl.ds(pl.multiple_of(8 * l, 8), 8), :]
        other = stat_ref[l]
        cx_0, cx_b = 0.5 * row_of(own, odd, 0), 0.5 * row_of(other, odd, 1)
        cy_0, cy_1, cy_b = (
            sg * row_of(own, odd, 2), sg * row_of(own, odd, 3), sg * row_of(other, odd, 3)
        )

        def along(mid, cx, lane):
            east = jnp.where(lane < LANES - 1, pltpu.roll(mid, LANES - 1, 1), 0.0)
            west = jnp.where(lane > 0, pltpu.roll(mid, 1, 1), 0.0)
            return (1.0 - 4.0 * KD) * mid + (KD - cx) * east + (KD + cx) * west

        fb = along(b1, cx_b, lane) + (KD - cy_b) * q0 + (KD + cy_b) * b2
        fb = fold(jnp.where(mask_b, fb, 0.0))
        f0 = fold(jnp.where(mask_0, (KD + cy_0) * b1, 0.0))
        kern_0, kern_1 = row_of(own, odd, 4), row_of(own, odd, 5)
        s0 = carry[0] + kern_0 * (along(f0, cx_0, lane8) + (KD + cy_0) * fb)
        s1 = carry[1] + kern_1 * (KD + cy_1) * f0
        step = jnp.where(head_0 & mask_b, kern_0 * weight_0 * (KD + cy_0), 0.0)
        left, right = step * (KD + cx_b), step * (KD - cx_b)
        corner = edge_lanes(z, l, left, right, carry[2])
        return s0, s1, corner

    s0, s1, corner = lax.fori_loop(
        0,
        z.levels,
        level,
        (sums_ref[0:8, :], sums_ref[8:16, :], jnp.zeros((NK, LANES), F32)),
        unroll=UNROLL,
    )
    corner_ref[...] = corner + old_ref[...]
    pixels = LANES // 2
    sub = iota((pixels, LANES), 0)
    total = jnp.zeros((8, LANES), F32)
    for y, sums in ((0, s0), (1, s1)):
        final = row_of(misc, odd, y) == (sub8 + 1).astype(F32)
        column = jnp.sum(jnp.where(final, sums, 0.0), axis=0, keepdims=True)
        column = column * row_of(misc, odd, 4 + y)
        hit = jnp.where(row_of(misc, odd, 2 + y) == sub.astype(F32), column, 0.0)
        tall = jnp.sum(hit, axis=1, keepdims=True)
        row = jnp.sum(
            jnp.where(sub == iota((pixels, LANES), 1), tall, 0.0), axis=0, keepdims=True
        )
        total = total + jnp.where(row_of(misc, odd, 6 + y) == sub8.astype(F32), row, 0.0)
    part_ref[...] = jnp.where(
        lane8 < pixels, total, jnp.where(sub8 == swath, st_ref[z.st : z.st + 1, :], 0.0)
    )


def corner_kernel(z, part_ref, corner_ref, far_ref, st_ref, out_ref, block_ref):
    _, _, t = z.place()
    odd = t % 2 == 1
    has_b = jnp.logical_and(t > 0, t < z.nt - 1)
    far = jnp.where(has_b, far_ref[...].astype(F32), 0.0)
    side = (far[NK : NK + 16] + far[NK + 16 :])[0:8]
    for l in range(z.levels + 1):
        block_ref[l] = spread(z, side, l)
    g = far[0:NK]
    g = jnp.where(odd, g, pltpu.roll(g, LANES - 4, 1))
    share = jnp.sum(corner_ref[...] * g, axis=0, keepdims=True)
    lane = iota((1, LANES), 1)
    sub8 = iota((8, LANES), 0)
    lane8 = iota((8, LANES), 1)
    misc = st_ref[z.base : z.base + 8, :]
    pixel = row_of(misc, odd, 2)
    owner = row_of(misc, odd, 6)
    total = part_ref[...]
    for c, column in ((1, 0), (2, LANES - 1)):
        value = jnp.sum(jnp.where(lane % 8 == c, share, 0.0), axis=1, keepdims=True)
        at = slice(column, column + 1)
        hit = (lane8.astype(F32) == pixel[:, at]) & (sub8.astype(F32) == owner[:, at])
        total = total + jnp.where(hit, value, 0.0)
    out_ref[...] = total


def weigh(v):
    return v * lane_roll(v, LANES // 2)


def outer_rows(z, swath):
    sub = iota((8, LANES), 0)
    return ((sub < 2) & (swath == 0)) | ((sub >= 4) & (swath == z.nsw - 1))


def find(z, outer, dep, owner, index):
    table = jnp.zeros((8, LANES), F32)
    for o in range(z.nsw):
        row = jnp.where(outer, dep[8 + o : 9 + o, :], dep[o : o + 1, :])
        table = jnp.where(owner == float(o), row, table)
    return jnp.take_along_axis(table, index, axis=1)


PLACE = [(s, y) for s in range(3) for y in range(2)]


def twice_back(miscs, back, stats):
    W = back.shape[1]
    m_of = iota((8, W), 0) % NM
    k_of = iota((NK, W), 0) // NM
    mech = [miscs[s][y : y + 1] for s, y in PLACE]
    cx = [0.5 * stats[s][y : y + 1] for s, y in PLACE]
    cy = [0.5 * stats[s][2 + y : 3 + y] for s, y in PLACE]
    kern = [stats[s][4 + y : 5 + y] for s, y in PLACE]

    def unadvect(v, i, at):
        return (
            (1.0 - 4.0 * KD) * v[at]
            + pltpu.roll((KD - cx[i]) * v[at], 1, 1)
            + pltpu.roll((KD + cx[i]) * v[at], W - 1, 1)
            + (KD - cy[i - 1]) * v[at - 1]
            + (KD + cy[i + 1]) * v[at + 1]
        )

    w = [
        kern[i] * jnp.where(mech[i] == (m_of + 1).astype(F32), back[i : i + 1, :], 0.0)
        for i in range(6)
    ]
    u = []
    for i in range(1, 5):
        mid = unadvect(w, i, i)
        both = jnp.concatenate([mid, mid], axis=0)
        u.append(jnp.where(mech[i] == (k_of + 1).astype(F32), both, 0.0))
    return [unadvect(u, 2 + y, 1 + y) for y in range(2)]


PER = 5


def tiles_of(z, oa_ref, stat_ref, block_ref):
    _, _, t = z.place()
    odd = t % 2 == 1

    def tiles(l):
        a = oa_ref[1, l]
        b = jnp.concatenate([stat_ref[l], block_ref[l]], axis=1)
        return jnp.where(odd, a, b), oa_ref[0, l], jnp.where(odd, b, a)

    return tiles


def stack(miscs, f):
    out = jnp.zeros((8, 2 * LANES), F32)
    for s, y in PLACE:
        row = miscs[s][2 * f + y : 2 * f + y + 1]
        out = jnp.where(iota(out.shape, 0) == 2 * s + y, row, out)
    return out


def coefs_kernel(z, oa_ref, stat_ref, block_ref, coef_ref, far_ref):
    tiles = tiles_of(z, oa_ref, stat_ref, block_ref)
    miscs = tiles(z.levels)
    for n, f in enumerate((3, 1, 2)):
        far_ref[8 * n : 8 * n + 8, :] = stack(miscs, f)[:, LANES:]
    sub = iota((8, LANES), 0)
    lane = iota((8, LANES), 1)

    def pack(block, g, old):
        b = 16 * g
        rel = lane - b
        own, side = block[:, 0:LANES], block[:, LANES:]
        out = old
        for lo, v, shift in ((0, own, 4), (4, side, 4), (8, side, 12), (12, own, 12)):
            out = jnp.where((rel >= lo) & (rel < lo + 4), lane_roll(v, b + shift), out)
        return out

    misc_seams = []
    for s in range(3):
        all_levels = jnp.zeros((8, LANES), F32)
        for g in range(PER):
            all_levels = pack(miscs[s], g, all_levels)
        misc_seams.append(all_levels)
    rel = lane % 16
    nearer = (rel == 4) | (rel == 11)
    farther = (rel == 5) | (rel == 10)
    for h in range(z.halves):
        packed = [jnp.zeros((8, LANES), F32)] * 3
        for g in range(min(PER, z.levels - PER * h)):
            blocks = tiles(PER * h + g)
            packed = [pack(blocks[s], g, packed[s]) for s in range(3)]

        def respond(columns, i, packed=packed):
            one = jnp.where(columns & (sub == i), 1.0, 0.0)
            return twice_back(misc_seams, one, packed)

        beside = {i: respond(nearer, i) for i in range(1, 5)}
        beyond = {i: respond(farther, i) for i in (2, 3)}
        for y in range(2):
            for c, v in enumerate(
                (beside[2 + y][y], beyond[2 + y][y], beside[1 + y][y], beside[3 + y][y])
            ):
                coef_ref[h, y, c] = v


def prepare_kernel(z, own_ref, oa_ref, stat_ref, block_ref, v_ref, dep_ref):
    _, swath, _ = z.place()
    tiles = tiles_of(z, oa_ref, stat_ref, block_ref)
    miscs = tiles(z.levels)
    dep = weigh(own_ref[...])
    sub = iota((8, LANES), 0)
    dep_ref[...] = jnp.sum(jnp.where(sub == swath, dep[0:8], 0.0), axis=0, keepdims=True)[
        :, 0 : LANES // 2
    ]
    owner, index, weight = (stack(miscs, f)[:, 0:LANES] for f in (3, 1, 2))
    near = find(z, outer_rows(z, swath), dep, owner, index.astype(jnp.int32))
    back = jnp.concatenate([weight * near, jnp.zeros((8, LANES), F32)], axis=1)

    def level(l, carry):
        out = twice_back(miscs, back, tiles(l))
        for y in range(2):
            at = pl.ds(pl.multiple_of((2 * l + y) * LANES, LANES), LANES)
            v_ref[:, at] = out[y][:, 0:LANES]
        return carry

    lax.fori_loop(0, z.levels, level, 0, unroll=UNROLL)


def join_kernel(part_ref, next_ref, far_ref, out_ref):
    out_ref[0:8, :] = part_ref[...]
    out_ref[8:16, :] = next_ref[...]


def product_kernel(
    z, x1_ref, x0_ref, v_ref, coef_ref, far_ref, d_ref, out_ref, v3, tall
):
    gx, swath, _ = z.place()
    left, right = sides_of(z, gx, x0_ref[...], x1_ref[...])
    outer = outer_rows(z, swath)
    owner, index = far_ref[0:8, :], far_ref[8:16, :].astype(jnp.int32)
    lane = iota((8, LANES), 1)
    beside = far_ref[16:24, :] * jnp.where(
        lane < 2,
        find(z, outer, weigh(right), owner[:, 0:1], index),
        find(z, outer, weigh(left), owner[:, LANES - 1 :], index),
    )
    on_left = lane % 16 >= 8
    near = jnp.where(on_left, beside[:, LANES - 1 :], beside[:, 0:1])
    away = jnp.where(on_left, beside[:, LANES - 2 : LANES - 1], beside[:, 1:2])
    wide = iota((NK, LANES), 1)
    for h in range(z.halves):
        seams = []
        for y in range(2):
            a, b, c, e = (coef_ref[h, y, i] for i in range(4))
            seams.append(
                (a * near[2 + y : 3 + y] + b * away[2 + y : 3 + y])
                + (c * near[1 + y : 2 + y] + e * near[3 + y : 4 + y])
            )
        for g in range(min(PER, z.levels - PER * h)):
            for y in range(2):
                r = 2 * (PER * h + g) + y
                first = lane_roll(seams[y], LANES - 16 * g - 12)
                last = lane_roll(seams[y], 124 - 16 * g)
                more = jnp.where(wide < 2, first, jnp.where(wide >= LANES - 2, last, 0.0))
                at = slice(r * LANES, (r + 1) * LANES)
                high, low = split(v_ref[:, at] + more)
                v3[0:NK, at] = high
                v3[NK : 2 * NK, at] = low
                v3[2 * NK :, at] = high
    d = d_ref[...]
    for r in range(0, z.rows, 2):
        both = lax.dot_general(
            d, v3[:, r * LANES : (r + 2) * LANES], (((0,), (0,)), ((), ())),
            preferred_element_type=F32,
        )
        tall[pl.ds(r, z.species, stride=z.rows), :] = both[:, 0:LANES]
        tall[pl.ds(r + 1, z.species, stride=z.rows), :] = both[:, LANES:]
    out_ref[...] = tall[...].astype(BF)


def shape(*dims, dtype=F32):
    return jax.ShapeDtypeStruct(dims, dtype)


LIMIT = pltpu.CompilerParams(vmem_limit_bytes=32 * 1024 * 1024)


def swaps_of(sizes):
    ngx, ngy, nsw = sizes
    nt = ngy * nsw

    def pairs(f):
        return [(g * nt + t, f(g, t)) for g in range(ngx) for t in range(nt)]

    def other(i, parity):
        return i + 1 if i % 2 == parity else i - 1

    def along_x(parity, flip):
        def to(g, t):
            n = other(g, parity)
            return n * nt + (t ^ flip) if 0 <= n < ngx else g * nt + (t ^ 1)

        return pairs(to)

    def along_y(parity):
        def to(g, t):
            n = other(t, parity)
            return g * nt + n if 0 <= n < nt else (g ^ 1) * nt + t

        return pairs(to)

    def along_z(g, t):
        gy, s = divmod(t, nsw)
        chip, core = divmod(s, 2)
        last = nsw // 2 - 1
        up = 1 if chip == 0 else -1
        if chip in (0, last) and 0 <= gy + up < ngy:
            gy, core = gy + up, 1 - core
        elif gy == ngy - 1 and chip < last:
            chip += 1
        elif gy == 0 and chip > 0:
            chip -= 1
        else:
            core = 1 - core
        return g * nt + gy * nsw + 2 * chip + core

    return along_x, along_y, pairs(along_z)


def per_device(
    sizes,
    direction,
    courant_x,
    courant_y,
    kernel,
    mechanism,
    propagator,
    footprint_pixel,
    footprint_weight,
    footprint_owner,
    precision,
):
    species, levels = direction.shape[:2]
    z = Sizes(sizes, species, levels)
    along_x, along_y, along_z = swaps_of(sizes)
    nsw = z.nsw

    def move(v, perm):
        return lax.ppermute(v, ALL, perm)

    cells = (species * z.rows, LANES)
    pixels = precision.shape[0]
    g, msg, edge, st, d = pl.pallas_call(
        functools.partial(project_kernel, z),
        out_shape=(
            shape(z.o_st, LANES),
            shape(z.msg, LANES, dtype=BF),
            shape(z.edge, LANES),
            shape(z.st16, LANES),
            shape(3 * NK, species, dtype=BF),
        ),
        in_specs=[HBM] * 10,
        out_specs=(VMEM,) * 5,
        scratch_shapes=[
            pltpu.VMEM(cells, BF),
            pltpu.VMEM(propagator.shape, BF),
            pltpu.VMEM(courant_x.shape, F32),
            pltpu.VMEM(courant_x.shape, F32),
            pltpu.VMEM(courant_x.shape, F32),
            pltpu.VMEM(mechanism.shape, jnp.int32),
            pltpu.VMEM(mechanism.shape, jnp.int32),
            pltpu.VMEM(mechanism.shape, F32),
            pltpu.VMEM((1, 2), jnp.int32),
            pltpu.VMEM((1, pixels), F32),
            pltpu.VMEM(cells, F32),
            pltpu.SemaphoreType.DMA((10,)),
        ],
        compiler_params=LIMIT,
        name="project",
    )(
        *(
            pltpu.with_memory_space_constraint(v, pltpu.HBM)
            for v in (
                direction.reshape(cells), propagator, courant_x, courant_y, kernel, mechanism,
                footprint_pixel, footprint_weight, footprint_owner.reshape(1, 2),
                precision.reshape(1, -1),
            )
        )
    )
    e0 = move(edge, along_x(0, 0))
    e1 = move(edge, along_x(1, 0))
    m_b = move(msg, along_y(1))
    m_a = move(msg, along_y(0))
    side, far = pl.pallas_call(
        functools.partial(edges_kernel, z),
        out_shape=(shape(z.edge, LANES), shape(z.far, LANES, dtype=BF)),
        in_specs=[VMEM, VMEM],
        out_specs=(VMEM, VMEM),
        compiler_params=LIMIT,
        cost_estimate=pl.CostEstimate(
            flops=20_000_000_000, bytes_accessed=1024, transcendentals=0
        ),
        name="edges",
    )(e1, e0)
    far_b = move(far, along_y(1))
    sums, ext, corner = pl.pallas_call(
        functools.partial(columns_kernel, z),
        out_shape=(
            shape(16, LANES), shape(2, levels + 1, 8, 2 * LANES), shape(NK, LANES)
        ),
        in_specs=[VMEM] * 5,
        out_specs=(VMEM,) * 3,
        scratch_shapes=[pltpu.VMEM((z.o_st, LANES), F32), pltpu.VMEM((NK, LANES), F32)],
        compiler_params=LIMIT,
        name="columns",
    )(m_a, g, st, side, move(side, along_y(0)))
    part, corner, stat = pl.pallas_call(
        functools.partial(beyond_kernel, z),
        out_shape=(shape(8, LANES), shape(NK, LANES), shape(levels + 1, 8, LANES)),
        in_specs=[VMEM] * 5,
        out_specs=(VMEM,) * 3,
        compiler_params=LIMIT,
        name="beyond",
    )(m_b, g, st, sums, corner)
    part, block = pl.pallas_call(
        functools.partial(corner_kernel, z),
        out_shape=(shape(8, LANES), shape(levels + 1, 8, LANES)),
        in_specs=[VMEM] * 4,
        out_specs=(VMEM, VMEM),
        compiler_params=LIMIT,
        name="corner",
    )(part, corner, far_b, st)
    part = part + lax.ppermute(part, "swath", [(i, i ^ 1) for i in range(nsw)])
    turns = [
        lax.ppermute(part, "swath", [(i, i ^ (2 * k) ^ 1) for i in range(nsw)])
        for k in (1, 3, 2)
    ]
    for turn in turns:
        part = part + turn
    coef, far = pl.pallas_call(
        functools.partial(coefs_kernel, z),
        out_shape=(shape(z.halves, 2, 4, NK, LANES), shape(24, LANES)),
        in_specs=[VMEM] * 3,
        out_specs=(VMEM, VMEM),
        compiler_params=LIMIT,
        name="coefs",
    )(ext, stat, block)
    both = pl.pallas_call(
        join_kernel,
        out_shape=shape(16, LANES),
        in_specs=[VMEM] * 3,
        out_specs=VMEM,
        compiler_params=LIMIT,
        name="join",
    )(part, move(part, along_z), far)
    b0 = move(both, along_x(0, 1))
    b1 = move(both, along_x(1, 1))
    v, dep = pl.pallas_call(
        functools.partial(prepare_kernel, z),
        out_shape=(
            shape(NK, z.rows * LANES),
            shape(1, pixels),
        ),
        in_specs=[VMEM] * 4,
        out_specs=(VMEM, VMEM),
        compiler_params=LIMIT,
        name="prepare",
    )(both, ext, stat, block)
    product = pl.pallas_call(
        functools.partial(product_kernel, z),
        out_shape=shape(*cells, dtype=BF),
        in_specs=[VMEM] * 6,
        out_specs=VMEM,
        scratch_shapes=[
            pltpu.VMEM((3 * NK, z.rows * LANES), BF),
            pltpu.VMEM(cells, F32),
        ],
        compiler_params=LIMIT,
        name="product",
    )(b1, b0, v, coef, far, d)
    return product.reshape(direction.shape), dep.reshape(-1)


def solution(mesh):
    placed = (
        P(None, None, ("gy", "swath"), "gx"),
        P(None, ("gy", "swath"), "gx"),
        P(None, ("gy", "swath"), "gx"),
        P(None, ("gy", "swath"), "gx"),
        P(("gy", "swath"), "gx"),
        P(),
        P(("gy", "swath"), "gx"),
        P(("gy", "swath"), "gx"),
        P(("gx", "gy", "swath"), None),
        P(("gx", "gy", "swath")),
    )
    sizes = tuple(mesh.shape[a] for a in ALL)
    return jax.shard_map(
        functools.partial(per_device, sizes),
        mesh=mesh,
        in_specs=placed,
        out_specs=(P(None, None, ("gy", "swath"), "gx"), P(("gx", "gy", "swath"))),
        check_vma=False,
    )
```

```python
import functools

import jax
import jax.numpy as jnp
from jax import lax
from jax.experimental import pallas as pl
from jax.experimental.pallas import tpu as pltpu
from jax.sharding import PartitionSpec as P

KD = 0.2
UNROLL = 10
ALL = ("gx", "gy", "swath")
LANES = 128
NM = 4
NK = NM * NM
BF = jnp.bfloat16
F32 = jnp.float32
VMEM = pl.BlockSpec(memory_space=pltpu.VMEM)
HBM = pl.BlockSpec(memory_space=pltpu.HBM)


def iota(shape, dim):
    return lax.broadcasted_iota(jnp.int32, shape, dim)


def lane_roll(v, shift):
    return pltpu.roll(v, shift % v.shape[-1], v.ndim - 1)


def split(v):
    high = v.astype(BF)
    return high, (v - high.astype(F32)).astype(BF)


class Sizes:
    def __init__(self, sizes, species, levels):
        self.ngx, self.ngy, self.nsw = sizes
        self.nt = self.ngy * self.nsw
        self.species = species
        self.levels = levels
        self.rows = 2 * levels
        self.base = 8 * levels
        self.st = self.base + 8
        self.st16 = -(-(self.st + 1) // 16) * 16
        self.o_st = self.rows * NK
        self.msg = self.o_st + 2 * self.st16
        self.edge = NK + 8
        self.halves = -(-levels // PER)
        self.far = NK + 2 * 16

    def place(self):
        gx = lax.axis_index("gx")
        swath = lax.axis_index("swath")
        return gx, swath, lax.axis_index("gy") * self.nsw + swath


def project_kernel(
    z, dir_hbm, prop_hbm, cx_hbm, cy_hbm, kern_hbm, mech_hbm, pix_hbm, wgt_hbm, own_hbm, prec_hbm,
    g_ref, msg_ref, edge_ref, st_ref, d_ref,
    dir_ref, prop_ref, cx_ref, cy_ref, kern_ref, mech_ref, pix_ref, wgt_ref, own_ref, prec_ref,
    wide, sems,
):
    sources = (
        prop_hbm, dir_hbm, cx_hbm, cy_hbm, kern_hbm, mech_hbm, pix_hbm, wgt_hbm, own_hbm, prec_hbm
    )
    targets = (
        prop_ref, dir_ref, cx_ref, cy_ref, kern_ref, mech_ref, pix_ref, wgt_ref, own_ref, prec_ref
    )
    copies = [
        pltpu.make_async_copy(a, b, sems.at[i]) for i, (a, b) in enumerate(zip(sources, targets))
    ]
    for copy in copies:
        copy.start()
    species = z.species
    copies[0].wait()
    k_of = iota((NK, species), 0)
    heads = jnp.zeros((NK, species), F32)
    for m in range(NM):
        row = prop_ref[m][0:1, :].astype(F32)
        heads = heads + jnp.where(k_of % NM == m, row, 0.0)
    total = heads + jnp.where(iota((NK, species), 1) == 0, 1.0, 0.0)
    lhs = heads.astype(BF)
    for m in range(NM):
        matrix = prop_ref[m]
        term = jnp.dot(lhs, matrix, preferred_element_type=F32)
        total = total + jnp.where(k_of // NM == m, term + matrix[0:1, :].astype(F32), 0.0)
    high, low = split(total)
    both = jnp.concatenate([high, low], axis=0)
    d_ref[...] = jnp.concatenate([high, high, low], axis=0)
    copies[1].wait()
    wide[...] = dir_ref[...].astype(F32)
    cells = jnp.concatenate(
        [wide[pl.ds(r, species, stride=z.rows), :].astype(BF) for r in range(z.rows)], axis=1
    )
    g32 = jnp.dot(both, cells, preferred_element_type=F32)
    g = g32[:NK] + g32[NK:]
    lane = iota((NK, LANES), 1)
    edge = jnp.zeros((NK, LANES), F32)
    for r in range(z.rows):
        part = g[:, r * LANES : (r + 1) * LANES]
        g_ref[r * NK : (r + 1) * NK, :] = part
        msg_ref[r * NK : (r + 1) * NK, :] = part.astype(BF)
        edge = jnp.where(lane // 4 == r, lane_roll(part, 4 * r + 2), edge)
    edge_ref[0:NK, :] = edge
    for copy in copies[2:]:
        copy.wait()
    lane = iota((8, LANES), 1)
    side = jnp.zeros((8, LANES), F32)
    blank = jnp.zeros((2, LANES), F32)
    own = jnp.where(iota((2, LANES), 0) == 0, own_ref[:, 0:1], own_ref[:, 1:2])
    for l in range(z.levels + 1):
        if l < z.levels:
            parts = [cx_ref[l], cy_ref[l], kern_ref[l], blank]
        else:
            parts = [
                (mech_ref[...] + 1).astype(F32),
                pix_ref[...].astype(F32),
                wgt_ref[...],
                own.astype(F32),
            ]
        block = jnp.concatenate(parts, axis=0)
        st_ref[8 * l : 8 * l + 8, :] = block
        side = jnp.where(lane // 4 == l, lane_roll(block, 4 * l + 2), side)
    pixels = prec_ref.shape[1]
    last = jnp.concatenate([jnp.zeros((1, LANES - pixels), F32), prec_ref[...]], axis=1)
    st_ref[z.st :, :] = jnp.broadcast_to(last, (z.st16 - z.st, LANES))
    edge_ref[NK:, :] = side
    high, low = split(st_ref[...])
    msg_ref[z.o_st : z.o_st + z.st16, :] = high
    msg_ref[z.o_st + z.st16 : z.o_st + 2 * z.st16, :] = low


def sides_of(z, gx, x0, x1):
    even = gx % 2 == 0
    right = jnp.where(even, x0, x1)
    left = jnp.where(even, x1, x0)
    return jnp.where(gx > 0, left, 0.0), jnp.where(gx < z.ngx - 1, right, 0.0)


def edges_kernel(z, x1_ref, x0_ref, side_ref, far_ref):
    gx, _, _ = z.place()
    left, right = sides_of(z, gx, x0_ref[...], x1_ref[...])
    side = jnp.where(iota(left.shape, 1) % 4 < 2, left, right)
    side_ref[...] = side
    far_ref[0:NK, :] = side[0:NK].astype(BF)
    high, low = split(jnp.concatenate([side[NK:], jnp.zeros((8, LANES), F32)], axis=0))
    far_ref[NK : NK + 16, :] = high
    far_ref[NK + 16 :, :] = low


def spread(z, side, l):
    return lane_roll(side, LANES - (4 * l + 2))


def edge_lanes(z, l, left, right, old):
    lane = iota((NK, LANES), 1)
    left = pltpu.roll(left, 8 * l + 1, 1)
    right = pltpu.roll(right, 8 * l + 3, 1)
    return jnp.where(lane == 8 * l + 1, left, jnp.where(lane == 8 * l + 2, right, old))


def fold(v):
    half = v[0:8] + v[8:16]
    return half + pltpu.roll(half, 4, 0)


def row_of(stats, odd, first):
    return jnp.where(odd, stats[first ^ 1 : (first ^ 1) + 1], stats[first : first + 1])


def columns_kernel(z, a_ref, g_ref, st_ref, side_ref, far_ref, sums_ref, ext_ref, corner_ref, ga, ha):
    _, _, t = z.place()
    odd = t % 2 == 1
    even = jnp.where(odd, 0, 1)
    sg = jnp.where(odd, -0.5, 0.5)
    W = 2 * LANES
    ga[...] = a_ref[0 : z.o_st, :].astype(F32)
    ha[...] = far_ref[0:NK, :]
    stat_a = a_ref[z.o_st : z.o_st + z.st16, :].astype(F32) + a_ref[
        z.o_st + z.st16 : z.msg, :
    ].astype(F32)
    for l in range(z.levels + 1):
        ext_ref[0, l, :, 0:LANES] = st_ref[8 * l : 8 * l + 8, :]
        ext_ref[0, l, :, LANES:] = spread(z, side_ref[NK:, :], l)
        ext_ref[1, l, :, 0:LANES] = stat_a[8 * l : 8 * l + 8]
        ext_ref[1, l, :, LANES:] = spread(z, far_ref[NK:, :], l)
    k_of = iota((NK, W), 0)
    misc = ext_ref[0, z.levels]
    misc_a = ext_ref[1, z.levels]

    def sort(mech):
        return mech == (k_of // NM + 1).astype(F32)

    mech_0 = row_of(misc, odd, 0)
    mask_0, mask_1, mask_a = sort(mech_0), sort(row_of(misc, odd, 1)), sort(row_of(misc_a, odd, 0))
    head_0 = mech_0 == (k_of % NM + 1).astype(F32)
    weight_0 = row_of(misc, odd, 4)

    def level(l, carry):
        def field(ref, side, y):
            r = 2 * l + y
            own = ref[pl.ds(pl.multiple_of(r * NK, NK), NK), :]
            return jnp.concatenate([own, pltpu.roll(side, LANES - 2 - 4 * r, 1)], axis=1)

        side = side_ref[0:NK, :]
        q0, q1 = field(g_ref, side, 1 - even), field(g_ref, side, even)
        a1, a2 = field(ga, ha[...], 1 - even), field(ga, ha[...], even)
        own, other = ext_ref[0, l], ext_ref[1, l]
        cx_0, cx_1, cx_a = (
            0.5 * row_of(own, odd, 0), 0.5 * row_of(own, odd, 1), 0.5 * row_of(other, odd, 0)
        )
        cy_0, cy_1, cy_a = (
            sg * row_of(own, odd, 2), sg * row_of(own, odd, 3), sg * row_of(other, odd, 2)
        )

        def along(mid, cx):
            return (
                (1.0 - 4.0 * KD) * mid
                + (KD - cx) * pltpu.roll(mid, W - 1, 1)
                + (KD + cx) * pltpu.roll(mid, 1, 1)
            )

        f0 = along(q0, cx_0) + (KD - cy_0) * q1
        f1 = along(q1, cx_1) + (KD - cy_1) * a1 + (KD + cy_1) * q0
        fa = along(a1, cx_a) + (KD - cy_a) * a2 + (KD + cy_a) * q1
        f0, f1, fa = (
            fold(jnp.where(m, f, 0.0)) for m, f in ((mask_0, f0), (mask_1, f1), (mask_a, fa))
        )
        h0 = along(f0, cx_0) + (KD - cy_0) * f1
        h1 = along(f1, cx_1) + (KD - cy_1) * fa + (KD + cy_1) * f0
        kern_0, kern_1 = row_of(own, odd, 4), row_of(own, odd, 5)
        s0 = carry[0] + (kern_0 * h0)[:, 0:LANES]
        s1 = carry[1] + (kern_1 * h1)[:, 0:LANES]
        step = jnp.where(mask_0, KD + cy_0, 0.0)
        scale = jnp.where(head_0, kern_0 * weight_0, 0.0)
        left = (scale * pltpu.roll(step, 1, 1) * (KD + cx_0))[:, 0:LANES]
        right = (scale * pltpu.roll(step, W - 1, 1) * (KD - cx_0))[:, 0:LANES]
        return s0, s1, edge_lanes(z, l, left, right, carry[2])

    none = jnp.zeros((8, LANES), F32)
    s0, s1, corner = lax.fori_loop(
        0, z.levels, level, (none, none, jnp.zeros((NK, LANES), F32)), unroll=UNROLL
    )
    sums_ref[0:8, :] = s0
    sums_ref[8:16, :] = s1
    corner_ref[...] = corner


def beyond_kernel(z, b_ref, g_ref, st_ref, sums_ref, old_ref, part_ref, corner_ref, stat_ref):
    _, swath, t = z.place()
    odd = t % 2 == 1
    even = jnp.where(odd, 0, 1)
    has_b = jnp.logical_and(t > 0, t < z.nt - 1)
    sg = jnp.where(odd, -0.5, 0.5)
    stat_b = b_ref[z.o_st : z.o_st + z.st16, :].astype(F32) + b_ref[
        z.o_st + z.st16 : z.msg, :
    ].astype(F32)
    stat_b = jnp.where(has_b, stat_b, 0.0)
    for l in range(z.levels + 1):
        stat_ref[l] = stat_b[8 * l : 8 * l + 8]
    k_of = iota((NK, LANES), 0)
    lane = iota((NK, LANES), 1)
    lane8 = iota((8, LANES), 1)
    sub8 = iota((8, LANES), 0)
    misc = st_ref[z.base : z.base + 8, :]
    mech_0 = row_of(misc, odd, 0)
    mech_b = row_of(stat_ref[z.levels], odd, 1)
    mask_0 = (mech_0 == (k_of // NM + 1).astype(F32)) & has_b
    mask_b = mech_b == (k_of // NM + 1).astype(F32)
    head_0 = mech_0 == (k_of % NM + 1).astype(F32)
    weight_0 = row_of(misc, odd, 4)

    def level(l, carry):
        def field(ref, y):
            at = pl.ds(pl.multiple_of((2 * l + y) * NK, NK), NK)
            return ref[at, :].astype(F32)

        q0 = field(g_ref, 1 - even)
        b1, b2 = field(b_ref, even), field(b_ref, 1 - even)
        own = st_ref[pl.ds(pl.multiple_of(8 * l, 8), 8), :]
        other = stat_ref[l]
        cx_0, cx_b = 0.5 * row_of(own, odd, 0), 0.5 * row_of(other, odd, 1)
        cy_0, cy_1, cy_b = (
            sg * row_of(own, odd, 2), sg * row_of(own, odd, 3), sg * row_of(other, odd, 3)
        )

        def along(mid, cx, lane):
            east = jnp.where(lane < LANES - 1, pltpu.roll(mid, LANES - 1, 1), 0.0)
            west = jnp.where(lane > 0, pltpu.roll(mid, 1, 1), 0.0)
            return (1.0 - 4.0 * KD) * mid + (KD - cx) * east + (KD + cx) * west

        fb = along(b1, cx_b, lane) + (KD - cy_b) * q0 + (KD + cy_b) * b2
        fb = fold(jnp.where(mask_b, fb, 0.0))
        f0 = fold(jnp.where(mask_0, (KD + cy_0) * b1, 0.0))
        kern_0, kern_1 = row_of(own, odd, 4), row_of(own, odd, 5)
        s0 = carry[0] + kern_0 * (along(f0, cx_0, lane8) + (KD + cy_0) * fb)
        s1 = carry[1] + kern_1 * (KD + cy_1) * f0
        step = jnp.where(head_0 & mask_b, kern_0 * weight_0 * (KD + cy_0), 0.0)
        left, right = step * (KD + cx_b), step * (KD - cx_b)
        corner = edge_lanes(z, l, left, right, carry[2])
        return s0, s1, corner

    s0, s1, corner = lax.fori_loop(
        0,
        z.levels,
        level,
        (sums_ref[0:8, :], sums_ref[8:16, :], jnp.zeros((NK, LANES), F32)),
        unroll=UNROLL,
    )
    corner_ref[...] = corner + old_ref[...]
    pixels = LANES // 2
    sub = iota((pixels, LANES), 0)
    total = jnp.zeros((8, LANES), F32)
    for y, sums in ((0, s0), (1, s1)):
        final = row_of(misc, odd, y) == (sub8 + 1).astype(F32)
        column = jnp.sum(jnp.where(final, sums, 0.0), axis=0, keepdims=True)
        column = column * row_of(misc, odd, 4 + y)
        hit = jnp.where(row_of(misc, odd, 2 + y) == sub.astype(F32), column, 0.0)
        tall = jnp.sum(hit, axis=1, keepdims=True)
        row = jnp.sum(
            jnp.where(sub == iota((pixels, LANES), 1), tall, 0.0), axis=0, keepdims=True
        )
        total = total + jnp.where(row_of(misc, odd, 6 + y) == sub8.astype(F32), row, 0.0)
    part_ref[...] = jnp.where(
        lane8 < pixels, total, jnp.where(sub8 == swath, st_ref[z.st : z.st + 1, :], 0.0)
    )


def corner_kernel(z, part_ref, corner_ref, far_ref, st_ref, out_ref, block_ref):
    _, _, t = z.place()
    odd = t % 2 == 1
    has_b = jnp.logical_and(t > 0, t < z.nt - 1)
    far = jnp.where(has_b, far_ref[...].astype(F32), 0.0)
    side = (far[NK : NK + 16] + far[NK + 16 :])[0:8]
    for l in range(z.levels + 1):
        block_ref[l] = spread(z, side, l)
    g = far[0:NK]
    g = jnp.where(odd, g, pltpu.roll(g, LANES - 4, 1))
    share = jnp.sum(corner_ref[...] * g, axis=0, keepdims=True)
    lane = iota((1, LANES), 1)
    sub8 = iota((8, LANES), 0)
    lane8 = iota((8, LANES), 1)
    misc = st_ref[z.base : z.base + 8, :]
    pixel = row_of(misc, odd, 2)
    owner = row_of(misc, odd, 6)
    total = part_ref[...]
    for c, column in ((1, 0), (2, LANES - 1)):
        value = jnp.sum(jnp.where(lane % 8 == c, share, 0.0), axis=1, keepdims=True)
        at = slice(column, column + 1)
        hit = (lane8.astype(F32) == pixel[:, at]) & (sub8.astype(F32) == owner[:, at])
        total = total + jnp.where(hit, value, 0.0)
    out_ref[...] = total


def weigh(v):
    return v * lane_roll(v, LANES // 2)


def outer_rows(z, swath):
    sub = iota((8, LANES), 0)
    return ((sub < 2) & (swath == 0)) | ((sub >= 4) & (swath == z.nsw - 1))


def table_of(outer, sums, owner):
    row = owner.astype(jnp.int32)
    return jnp.where(
        outer,
        jnp.take_along_axis(sums[8:16], row, axis=0),
        jnp.take_along_axis(sums[0:8], row, axis=0),
    )


def find(table, index):
    at = index.astype(jnp.int32)
    half = LANES // 2
    return jnp.take_along_axis(table, at, axis=1) * jnp.take_along_axis(table, at + half, axis=1)


PLACE = [(s, y) for s in range(3) for y in range(2)]


def twice_back(miscs, back, stats):
    W = back.shape[1]
    m_of = iota((8, W), 0) % NM
    k_of = iota((NK, W), 0) // NM
    mech = [miscs[s][y : y + 1] for s, y in PLACE]
    cx = [0.5 * stats[s][y : y + 1] for s, y in PLACE]
    cy = [0.5 * stats[s][2 + y : 3 + y] for s, y in PLACE]
    kern = [stats[s][4 + y : 5 + y] for s, y in PLACE]

    def unadvect(v, i, at):
        return (
            (1.0 - 4.0 * KD) * v[at]
            + pltpu.roll((KD - cx[i]) * v[at], 1, 1)
            + pltpu.roll((KD + cx[i]) * v[at], W - 1, 1)
            + (KD - cy[i - 1]) * v[at - 1]
            + (KD + cy[i + 1]) * v[at + 1]
        )

    w = [
        kern[i] * jnp.where(mech[i] == (m_of + 1).astype(F32), back[i : i + 1, :], 0.0)
        for i in range(6)
    ]
    u = []
    for i in range(1, 5):
        mid = unadvect(w, i, i)
        both = jnp.concatenate([mid, mid], axis=0)
        u.append(jnp.where(mech[i] == (k_of + 1).astype(F32), both, 0.0))
    return [unadvect(u, 2 + y, 1 + y) for y in range(2)]


PER = 5


def tiles_of(z, oa_ref, stat_ref, block_ref):
    _, _, t = z.place()
    odd = t % 2 == 1

    def tiles(l):
        a = oa_ref[1, l]
        b = jnp.concatenate([stat_ref[l], block_ref[l]], axis=1)
        return jnp.where(odd, a, b), oa_ref[0, l], jnp.where(odd, b, a)

    return tiles


def stack(miscs, f):
    out = jnp.zeros((8, 2 * LANES), F32)
    for s, y in PLACE:
        row = miscs[s][2 * f + y : 2 * f + y + 1]
        out = jnp.where(iota(out.shape, 0) == 2 * s + y, row, out)
    return out


def coefs_kernel(z, oa_ref, stat_ref, block_ref, coef_ref, far_ref):
    tiles = tiles_of(z, oa_ref, stat_ref, block_ref)
    miscs = tiles(z.levels)
    sub = iota((8, LANES), 0)
    lane = iota((8, LANES), 1)
    on_left = lane % 16 >= 8
    owner, index, weight = (stack(miscs, f)[:, LANES:] for f in (3, 1, 2))
    far_ref[0:8, :] = jnp.broadcast_to(owner[:, 0:1], (8, LANES))
    far_ref[8:16, :] = jnp.broadcast_to(owner[:, LANES - 1 :], (8, LANES))
    for n, v in ((2, index), (4, weight)):
        nearer = jnp.where(on_left, v[:, LANES - 1 :], v[:, 0:1])
        farther = jnp.where(on_left, v[:, LANES - 2 : LANES - 1], v[:, 1:2])
        far_ref[8 * n : 8 * n + 8, :] = nearer
        far_ref[8 * n + 8 : 8 * n + 16, :] = farther

    def pack(block, g, old):
        b = 16 * g
        rel = lane - b
        own, side = block[:, 0:LANES], block[:, LANES:]
        out = old
        for lo, v, shift in ((0, own, 4), (4, side, 4), (8, side, 12), (12, own, 12)):
            out = jnp.where((rel >= lo) & (rel < lo + 4), lane_roll(v, b + shift), out)
        return out

    misc_seams = []
    for s in range(3):
        all_levels = jnp.zeros((8, LANES), F32)
        for g in range(PER):
            all_levels = pack(miscs[s], g, all_levels)
        misc_seams.append(all_levels)
    rel = lane % 16
    nearer = (rel == 4) | (rel == 11)
    farther = (rel == 5) | (rel == 10)
    for h in range(z.halves):
        packed = [jnp.zeros((8, LANES), F32)] * 3
        for g in range(min(PER, z.levels - PER * h)):
            blocks = tiles(PER * h + g)
            packed = [pack(blocks[s], g, packed[s]) for s in range(3)]

        def respond(columns, i, packed=packed):
            one = jnp.where(columns & (sub == i), 1.0, 0.0)
            return twice_back(misc_seams, one, packed)

        beside = {i: respond(nearer, i) for i in range(1, 5)}
        beyond = {i: respond(farther, i) for i in (2, 3)}
        for y in range(2):
            for c, v in enumerate(
                (beside[2 + y][y], beyond[2 + y][y], beside[1 + y][y], beside[3 + y][y])
            ):
                coef_ref[h, y, c] = v


def prepare_kernel(z, own_ref, oa_ref, stat_ref, block_ref, v_ref, dep_ref):
    _, swath, _ = z.place()
    tiles = tiles_of(z, oa_ref, stat_ref, block_ref)
    miscs = tiles(z.levels)
    dep = weigh(own_ref[...])
    sub = iota((8, LANES), 0)
    dep_ref[...] = jnp.sum(jnp.where(sub == swath, dep[0:8], 0.0), axis=0, keepdims=True)[
        :, 0 : LANES // 2
    ]
    owner, index, weight = (stack(miscs, f)[:, 0:LANES] for f in (3, 1, 2))
    near = find(table_of(outer_rows(z, swath), own_ref[...], owner), index)
    back = jnp.concatenate([weight * near, jnp.zeros((8, LANES), F32)], axis=1)

    def level(l, carry):
        out = twice_back(miscs, back, tiles(l))
        for y in range(2):
            at = pl.ds(pl.multiple_of((2 * l + y) * LANES, LANES), LANES)
            v_ref[:, at] = out[y][:, 0:LANES]
        return carry

    lax.fori_loop(0, z.levels, level, 0, unroll=UNROLL)


def join_kernel(part_ref, next_ref, far_ref, out_ref):
    out_ref[0:8, :] = part_ref[...]
    out_ref[8:16, :] = next_ref[...]


def product_kernel(
    z, x1_ref, x0_ref, v_ref, coef_ref, far_ref, d_ref, out_ref, v3, tall
):
    gx, swath, _ = z.place()
    left, right = sides_of(z, gx, x0_ref[...], x1_ref[...])
    outer = outer_rows(z, swath)
    right = table_of(outer, right, far_ref[0:8, :])
    left = table_of(outer, left, far_ref[8:16, :])
    on_left = iota((8, LANES), 1) % 16 >= 8

    def back(n):
        index = far_ref[16 + 8 * n : 24 + 8 * n, :]
        weight = far_ref[32 + 8 * n : 40 + 8 * n, :]
        return weight * jnp.where(on_left, find(left, index), find(right, index))

    near, away = back(0), back(1)
    wide = iota((NK, LANES), 1)
    for h in range(z.halves):
        seams = []
        for y in range(2):
            a, b, c, e = (coef_ref[h, y, i] for i in range(4))
            seams.append(
                (a * near[2 + y : 3 + y] + b * away[2 + y : 3 + y])
                + (c * near[1 + y : 2 + y] + e * near[3 + y : 4 + y])
            )
        for g in range(min(PER, z.levels - PER * h)):
            for y in range(2):
                r = 2 * (PER * h + g) + y
                first = lane_roll(seams[y], LANES - 16 * g - 12)
                last = lane_roll(seams[y], 124 - 16 * g)
                more = jnp.where(wide < 2, first, jnp.where(wide >= LANES - 2, last, 0.0))
                at = slice(r * LANES, (r + 1) * LANES)
                high, low = split(v_ref[:, at] + more)
                v3[0:NK, at] = high
                v3[NK : 2 * NK, at] = low
                v3[2 * NK :, at] = high
    d = d_ref[...]
    for r in range(0, z.rows, 2):
        both = lax.dot_general(
            d, v3[:, r * LANES : (r + 2) * LANES], (((0,), (0,)), ((), ())),
            preferred_element_type=F32,
        )
        tall[pl.ds(r, z.species, stride=z.rows), :] = both[:, 0:LANES]
        tall[pl.ds(r + 1, z.species, stride=z.rows), :] = both[:, LANES:]
    out_ref[...] = tall[...].astype(BF)


def shape(*dims, dtype=F32):
    return jax.ShapeDtypeStruct(dims, dtype)


LIMIT = pltpu.CompilerParams(vmem_limit_bytes=32 * 1024 * 1024)


def swaps_of(sizes):
    ngx, ngy, nsw = sizes
    nt = ngy * nsw

    def pairs(f):
        return [(g * nt + t, f(g, t)) for g in range(ngx) for t in range(nt)]

    def other(i, parity):
        return i + 1 if i % 2 == parity else i - 1

    def along_x(parity, flip):
        def to(g, t):
            n = other(g, parity)
            return n * nt + (t ^ flip) if 0 <= n < ngx else g * nt + (t ^ 1)

        return pairs(to)

    def along_y(parity):
        def to(g, t):
            n = other(t, parity)
            return g * nt + n if 0 <= n < nt else (g ^ 1) * nt + t

        return pairs(to)

    def along_z(g, t):
        gy, s = divmod(t, nsw)
        chip, core = divmod(s, 2)
        last = nsw // 2 - 1
        up = 1 if chip == 0 else -1
        if chip in (0, last) and 0 <= gy + up < ngy:
            gy, core = gy + up, 1 - core
        elif gy == ngy - 1 and chip < last:
            chip += 1
        elif gy == 0 and chip > 0:
            chip -= 1
        else:
            core = 1 - core
        return g * nt + gy * nsw + 2 * chip + core

    return along_x, along_y, pairs(along_z)


def per_device(
    sizes,
    direction,
    courant_x,
    courant_y,
    kernel,
    mechanism,
    propagator,
    footprint_pixel,
    footprint_weight,
    footprint_owner,
    precision,
):
    species, levels = direction.shape[:2]
    z = Sizes(sizes, species, levels)
    along_x, along_y, along_z = swaps_of(sizes)
    nsw = z.nsw

    def move(v, perm):
        return lax.ppermute(v, ALL, perm)

    cells = (species * z.rows, LANES)
    pixels = precision.shape[0]
    g, msg, edge, st, d = pl.pallas_call(
        functools.partial(project_kernel, z),
        out_shape=(
            shape(z.o_st, LANES),
            shape(z.msg, LANES, dtype=BF),
            shape(z.edge, LANES),
            shape(z.st16, LANES),
            shape(3 * NK, species, dtype=BF),
        ),
        in_specs=[HBM] * 10,
        out_specs=(VMEM,) * 5,
        scratch_shapes=[
            pltpu.VMEM(cells, BF),
            pltpu.VMEM(propagator.shape, BF),
            pltpu.VMEM(courant_x.shape, F32),
            pltpu.VMEM(courant_x.shape, F32),
            pltpu.VMEM(courant_x.shape, F32),
            pltpu.VMEM(mechanism.shape, jnp.int32),
            pltpu.VMEM(mechanism.shape, jnp.int32),
            pltpu.VMEM(mechanism.shape, F32),
            pltpu.VMEM((1, 2), jnp.int32),
            pltpu.VMEM((1, pixels), F32),
            pltpu.VMEM(cells, F32),
            pltpu.SemaphoreType.DMA((10,)),
        ],
        compiler_params=LIMIT,
        name="project",
    )(
        *(
            pltpu.with_memory_space_constraint(v, pltpu.HBM)
            for v in (
                direction.reshape(cells), propagator, courant_x, courant_y, kernel, mechanism,
                footprint_pixel, footprint_weight, footprint_owner.reshape(1, 2),
                precision.reshape(1, -1),
            )
        )
    )
    e0 = move(edge, along_x(0, 0))
    e1 = move(edge, along_x(1, 0))
    m_b = move(msg, along_y(1))
    m_a = move(msg, along_y(0))
    side, far = pl.pallas_call(
        functools.partial(edges_kernel, z),
        out_shape=(shape(z.edge, LANES), shape(z.far, LANES, dtype=BF)),
        in_specs=[VMEM, VMEM],
        out_specs=(VMEM, VMEM),
        compiler_params=LIMIT,
        cost_estimate=pl.CostEstimate(
            flops=20_000_000_000, bytes_accessed=1024, transcendentals=0
        ),
        name="edges",
    )(e1, e0)
    far_b = move(far, along_y(1))
    sums, ext, corner = pl.pallas_call(
        functools.partial(columns_kernel, z),
        out_shape=(
            shape(16, LANES), shape(2, levels + 1, 8, 2 * LANES), shape(NK, LANES)
        ),
        in_specs=[VMEM] * 5,
        out_specs=(VMEM,) * 3,
        scratch_shapes=[pltpu.VMEM((z.o_st, LANES), F32), pltpu.VMEM((NK, LANES), F32)],
        compiler_params=LIMIT,
        name="columns",
    )(m_a, g, st, side, move(side, along_y(0)))
    part, corner, stat = pl.pallas_call(
        functools.partial(beyond_kernel, z),
        out_shape=(shape(8, LANES), shape(NK, LANES), shape(levels + 1, 8, LANES)),
        in_specs=[VMEM] * 5,
        out_specs=(VMEM,) * 3,
        compiler_params=LIMIT,
        name="beyond",
    )(m_b, g, st, sums, corner)
    part, block = pl.pallas_call(
        functools.partial(corner_kernel, z),
        out_shape=(shape(8, LANES), shape(levels + 1, 8, LANES)),
        in_specs=[VMEM] * 4,
        out_specs=(VMEM, VMEM),
        compiler_params=LIMIT,
        name="corner",
    )(part, corner, far_b, st)
    part = part + lax.ppermute(part, "swath", [(i, i ^ 1) for i in range(nsw)])
    turns = [
        lax.ppermute(part, "swath", [(i, i ^ (2 * k) ^ 1) for i in range(nsw)])
        for k in (1, 3, 2)
    ]
    for turn in turns:
        part = part + turn
    coef, far = pl.pallas_call(
        functools.partial(coefs_kernel, z),
        out_shape=(shape(z.halves, 2, 4, NK, LANES), shape(48, LANES)),
        in_specs=[VMEM] * 3,
        out_specs=(VMEM, VMEM),
        compiler_params=LIMIT,
        name="coefs",
    )(ext, stat, block)
    both = pl.pallas_call(
        join_kernel,
        out_shape=shape(16, LANES),
        in_specs=[VMEM] * 3,
        out_specs=VMEM,
        compiler_params=LIMIT,
        name="join",
    )(part, move(part, along_z), far)
    b0 = move(both, along_x(0, 1))
    b1 = move(both, along_x(1, 1))
    v, dep = pl.pallas_call(
        functools.partial(prepare_kernel, z),
        out_shape=(
            shape(NK, z.rows * LANES),
            shape(1, pixels),
        ),
        in_specs=[VMEM] * 4,
        out_specs=(VMEM, VMEM),
        compiler_params=LIMIT,
        name="prepare",
    )(both, ext, stat, block)
    product = pl.pallas_call(
        functools.partial(product_kernel, z),
        out_shape=shape(*cells, dtype=BF),
        in_specs=[VMEM] * 6,
        out_specs=VMEM,
        scratch_shapes=[
            pltpu.VMEM((3 * NK, z.rows * LANES), BF),
            pltpu.VMEM(cells, F32),
        ],
        compiler_params=LIMIT,
        name="product",
    )(b1, b0, v, coef, far, d)
    return product.reshape(direction.shape), dep.reshape(-1)


def solution(mesh):
    placed = (
        P(None, None, ("gy", "swath"), "gx"),
        P(None, ("gy", "swath"), "gx"),
        P(None, ("gy", "swath"), "gx"),
        P(None, ("gy", "swath"), "gx"),
        P(("gy", "swath"), "gx"),
        P(),
        P(("gy", "swath"), "gx"),
        P(("gy", "swath"), "gx"),
        P(("gx", "gy", "swath"), None),
        P(("gx", "gy", "swath")),
    )
    sizes = tuple(mesh.shape[a] for a in ALL)
    return jax.shard_map(
        functools.partial(per_device, sizes),
        mesh=mesh,
        in_specs=placed,
        out_specs=(P(None, None, ("gy", "swath"), "gx"), P(("gx", "gy", "swath"))),
        check_vma=False,
    )
```

```python
import functools

import jax
import jax.numpy as jnp
from jax import lax
from jax.experimental import pallas as pl
from jax.experimental.pallas import tpu as pltpu
from jax.sharding import PartitionSpec as P

KD = 0.2
UNROLL = 10
ALL = ("gx", "gy", "swath")
LANES = 128
NM = 4
NK = NM * NM
BF = jnp.bfloat16
F32 = jnp.float32
VMEM = pl.BlockSpec(memory_space=pltpu.VMEM)
HBM = pl.BlockSpec(memory_space=pltpu.HBM)


def iota(shape, dim):
    return lax.broadcasted_iota(jnp.int32, shape, dim)


def lane_roll(v, shift):
    return pltpu.roll(v, shift % v.shape[-1], v.ndim - 1)


def split(v):
    high = v.astype(BF)
    return high, (v - high.astype(F32)).astype(BF)


class Sizes:
    def __init__(self, sizes, species, levels):
        self.ngx, self.ngy, self.nsw = sizes
        self.nt = self.ngy * self.nsw
        self.species = species
        self.levels = levels
        self.rows = 2 * levels
        self.base = 8 * levels
        self.st = self.base + 8
        self.st16 = -(-(self.st + 1) // 16) * 16
        self.o_st = self.rows * NK
        self.msg = self.o_st + 2 * self.st16
        self.edge = NK + 8
        self.halves = -(-levels // PER)
        self.far = NK + 2 * 16

    def place(self):
        gx = lax.axis_index("gx")
        swath = lax.axis_index("swath")
        return gx, swath, lax.axis_index("gy") * self.nsw + swath


def project_kernel(
    z, dir_hbm, prop_hbm, cx_hbm, cy_hbm, kern_hbm, mech_hbm, pix_hbm, wgt_hbm, own_hbm, prec_hbm,
    g_ref, msg_ref, edge_ref, st_ref, d_ref,
    dir_ref, prop_ref, cx_ref, cy_ref, kern_ref, mech_ref, pix_ref, wgt_ref, own_ref, prec_ref,
    wide, sems,
):
    sources = (
        prop_hbm, dir_hbm, cx_hbm, cy_hbm, kern_hbm, mech_hbm, pix_hbm, wgt_hbm, own_hbm, prec_hbm
    )
    targets = (
        prop_ref, dir_ref, cx_ref, cy_ref, kern_ref, mech_ref, pix_ref, wgt_ref, own_ref, prec_ref
    )
    copies = [
        pltpu.make_async_copy(a, b, sems.at[i]) for i, (a, b) in enumerate(zip(sources, targets))
    ]
    for copy in copies:
        copy.start()
    species = z.species
    copies[0].wait()
    k_of = iota((NK, species), 0)
    heads = jnp.zeros((NK, species), F32)
    for m in range(NM):
        row = prop_ref[m][0:1, :].astype(F32)
        heads = heads + jnp.where(k_of % NM == m, row, 0.0)
    total = heads + jnp.where(iota((NK, species), 1) == 0, 1.0, 0.0)
    lhs = heads.astype(BF)
    for m in range(NM):
        matrix = prop_ref[m]
        term = jnp.dot(lhs, matrix, preferred_element_type=F32)
        total = total + jnp.where(k_of // NM == m, term + matrix[0:1, :].astype(F32), 0.0)
    high, low = split(total)
    both = jnp.concatenate([high, low], axis=0)
    d_ref[...] = jnp.concatenate([high, high, low], axis=0)
    copies[1].wait()
    wide[...] = dir_ref[...].astype(F32)
    cells = jnp.concatenate(
        [wide[pl.ds(r, species, stride=z.rows), :].astype(BF) for r in range(z.rows)], axis=1
    )
    g32 = jnp.dot(both, cells, preferred_element_type=F32)
    g = g32[:NK] + g32[NK:]
    lane = iota((NK, LANES), 1)
    edge = jnp.zeros((NK, LANES), F32)
    for r in range(z.rows):
        part = g[:, r * LANES : (r + 1) * LANES]
        g_ref[r * NK : (r + 1) * NK, :] = part
        msg_ref[r * NK : (r + 1) * NK, :] = part.astype(BF)
        edge = jnp.where(lane // 4 == r, lane_roll(part, 4 * r + 2), edge)
    edge_ref[0:NK, :] = edge
    for copy in copies[2:]:
        copy.wait()
    lane = iota((8, LANES), 1)
    side = jnp.zeros((8, LANES), F32)
    blank = jnp.zeros((2, LANES), F32)
    own = jnp.where(iota((2, LANES), 0) == 0, own_ref[:, 0:1], own_ref[:, 1:2])
    for l in range(z.levels + 1):
        if l < z.levels:
            parts = [cx_ref[l], cy_ref[l], kern_ref[l], blank]
        else:
            parts = [
                (mech_ref[...] + 1).astype(F32),
                pix_ref[...].astype(F32),
                wgt_ref[...],
                own.astype(F32),
            ]
        block = jnp.concatenate(parts, axis=0)
        st_ref[8 * l : 8 * l + 8, :] = block
        side = jnp.where(lane // 4 == l, lane_roll(block, 4 * l + 2), side)
    pixels = prec_ref.shape[1]
    last = jnp.concatenate([jnp.zeros((1, LANES - pixels), F32), prec_ref[...]], axis=1)
    st_ref[z.st :, :] = jnp.broadcast_to(last, (z.st16 - z.st, LANES))
    edge_ref[NK:, :] = side
    high, low = split(st_ref[...])
    msg_ref[z.o_st : z.o_st + z.st16, :] = high
    msg_ref[z.o_st + z.st16 : z.o_st + 2 * z.st16, :] = low


def sides_of(z, gx, x0, x1):
    even = gx % 2 == 0
    right = jnp.where(even, x0, x1)
    left = jnp.where(even, x1, x0)
    return jnp.where(gx > 0, left, 0.0), jnp.where(gx < z.ngx - 1, right, 0.0)


def edges_kernel(z, x1_ref, x0_ref, side_ref, far_ref):
    gx, _, _ = z.place()
    left, right = sides_of(z, gx, x0_ref[...], x1_ref[...])
    side = jnp.where(iota(left.shape, 1) % 4 < 2, left, right)
    side_ref[...] = side
    far_ref[0:NK, :] = side[0:NK].astype(BF)
    high, low = split(jnp.concatenate([side[NK:], jnp.zeros((8, LANES), F32)], axis=0))
    far_ref[NK : NK + 16, :] = high
    far_ref[NK + 16 :, :] = low


def spread(z, side, l):
    return lane_roll(side, LANES - (4 * l + 2))


def edge_lanes(z, l, left, right, old):
    lane = iota((NK, LANES), 1)
    left = pltpu.roll(left, 8 * l + 1, 1)
    right = pltpu.roll(right, 8 * l + 3, 1)
    return jnp.where(lane == 8 * l + 1, left, jnp.where(lane == 8 * l + 2, right, old))


def fold(v):
    half = v[0:8] + v[8:16]
    return half + pltpu.roll(half, 4, 0)


def row_of(stats, odd, first):
    return jnp.where(odd, stats[first ^ 1 : (first ^ 1) + 1], stats[first : first + 1])


def columns_kernel(z, a_ref, g_ref, st_ref, side_ref, far_ref, sums_ref, ext_ref, corner_ref, ga, ha):
    _, _, t = z.place()
    odd = t % 2 == 1
    even = jnp.where(odd, 0, 1)
    sg = jnp.where(odd, -0.5, 0.5)
    W = 2 * LANES
    ga[...] = a_ref[0 : z.o_st, :].astype(F32)
    ha[...] = far_ref[0:NK, :]
    stat_a = a_ref[z.o_st : z.o_st + z.st16, :].astype(F32) + a_ref[
        z.o_st + z.st16 : z.msg, :
    ].astype(F32)
    for l in range(z.levels + 1):
        ext_ref[0, l, :, 0:LANES] = st_ref[8 * l : 8 * l + 8, :]
        ext_ref[0, l, :, LANES:] = spread(z, side_ref[NK:, :], l)
        ext_ref[1, l, :, 0:LANES] = stat_a[8 * l : 8 * l + 8]
        ext_ref[1, l, :, LANES:] = spread(z, far_ref[NK:, :], l)
    k_of = iota((NK, W), 0)
    misc = ext_ref[0, z.levels]
    misc_a = ext_ref[1, z.levels]

    def sort(mech):
        return mech == (k_of // NM + 1).astype(F32)

    mech_0 = row_of(misc, odd, 0)
    mask_0, mask_1, mask_a = sort(mech_0), sort(row_of(misc, odd, 1)), sort(row_of(misc_a, odd, 0))
    head_0 = mech_0 == (k_of % NM + 1).astype(F32)
    weight_0 = row_of(misc, odd, 4)

    def level(l, carry):
        def field(ref, side, y):
            r = 2 * l + y
            own = ref[pl.ds(pl.multiple_of(r * NK, NK), NK), :]
            return jnp.concatenate([own, pltpu.roll(side, LANES - 2 - 4 * r, 1)], axis=1)

        side = side_ref[0:NK, :]
        q0, q1 = field(g_ref, side, 1 - even), field(g_ref, side, even)
        a1, a2 = field(ga, ha[...], 1 - even), field(ga, ha[...], even)
        own, other = ext_ref[0, l], ext_ref[1, l]
        cx_0, cx_1, cx_a = (
            0.5 * row_of(own, odd, 0), 0.5 * row_of(own, odd, 1), 0.5 * row_of(other, odd, 0)
        )
        cy_0, cy_1, cy_a = (
            sg * row_of(own, odd, 2), sg * row_of(own, odd, 3), sg * row_of(other, odd, 2)
        )

        def along(mid, cx):
            return (
                (1.0 - 4.0 * KD) * mid
                + (KD - cx) * pltpu.roll(mid, W - 1, 1)
                + (KD + cx) * pltpu.roll(mid, 1, 1)
            )

        f0 = along(q0, cx_0) + (KD - cy_0) * q1
        f1 = along(q1, cx_1) + (KD - cy_1) * a1 + (KD + cy_1) * q0
        fa = along(a1, cx_a) + (KD - cy_a) * a2 + (KD + cy_a) * q1
        f0, f1, fa = (
            fold(jnp.where(m, f, 0.0)) for m, f in ((mask_0, f0), (mask_1, f1), (mask_a, fa))
        )
        h0 = along(f0, cx_0) + (KD - cy_0) * f1
        h1 = along(f1, cx_1) + (KD - cy_1) * fa + (KD + cy_1) * f0
        kern_0, kern_1 = row_of(own, odd, 4), row_of(own, odd, 5)
        s0 = carry[0] + (kern_0 * h0)[:, 0:LANES]
        s1 = carry[1] + (kern_1 * h1)[:, 0:LANES]
        step = jnp.where(mask_0, KD + cy_0, 0.0)
        scale = jnp.where(head_0, kern_0 * weight_0, 0.0)
        left = (scale * pltpu.roll(step, 1, 1) * (KD + cx_0))[:, 0:LANES]
        right = (scale * pltpu.roll(step, W - 1, 1) * (KD - cx_0))[:, 0:LANES]
        return s0, s1, edge_lanes(z, l, left, right, carry[2])

    none = jnp.zeros((8, LANES), F32)
    s0, s1, corner = lax.fori_loop(
        0, z.levels, level, (none, none, jnp.zeros((NK, LANES), F32)), unroll=UNROLL
    )
    sums_ref[0:8, :] = s0
    sums_ref[8:16, :] = s1
    corner_ref[...] = corner


def beyond_kernel(z, b_ref, g_ref, st_ref, sums_ref, old_ref, part_ref, corner_ref, stat_ref):
    _, swath, t = z.place()
    odd = t % 2 == 1
    even = jnp.where(odd, 0, 1)
    has_b = jnp.logical_and(t > 0, t < z.nt - 1)
    sg = jnp.where(odd, -0.5, 0.5)
    stat_b = b_ref[z.o_st : z.o_st + z.st16, :].astype(F32) + b_ref[
        z.o_st + z.st16 : z.msg, :
    ].astype(F32)
    stat_b = jnp.where(has_b, stat_b, 0.0)
    for l in range(z.levels + 1):
        stat_ref[l] = stat_b[8 * l : 8 * l + 8]
    k_of = iota((NK, LANES), 0)
    lane = iota((NK, LANES), 1)
    lane8 = iota((8, LANES), 1)
    sub8 = iota((8, LANES), 0)
    misc = st_ref[z.base : z.base + 8, :]
    mech_0 = row_of(misc, odd, 0)
    mech_b = row_of(stat_ref[z.levels], odd, 1)
    mask_0 = (mech_0 == (k_of // NM + 1).astype(F32)) & has_b
    mask_b = mech_b == (k_of // NM + 1).astype(F32)
    head_0 = mech_0 == (k_of % NM + 1).astype(F32)
    weight_0 = row_of(misc, odd, 4)

    def level(l, carry):
        def field(ref, y):
            at = pl.ds(pl.multiple_of((2 * l + y) * NK, NK), NK)
            return ref[at, :].astype(F32)

        q0 = field(g_ref, 1 - even)
        b1, b2 = field(b_ref, even), field(b_ref, 1 - even)
        own = st_ref[pl.ds(pl.multiple_of(8 * l, 8), 8), :]
        other = stat_ref[l]
        cx_0, cx_b = 0.5 * row_of(own, odd, 0), 0.5 * row_of(other, odd, 1)
        cy_0, cy_1, cy_b = (
            sg * row_of(own, odd, 2), sg * row_of(own, odd, 3), sg * row_of(other, odd, 3)
        )

        def along(mid, cx, lane):
            east = jnp.where(lane < LANES - 1, pltpu.roll(mid, LANES - 1, 1), 0.0)
            west = jnp.where(lane > 0, pltpu.roll(mid, 1, 1), 0.0)
            return (1.0 - 4.0 * KD) * mid + (KD - cx) * east + (KD + cx) * west

        fb = along(b1, cx_b, lane) + (KD - cy_b) * q0 + (KD + cy_b) * b2
        fb = fold(jnp.where(mask_b, fb, 0.0))
        f0 = fold(jnp.where(mask_0, (KD + cy_0) * b1, 0.0))
        kern_0, kern_1 = row_of(own, odd, 4), row_of(own, odd, 5)
        s0 = carry[0] + kern_0 * (along(f0, cx_0, lane8) + (KD + cy_0) * fb)
        s1 = carry[1] + kern_1 * (KD + cy_1) * f0
        step = jnp.where(head_0 & mask_b, kern_0 * weight_0 * (KD + cy_0), 0.0)
        left, right = step * (KD + cx_b), step * (KD - cx_b)
        corner = edge_lanes(z, l, left, right, carry[2])
        return s0, s1, corner

    s0, s1, corner = lax.fori_loop(
        0,
        z.levels,
        level,
        (sums_ref[0:8, :], sums_ref[8:16, :], jnp.zeros((NK, LANES), F32)),
        unroll=UNROLL,
    )
    corner_ref[...] = corner + old_ref[...]
    pixels = LANES // 2
    sub = iota((pixels, LANES), 0)
    total = jnp.zeros((8, LANES), F32)
    for y, sums in ((0, s0), (1, s1)):
        final = row_of(misc, odd, y) == (sub8 + 1).astype(F32)
        column = jnp.sum(jnp.where(final, sums, 0.0), axis=0, keepdims=True)
        column = column * row_of(misc, odd, 4 + y)
        hit = jnp.where(row_of(misc, odd, 2 + y) == sub.astype(F32), column, 0.0)
        tall = jnp.sum(hit, axis=1, keepdims=True)
        row = jnp.sum(
            jnp.where(sub == iota((pixels, LANES), 1), tall, 0.0), axis=0, keepdims=True
        )
        total = total + jnp.where(row_of(misc, odd, 6 + y) == sub8.astype(F32), row, 0.0)
    part_ref[...] = jnp.where(
        lane8 < pixels, total, jnp.where(sub8 == swath, st_ref[z.st : z.st + 1, :], 0.0)
    )


def corner_kernel(z, part_ref, corner_ref, far_ref, st_ref, out_ref, block_ref):
    _, _, t = z.place()
    odd = t % 2 == 1
    has_b = jnp.logical_and(t > 0, t < z.nt - 1)
    far = jnp.where(has_b, far_ref[...].astype(F32), 0.0)
    side = (far[NK : NK + 16] + far[NK + 16 :])[0:8]
    for l in range(z.levels + 1):
        block_ref[l] = spread(z, side, l)
    g = far[0:NK]
    g = jnp.where(odd, g, pltpu.roll(g, LANES - 4, 1))
    share = jnp.sum(corner_ref[...] * g, axis=0, keepdims=True)
    lane = iota((1, LANES), 1)
    sub8 = iota((8, LANES), 0)
    lane8 = iota((8, LANES), 1)
    misc = st_ref[z.base : z.base + 8, :]
    pixel = row_of(misc, odd, 2)
    owner = row_of(misc, odd, 6)
    total = part_ref[...]
    for c, column in ((1, 0), (2, LANES - 1)):
        value = jnp.sum(jnp.where(lane % 8 == c, share, 0.0), axis=1, keepdims=True)
        at = slice(column, column + 1)
        hit = (lane8.astype(F32) == pixel[:, at]) & (sub8.astype(F32) == owner[:, at])
        total = total + jnp.where(hit, value, 0.0)
    out_ref[...] = total


def weigh(v):
    return v * lane_roll(v, LANES // 2)


def outer_rows(z, swath):
    sub = iota((8, LANES), 0)
    return ((sub < 2) & (swath == 0)) | ((sub >= 4) & (swath == z.nsw - 1))


def table_of(outer, sums, owner):
    row = owner.astype(jnp.int32)
    return jnp.where(
        outer,
        jnp.take_along_axis(sums[8:16], row, axis=0),
        jnp.take_along_axis(sums[0:8], row, axis=0),
    )


def find(table, index):
    at = index.astype(jnp.int32)
    half = LANES // 2
    return jnp.take_along_axis(table, at, axis=1) * jnp.take_along_axis(table, at + half, axis=1)


PLACE = [(s, y) for s in range(3) for y in range(2)]


def twice_back(miscs, back, stats):
    W = back.shape[1]
    m_of = iota((8, W), 0) % NM
    k_of = iota((NK, W), 0) // NM
    mech = [miscs[s][y : y + 1] for s, y in PLACE]
    cx = [0.5 * stats[s][y : y + 1] for s, y in PLACE]
    cy = [0.5 * stats[s][2 + y : 3 + y] for s, y in PLACE]
    kern = [stats[s][4 + y : 5 + y] for s, y in PLACE]

    def unadvect(v, i, at):
        return (
            (1.0 - 4.0 * KD) * v[at]
            + pltpu.roll((KD - cx[i]) * v[at], 1, 1)
            + pltpu.roll((KD + cx[i]) * v[at], W - 1, 1)
            + (KD - cy[i - 1]) * v[at - 1]
            + (KD + cy[i + 1]) * v[at + 1]
        )

    w = [
        kern[i] * jnp.where(mech[i] == (m_of + 1).astype(F32), back[i : i + 1, :], 0.0)
        for i in range(6)
    ]
    u = []
    for i in range(1, 5):
        mid = unadvect(w, i, i)
        both = jnp.concatenate([mid, mid], axis=0)
        u.append(jnp.where(mech[i] == (k_of + 1).astype(F32), both, 0.0))
    return [unadvect(u, 2 + y, 1 + y) for y in range(2)]


PER = 5


def tiles_of(z, oa_ref, stat_ref, block_ref):
    _, _, t = z.place()
    odd = t % 2 == 1

    def tiles(l):
        a = oa_ref[1, l]
        b = jnp.concatenate([stat_ref[l], block_ref[l]], axis=1)
        return jnp.where(odd, a, b), oa_ref[0, l], jnp.where(odd, b, a)

    return tiles


def stack(miscs, f):
    out = jnp.zeros((8, 2 * LANES), F32)
    for s, y in PLACE:
        row = miscs[s][2 * f + y : 2 * f + y + 1]
        out = jnp.where(iota(out.shape, 0) == 2 * s + y, row, out)
    return out


def coefs_kernel(z, oa_ref, stat_ref, block_ref, coef_ref, far_ref):
    tiles = tiles_of(z, oa_ref, stat_ref, block_ref)
    miscs = tiles(z.levels)
    sub = iota((8, LANES), 0)
    lane = iota((8, LANES), 1)
    on_left = lane % 16 >= 4
    owner, index, weight = (stack(miscs, f)[:, LANES:] for f in (3, 1, 2))
    far_ref[0:8, :] = jnp.broadcast_to(owner[:, 0:1], (8, LANES))
    far_ref[8:16, :] = jnp.broadcast_to(owner[:, LANES - 1 :], (8, LANES))
    for n, v in ((2, index), (4, weight)):
        nearer = jnp.where(on_left, v[:, LANES - 1 :], v[:, 0:1])
        farther = jnp.where(on_left, v[:, LANES - 2 : LANES - 1], v[:, 1:2])
        far_ref[8 * n : 8 * n + 8, :] = nearer
        far_ref[8 * n + 8 : 8 * n + 16, :] = farther

    def pack(block, g, old):
        b = 16 * g
        rel = lane - b
        own, side = block[:, 0:LANES], block[:, LANES:]
        out = old
        for lo, v, shift in ((0, own, 4), (4, side, 4), (8, side, 12), (12, own, 12)):
            out = jnp.where((rel >= lo) & (rel < lo + 4), lane_roll(v, b + shift), out)
        return out

    misc_seams = []
    for s in range(3):
        all_levels = jnp.zeros((8, LANES), F32)
        for g in range(PER):
            all_levels = pack(miscs[s], g, all_levels)
        misc_seams.append(all_levels)
    rel = lane % 16
    nearer = (rel == 4) | (rel == 11)
    farther = (rel == 5) | (rel == 10)
    for h in range(z.halves):
        packed = [jnp.zeros((8, LANES), F32)] * 3
        for g in range(min(PER, z.levels - PER * h)):
            blocks = tiles(PER * h + g)
            packed = [pack(blocks[s], g, packed[s]) for s in range(3)]

        def respond(columns, i, packed=packed):
            one = jnp.where(columns & (sub == i), 1.0, 0.0)
            return twice_back(misc_seams, one, packed)

        beside = {i: respond(nearer, i) for i in range(1, 5)}
        beyond = {i: respond(farther, i) for i in (2, 3)}
        for y in range(2):
            for c, v in enumerate(
                (beside[2 + y][y], beyond[2 + y][y], beside[1 + y][y], beside[3 + y][y])
            ):
                coef_ref[h, y, c] = jnp.where(
                    iota((NK, LANES), 1) % 16 < 4, v, lane_roll(v, LANES - 8)
                )


def prepare_kernel(z, own_ref, oa_ref, stat_ref, block_ref, v_ref, dep_ref):
    _, swath, _ = z.place()
    tiles = tiles_of(z, oa_ref, stat_ref, block_ref)
    miscs = tiles(z.levels)
    dep = weigh(own_ref[...])
    sub = iota((8, LANES), 0)
    dep_ref[...] = jnp.sum(jnp.where(sub == swath, dep[0:8], 0.0), axis=0, keepdims=True)[
        :, 0 : LANES // 2
    ]
    owner, index, weight = (stack(miscs, f)[:, 0:LANES] for f in (3, 1, 2))
    near = find(table_of(outer_rows(z, swath), own_ref[...], owner), index)
    back = jnp.concatenate([weight * near, jnp.zeros((8, LANES), F32)], axis=1)

    def level(l, carry):
        out = twice_back(miscs, back, tiles(l))
        for y in range(2):
            at = pl.ds(pl.multiple_of((2 * l + y) * LANES, LANES), LANES)
            v_ref[:, at] = out[y][:, 0:LANES]
        return carry

    lax.fori_loop(0, z.levels, level, 0, unroll=UNROLL)


def join_kernel(part_ref, next_ref, far_ref, out_ref):
    out_ref[0:8, :] = part_ref[...]
    out_ref[8:16, :] = next_ref[...]


def product_kernel(
    z, x1_ref, x0_ref, v_ref, coef_ref, far_ref, d_ref, out_ref, v3, tall
):
    gx, swath, _ = z.place()
    left, right = sides_of(z, gx, x0_ref[...], x1_ref[...])
    outer = outer_rows(z, swath)
    right = table_of(outer, right, far_ref[0:8, :])
    left = table_of(outer, left, far_ref[8:16, :])
    on_left = iota((8, LANES), 1) % 16 >= 4

    def back(n):
        index = far_ref[16 + 8 * n : 24 + 8 * n, :]
        weight = far_ref[32 + 8 * n : 40 + 8 * n, :]
        return weight * jnp.where(on_left, find(left, index), find(right, index))

    near, away = back(0), back(1)
    wide = iota((NK, LANES), 1)
    for h in range(z.halves):
        seams = []
        for y in range(2):
            a, b, c, e = (coef_ref[h, y, i] for i in range(4))
            seams.append(
                (a * near[2 + y : 3 + y] + b * away[2 + y : 3 + y])
                + (c * near[1 + y : 2 + y] + e * near[3 + y : 4 + y])
            )
        for g in range(min(PER, z.levels - PER * h)):
            for y in range(2):
                r = 2 * (PER * h + g) + y
                more = lane_roll(seams[y], LANES - 16 * g - 4)
                more = jnp.where((wide < 2) | (wide >= LANES - 2), more, 0.0)
                at = slice(r * LANES, (r + 1) * LANES)
                high, low = split(v_ref[:, at] + more)
                v3[0:NK, at] = high
                v3[NK : 2 * NK, at] = low
                v3[2 * NK :, at] = high
    d = d_ref[...]
    for r in range(0, z.rows, 2):
        both = lax.dot_general(
            d, v3[:, r * LANES : (r + 2) * LANES], (((0,), (0,)), ((), ())),
            preferred_element_type=F32,
        )
        tall[pl.ds(r, z.species, stride=z.rows), :] = both[:, 0:LANES]
        tall[pl.ds(r + 1, z.species, stride=z.rows), :] = both[:, LANES:]
    out_ref[...] = tall[...].astype(BF)


def shape(*dims, dtype=F32):
    return jax.ShapeDtypeStruct(dims, dtype)


LIMIT = pltpu.CompilerParams(vmem_limit_bytes=32 * 1024 * 1024)


def swaps_of(sizes):
    ngx, ngy, nsw = sizes
    nt = ngy * nsw

    def pairs(f):
        return [(g * nt + t, f(g, t)) for g in range(ngx) for t in range(nt)]

    def other(i, parity):
        return i + 1 if i % 2 == parity else i - 1

    def along_x(parity, flip):
        def to(g, t):
            n = other(g, parity)
            return n * nt + (t ^ flip) if 0 <= n < ngx else g * nt + (t ^ 1)

        return pairs(to)

    def along_y(parity):
        def to(g, t):
            n = other(t, parity)
            return g * nt + n if 0 <= n < nt else (g ^ 1) * nt + t

        return pairs(to)

    def along_z(g, t):
        gy, s = divmod(t, nsw)
        chip, core = divmod(s, 2)
        last = nsw // 2 - 1
        up = 1 if chip == 0 else -1
        if chip in (0, last) and 0 <= gy + up < ngy:
            gy, core = gy + up, 1 - core
        elif gy == ngy - 1 and chip < last:
            chip += 1
        elif gy == 0 and chip > 0:
            chip -= 1
        else:
            core = 1 - core
        return g * nt + gy * nsw + 2 * chip + core

    return along_x, along_y, pairs(along_z)


def per_device(
    sizes,
    direction,
    courant_x,
    courant_y,
    kernel,
    mechanism,
    propagator,
    footprint_pixel,
    footprint_weight,
    footprint_owner,
    precision,
):
    species, levels = direction.shape[:2]
    z = Sizes(sizes, species, levels)
    along_x, along_y, along_z = swaps_of(sizes)
    nsw = z.nsw

    def move(v, perm):
        return lax.ppermute(v, ALL, perm)

    cells = (species * z.rows, LANES)
    pixels = precision.shape[0]
    g, msg, edge, st, d = pl.pallas_call(
        functools.partial(project_kernel, z),
        out_shape=(
            shape(z.o_st, LANES),
            shape(z.msg, LANES, dtype=BF),
            shape(z.edge, LANES),
            shape(z.st16, LANES),
            shape(3 * NK, species, dtype=BF),
        ),
        in_specs=[HBM] * 10,
        out_specs=(VMEM,) * 5,
        scratch_shapes=[
            pltpu.VMEM(cells, BF),
            pltpu.VMEM(propagator.shape, BF),
            pltpu.VMEM(courant_x.shape, F32),
            pltpu.VMEM(courant_x.shape, F32),
            pltpu.VMEM(courant_x.shape, F32),
            pltpu.VMEM(mechanism.shape, jnp.int32),
            pltpu.VMEM(mechanism.shape, jnp.int32),
            pltpu.VMEM(mechanism.shape, F32),
            pltpu.VMEM((1, 2), jnp.int32),
            pltpu.VMEM((1, pixels), F32),
            pltpu.VMEM(cells, F32),
            pltpu.SemaphoreType.DMA((10,)),
        ],
        compiler_params=LIMIT,
        name="project",
    )(
        *(
            pltpu.with_memory_space_constraint(v, pltpu.HBM)
            for v in (
                direction.reshape(cells), propagator, courant_x, courant_y, kernel, mechanism,
                footprint_pixel, footprint_weight, footprint_owner.reshape(1, 2),
                precision.reshape(1, -1),
            )
        )
    )
    e0 = move(edge, along_x(0, 0))
    e1 = move(edge, along_x(1, 0))
    m_b = move(msg, along_y(1))
    m_a = move(msg, along_y(0))
    side, far = pl.pallas_call(
        functools.partial(edges_kernel, z),
        out_shape=(shape(z.edge, LANES), shape(z.far, LANES, dtype=BF)),
        in_specs=[VMEM, VMEM],
        out_specs=(VMEM, VMEM),
        compiler_params=LIMIT,
        cost_estimate=pl.CostEstimate(
            flops=20_000_000_000, bytes_accessed=1024, transcendentals=0
        ),
        name="edges",
    )(e1, e0)
    far_b = move(far, along_y(1))
    sums, ext, corner = pl.pallas_call(
        functools.partial(columns_kernel, z),
        out_shape=(
            shape(16, LANES), shape(2, levels + 1, 8, 2 * LANES), shape(NK, LANES)
        ),
        in_specs=[VMEM] * 5,
        out_specs=(VMEM,) * 3,
        scratch_shapes=[pltpu.VMEM((z.o_st, LANES), F32), pltpu.VMEM((NK, LANES), F32)],
        compiler_params=LIMIT,
        name="columns",
    )(m_a, g, st, side, move(side, along_y(0)))
    part, corner, stat = pl.pallas_call(
        functools.partial(beyond_kernel, z),
        out_shape=(shape(8, LANES), shape(NK, LANES), shape(levels + 1, 8, LANES)),
        in_specs=[VMEM] * 5,
        out_specs=(VMEM,) * 3,
        compiler_params=LIMIT,
        name="beyond",
    )(m_b, g, st, sums, corner)
    part, block = pl.pallas_call(
        functools.partial(corner_kernel, z),
        out_shape=(shape(8, LANES), shape(levels + 1, 8, LANES)),
        in_specs=[VMEM] * 4,
        out_specs=(VMEM, VMEM),
        compiler_params=LIMIT,
        name="corner",
    )(part, corner, far_b, st)
    part = part + lax.ppermute(part, "swath", [(i, i ^ 1) for i in range(nsw)])
    turns = [
        lax.ppermute(part, "swath", [(i, i ^ (2 * k) ^ 1) for i in range(nsw)])
        for k in (1, 3, 2)
    ]
    for turn in turns:
        part = part + turn
    coef, far = pl.pallas_call(
        functools.partial(coefs_kernel, z),
        out_shape=(shape(z.halves, 2, 4, NK, LANES), shape(48, LANES)),
        in_specs=[VMEM] * 3,
        out_specs=(VMEM, VMEM),
        compiler_params=LIMIT,
        name="coefs",
    )(ext, stat, block)
    both = pl.pallas_call(
        join_kernel,
        out_shape=shape(16, LANES),
        in_specs=[VMEM] * 3,
        out_specs=VMEM,
        compiler_params=LIMIT,
        name="join",
    )(part, move(part, along_z), far)
    b0 = move(both, along_x(0, 1))
    b1 = move(both, along_x(1, 1))
    v, dep = pl.pallas_call(
        functools.partial(prepare_kernel, z),
        out_shape=(
            shape(NK, z.rows * LANES),
            shape(1, pixels),
        ),
        in_specs=[VMEM] * 4,
        out_specs=(VMEM, VMEM),
        compiler_params=LIMIT,
        name="prepare",
    )(both, ext, stat, block)
    product = pl.pallas_call(
        functools.partial(product_kernel, z),
        out_shape=shape(*cells, dtype=BF),
        in_specs=[VMEM] * 6,
        out_specs=VMEM,
        scratch_shapes=[
            pltpu.VMEM((3 * NK, z.rows * LANES), BF),
            pltpu.VMEM(cells, F32),
        ],
        compiler_params=LIMIT,
        name="product",
    )(b1, b0, v, coef, far, d)
    return product.reshape(direction.shape), dep.reshape(-1)


def solution(mesh):
    placed = (
        P(None, None, ("gy", "swath"), "gx"),
        P(None, ("gy", "swath"), "gx"),
        P(None, ("gy", "swath"), "gx"),
        P(None, ("gy", "swath"), "gx"),
        P(("gy", "swath"), "gx"),
        P(),
        P(("gy", "swath"), "gx"),
        P(("gy", "swath"), "gx"),
        P(("gx", "gy", "swath"), None),
        P(("gx", "gy", "swath")),
    )
    sizes = tuple(mesh.shape[a] for a in ALL)
    return jax.shard_map(
        functools.partial(per_device, sizes),
        mesh=mesh,
        in_specs=placed,
        out_specs=(P(None, None, ("gy", "swath"), "gx"), P(("gx", "gy", "swath"))),
        check_vma=False,
    )
```
